32 devices in a mesh: leaf: 8 (over z, y), panel: 4 (over x, core).
Axes of the slice: x: 2, y: 2, z: 4, core: 2. Of those that a mesh axis runs over, the one named last changes fastest.
Arguments:
- border: bfloat16 [8, 128, 8192], P('leaf', 'panel'), may hold values from -0.1875 to 0.1875
- solution: bfloat16 [8, 128, 128], P('leaf', 'panel'), may hold values from -6 to 6
- winv_top: bfloat16 [4096, 4096], P(None, ('leaf', 'panel')), as said below
- winv_mid: bfloat16 [4096, 8192], P(None, ('leaf', 'panel')), as said below
- coupling: bfloat16 [8192, 4096], P(('leaf', 'panel')), may hold values from -0.0625 to 0.0625
Outputs:
- top_adjoint: float32 [4096, 128], P(('leaf', 'panel'))
- mid_adjoint: float32 [8192, 128], P(('leaf', 'panel'))
The draws below stay inside these ranges and needn't reach their ends.
Inputs may be any that keep to these rules, and one draw needn't show every extreme that they name: `winv_top`: each 4096 x 4096 block of the factor is lower triangular with a positive diagonal. `winv_mid`: each 4096 x 4096 block of the factor is lower triangular with a positive diagonal.
All inputs are finite; a program needn't handle non-finite values.
Results may differ from the reference program's by a relative error of at most 0.0003.
Values sent between devices are 32-bit elements; how exact they have to be, the bound alone decides.
No kernel may reach another device: no remote copies, remote signals or barrier semaphores. Data moves between devices by JAX's collectives and lax.ppermute only.
A program may use at most 64 MiB of HBM per device.

```python
import math
import jax
import jax.numpy as jnp
from jax import lax

S = 4096
R = 128
K = 128
N_LEAF = 8


def lower_blocks(key, row_count, col_count):
    first_key, second_key = jax.random.split(key)
    lower_part = jax.random.normal(first_key, (row_count, col_count), jnp.float32) * (0.6 / math.sqrt(S))
    diag_part = jax.random.uniform(second_key, (row_count, col_count), jnp.float32, 0.5, 1.5)
    row_ids = jax.lax.broadcasted_iota(jnp.int32, (row_count, col_count), 0)
    col_ids = jax.lax.broadcasted_iota(jnp.int32, (row_count, col_count), 1) % S
    return jnp.where(col_ids < row_ids, lower_part, jnp.where(col_ids == row_ids, diag_part, 0.0))


def draw_winv_top(key, part):
    return lower_blocks(jax.random.fold_in(key, 11), S, S).astype(jnp.bfloat16)


def draw_winv_mid(key, part):
    return lower_blocks(jax.random.fold_in(key, 23), S, 2 * S).astype(jnp.bfloat16)


def steps_of(own_key, dims, cuts, low, largest):
    def one(position, shards_of):
        steps = jax.random.uniform(jax.random.fold_in(jax.random.fold_in(own_key, 6), position), (shards_of,), jnp.float32, low / len(cuts), largest / len(cuts))
        return jnp.repeat(jnp.exp(steps), dims[position] // shards_of).reshape((-1,) + (1,) * (len(dims) - position - 1))

    gain = one(*cuts[0])
    for cut in cuts[1:]:
        gain = gain * one(*cut)
    return gain


def gaussian(stream_key, shape, scale, bound, pieces=(), held_as=jnp.bfloat16):
    entries = jax.random.normal(stream_key, shape, jnp.float32) * scale
    if len(pieces) > 0:
        entries = steps_of(stream_key, shape, pieces, -0.22, 0.18) * entries
    return jnp.clip(entries, min=-bound, max=bound).astype(held_as)


def setup_inputs(seed: int = 0) -> dict:
    seeds = jax.random.split(jax.random.key(seed), 6)
    border = gaussian(seeds[0], (N_LEAF, K, 2 * S), (K * N_LEAF) ** -0.5, 0.1875, ((0, 8), (1, 4)))
    solution = gaussian(seeds[1], (N_LEAF, K, R), 1.0, 6.0, ((0, 8), (1, 4)))
    winv_top = draw_winv_top(jax.random.fold_in(seeds[5], 71), 0)
    winv_mid = draw_winv_mid(jax.random.fold_in(seeds[5], 71), 0)
    coupling = gaussian(seeds[4], (2 * S, S), (2 * S) ** -0.5, 0.0625, ((0, 32),))
    return dict(border=border, solution=solution, winv_top=winv_top, winv_mid=winv_mid, coupling=coupling)


def add_leaf(running, inputs):
    border_rows, leaf_solution = inputs
    term = lax.dot_general(border_rows, leaf_solution, (((0,), (0,)), ((), ())), preferred_element_type=jnp.float32)
    return running + term, None


def reference(border, solution, winv_top, winv_mid, coupling):
    half_leaves = N_LEAF // 2
    totals = []
    for group_idx in range(2):
        initial = jnp.zeros((2 * S, R), jnp.float32)
        summed, unused = lax.scan(add_leaf, initial, (border[group_idx * half_leaves:(group_idx + 1) * half_leaves], solution[group_idx * half_leaves:(group_idx + 1) * half_leaves]))
        totals.append(summed)
    top_load = totals[0][:S] + totals[1][:S]
    top_factor = winv_top.astype(jnp.float32)
    top_inner = jnp.dot(top_factor, top_load, precision=lax.Precision.HIGHEST)
    top_adjoint = jnp.dot(top_factor.T, top_inner, precision=lax.Precision.HIGHEST)
    results = []
    for group_idx in range(2):
        factor = winv_mid[:, group_idx * S:(group_idx + 1) * S].astype(jnp.float32)
        couple = coupling[group_idx * S:(group_idx + 1) * S].astype(jnp.float32)
        mid_rhs = totals[group_idx][S:] - jnp.dot(couple, top_adjoint, precision=lax.Precision.HIGHEST)
        mid_inner = jnp.dot(factor, mid_rhs, precision=lax.Precision.HIGHEST)
        results.append(jnp.dot(factor.T, mid_inner, precision=lax.Precision.HIGHEST))
    return top_adjoint, jnp.concatenate(results, 0)
```

```python
import functools

import jax
import jax.numpy as jnp
from jax import lax
from jax.experimental import pallas as pl
from jax.experimental.pallas import tpu as pltpu
from jax.sharding import PartitionSpec as P

AXES = ("leaf", "panel")
F32 = jnp.float32
BF16 = jnp.bfloat16
LANES = 128


def plain_body(border, solution, winv_top, winv_mid, coupling):
    leaves = lax.axis_size("leaf")
    panels = lax.axis_size("panel")
    half = leaves // 2
    leaf_id = lax.axis_index("leaf")
    front = winv_top.shape[0]
    top_cols = winv_top.shape[1]
    mid_cols = winv_mid.shape[1]
    contribution = lax.dot_general(
        border[0], solution[0], (((0,), (0,)), ((), ())), preferred_element_type=F32
    )
    groups = [list(range(half)), list(range(half, leaves))]
    device = leaf_id * panels + lax.axis_index("panel")
    in_half = device % (half * panels)
    top_load = lax.psum(contribution[:front], AXES)
    top_block = lax.dynamic_slice_in_dim(top_load, device * top_cols, top_cols, 0)
    mid_load = lax.psum(contribution[front:], "panel")
    mid_load = lax.psum(mid_load, "leaf", axis_index_groups=groups)
    mid_block = lax.dynamic_slice_in_dim(mid_load, in_half * mid_cols, mid_cols, 0)
    top_factor = winv_top.astype(F32)
    mid_factor = winv_mid.astype(F32)
    exact = lax.Precision.HIGHEST
    top_inner = lax.psum(jnp.dot(top_factor, top_block, precision=exact), AXES)
    top_adjoint = jnp.dot(top_factor.T, top_inner, precision=exact)
    top_whole = lax.all_gather(top_adjoint, AXES, axis=0, tiled=True)
    mid_rhs = mid_block - jnp.dot(coupling.astype(F32), top_whole, precision=exact)
    mid_inner = lax.psum(jnp.dot(mid_factor, mid_rhs, precision=exact), "panel")
    mid_inner = lax.psum(mid_inner, "leaf", axis_index_groups=groups)
    mid_adjoint = jnp.dot(mid_factor.T, mid_inner, precision=exact)
    return top_adjoint, mid_adjoint


def swap(value, mask):
    count = lax.axis_size("leaf") * lax.axis_size("panel")
    return lax.ppermute(value, AXES, [(i, i ^ mask) for i in range(count)])


CORE, XBIT, YBIT, ZBIT = 1, 2, 4, 8


def coords():
    leaf = lax.axis_index("leaf")
    panel = lax.axis_index("panel")
    return leaf // 2, leaf % 2, panel // 2, panel % 2


def kernel_call(kernel, outs, ins, scratch=(), flops=0, limit=24):
    vmem = pl.BlockSpec(memory_space=pltpu.VMEM)
    size = lambda s: s.size * s.dtype.itemsize
    return pl.pallas_call(
        kernel,
        out_shape=[jax.ShapeDtypeStruct(*o) for o in outs],
        in_specs=[vmem] * len(ins),
        out_specs=[vmem] * len(outs),
        scratch_shapes=list(scratch),
        compiler_params=pltpu.CompilerParams(vmem_limit_bytes=limit * 2**20),
        cost_estimate=pl.CostEstimate(
            flops=flops,
            transcendentals=0,
            bytes_accessed=sum(map(size, ins))
            + sum(size(jax.ShapeDtypeStruct(*o)) for o in outs),
        ),
    )(*ins)


def split2(value):
    high = value.astype(BF16)
    low = (value - high.astype(F32)).astype(BF16)
    return high, low


def xor(a, k):
    return lax.bitwise_xor(a, jnp.int32(k))


def flip(a, k):
    return a + k - 2 * a * k if k else a


def zrel(z, k, nz):
    low, high = z % 2, z // 2
    if nz == 2:
        return flip(low, k)
    return flip(high, k // 2) * 2 + flip(low, k % 2)


def block_row(z, y, x, nz, rows, zk, yk, xk, colour):
    block = zrel(z, zk, nz) * 4 + flip(y, yk) * 2 + flip(x, xk)
    return pl.multiple_of(block * (2 * rows) + colour * rows, rows)


def prep_border(border_ref, sol_ref, *out_refs):
    z, y, x, c = coords()
    tops, mids = out_refs[:8], out_refs[8:]
    front = border_ref.shape[1] // 2
    sol = sol_ref[...].astype(F32)
    for rel in range(8):
        peer = flip(y, rel // 4) * 4 + flip(x, rel // 2 % 2) * 2 + flip(c, rel % 2)
        for k in range(4):
            cols = pl.ds(pl.multiple_of(k * 1024 + peer * 128, 128), 128)
            tops[rel][:, k * 128 : (k + 1) * 128] = border_ref[:, cols].astype(F32)
        tops[rel][:, 512:640] = sol
        for k in range(2):
            cols = pl.ds(pl.multiple_of(front + k * 2048 + peer * 256, 256), 256)
            mids[rel][:, k * 256 : (k + 1) * 256] = border_ref[:, cols].astype(F32)


def top_load_kernel(*refs):
    ins, outs, (rows_ref, sol_ref, sum_ref) = refs[:8], refs[8:13], refs[13:]
    z, y, x, c = coords()
    for i in range(8):
        rows_ref[i * 32 : (i + 1) * 32, :] = ins[i][:, :512].astype(BF16)
        sol_ref[i * 32 : (i + 1) * 32, :] = ins[i][:, 512:640].astype(BF16)
    sum_ref[...] = lax.dot_general(
        sol_ref[...], rows_ref[...], (((0,), (0,)), ((), ())), preferred_element_type=F32
    )
    for k in range(4):
        cols = pl.ds(pl.multiple_of(zrel(z, k, 4) * 128, 128), 128)
        outs[k][...] = sum_ref[:, cols].T
    outs[4][...] = sol_ref[...]


def mid_load_kernel(*refs):
    ins, sol_ref, outs, (rows_ref, sum_ref) = refs[:8], refs[8], refs[9:11], refs[11:]
    z, y, x, c = coords()
    for i in range(8):
        rows_ref[i * 32 : (i + 1) * 32, :] = ins[i][...].astype(BF16)
    sum_ref[...] = lax.dot_general(
        sol_ref[...], rows_ref[...], (((0,), (0,)), ((), ())), preferred_element_type=F32
    )
    for k in range(2):
        cols = pl.ds(pl.multiple_of(zrel(z, k, 2) * 256, 256), 256)
        outs[k][...] = sum_ref[:, cols].T


def halve_rows(w_ref, keep_ref, send_ref):
    z, y, x, c = coords()
    rows = w_ref.shape[0] // 2
    keep_ref[...] = w_ref[pl.ds(pl.multiple_of(c * rows, rows), rows), :]
    send_ref[...] = w_ref[pl.ds(pl.multiple_of((1 - c) * rows, rows), rows), :].astype(F32)


def halve_cols(w_ref, keep_ref, send_ref):
    z, y, x, c = coords()
    for i in range(w_ref.shape[1] // 256):
        here = slice(i * 128, (i + 1) * 128)
        kept = pl.multiple_of(i * 256 + c * 128, 128)
        sent = pl.multiple_of(i * 256 + (1 - c) * 128, 128)
        keep_ref[:, here] = w_ref[:, pl.ds(kept, 128)]
        send_ref[:, here] = w_ref[:, pl.ds(sent, 128)].astype(F32)


def join_cols(keep_ref, recv_ref, w_ref, t_ref):
    n = keep_ref.shape[1]
    w_ref[:, :n] = keep_ref[...]
    w_ref[:, n:] = recv_ref[...].astype(BF16)
    t_ref[:n, :] = keep_ref[...].T
    t_ref[n:, :] = recv_ref[...].astype(BF16).T


def join_rows(keep_ref, recv_ref, w_ref):
    n = keep_ref.shape[0]
    w_ref[:n, :] = keep_ref[...]
    w_ref[n:, :] = recv_ref[...].astype(BF16)


PLACES = [(xk, yk) for xk in range(2) for yk in range(2)]


def scatter_blocks(sum_ref, outs, nz, rows):
    z, y, x, c = coords()
    for colour in range(2):
        for p, (xk, yk) in enumerate(PLACES):
            for zk in range(nz):
                start = block_row(z, y, x, nz, rows, zk, yk, xk, colour)
                outs[colour * 4 + p][zk * rows : (zk + 1) * rows, :] = sum_ref[
                    pl.ds(start, rows), :
                ]


def gather_blocks(pieces, rhs_ref, nz, rows):
    z, y, x, c = coords()
    for colour in range(2):
        for p, (xk, yk) in enumerate(PLACES):
            for zk in range(nz):
                start = block_row(z, y, x, nz, rows, zk, yk, xk, colour)
                high, low = split2(pieces[colour * 4 + p][zk * rows : (zk + 1) * rows, :])
                rhs_ref[pl.ds(start, rows), :LANES] = high
                rhs_ref[pl.ds(start, rows), LANES:] = low


def forward(nz, rows, w_ref, *refs):
    vec, outs, (rhs_ref, sum_ref) = refs[:-10], refs[-10:-2], refs[-2:]
    if len(vec) == 2:
        pair = [vec[0][...], vec[1][...]]
    else:
        mine, theirs, part0, part1, recv0, recv1 = vec
        pair = [
            mine[...] - part0[...] - recv1[...],
            theirs[...] - part1[...] - recv0[...],
        ]
    n = pair[0].shape[0]
    for i in range(2):
        high, low = split2(pair[i])
        rhs_ref[i * n : (i + 1) * n, :LANES] = high
        rhs_ref[i * n : (i + 1) * n, LANES:] = low
    both = jnp.dot(w_ref[...], rhs_ref[...], preferred_element_type=F32)
    sum_ref[...] = both[:, :LANES] + both[:, LANES:]
    scatter_blocks(sum_ref, outs, nz, rows)


def backward(nz, rows, w_ref, *refs):
    pieces, (own_ref, other_ref), rhs_ref = refs[:8], refs[8:10], refs[10]
    gather_blocks(pieces, rhs_ref, nz, rows)
    both = jnp.dot(w_ref[...], rhs_ref[...], preferred_element_type=F32)
    total = both[:, :LANES] + both[:, LANES:]
    n = own_ref.shape[0]
    own_ref[...] = total[:n]
    other_ref[...] = total[n:]


def run_forward(w, vec, nz, rows):
    m, k = w.shape
    return kernel_call(
        functools.partial(forward, nz, rows),
        [((m // 8, LANES), F32)] * 8,
        [w, *vec],
        [pltpu.VMEM((k, 2 * LANES), BF16), pltpu.VMEM((m, LANES), F32)],
        flops=4 * m * k * LANES,
    )


def run_backward(w, pieces, nz, rows):
    m, k = w.shape
    return kernel_call(
        functools.partial(backward, nz, rows),
        [((m // 2, LANES), F32)] * 2,
        [w, *pieces],
        [pltpu.VMEM((k, 2 * LANES), BF16)],
        flops=4 * m * k * LANES,
    )


def plane_sum(pieces):
    a00, a01, a10, a11, b00, b01, b10, b11 = pieces
    ra = swap(a11, XBIT)
    rb = swap(b11, YBIT)
    qa = swap(a10, XBIT)
    qb = swap(b01, YBIT)
    sa = swap(a01 + ra, YBIT)
    sb = swap(b10 + rb, XBIT)
    return a00 + qa + sa, b00 + qb + sb


def plane_spread(a, b):
    ya = swap(a, YBIT)
    xb = swap(b, XBIT)
    xa = swap(a, XBIT)
    yb = swap(b, YBIT)
    return [a, ya, xa, swap(ya, XBIT), b, yb, xb, swap(xb, YBIT)]


def depth_sum(a, b, nz, rows):
    cut = lambda k: jnp.concatenate(
        [a[k * rows : (k + 1) * rows], b[k * rows : (k + 1) * rows]], 0
    )
    got = [swap(cut(k), ZBIT * k) for k in range(1, nz)]
    total = cut(0)
    for g in got:
        total = total + g
    return total


def depth_spread(own, nz, rows):
    parts = [own] + [swap(own, ZBIT * k) for k in range(1, nz)]
    a = jnp.concatenate([p[:rows] for p in parts], 0)
    b = jnp.concatenate([p[rows:] for p in parts], 0)
    return a, b


def everywhere(own, nz, rows):
    return plane_spread(*depth_spread(own, nz, rows))


def fast_body(border, solution, winv_top, winv_mid, coupling):
    front = winv_top.shape[0]
    half = front // 2
    out = kernel_call(
        prep_border,
        [((32, 640), F32)] * 8 + [((32, 512), F32)] * 8,
        [border[0], solution[0]],
    )
    tops, mids = out[:8], out[8:]
    tops = [tops[0]] + [swap(tops[r], r) for r in range(1, 8)]
    *loads, sol_all = kernel_call(
        top_load_kernel,
        [((128, LANES), F32)] * 4 + [((256, LANES), BF16)],
        tops,
        [
            pltpu.VMEM((256, 512), BF16),
            pltpu.VMEM((256, LANES), BF16),
            pltpu.VMEM((LANES, 512), F32),
        ],
        flops=2 * 256 * 512 * 128,
    )
    load = loads[0]
    for k in range(1, 4):
        load = load + swap(loads[k], ZBIT * k)
    load_other = swap(load, CORE)

    top_keep, top_send = kernel_call(
        halve_rows, [((half, 128), BF16), ((half, 128), F32)], [winv_top]
    )
    cou_keep, cou_send = kernel_call(
        halve_cols, [((256, half), BF16), ((256, half), F32)], [coupling]
    )
    mid_keep, mid_send = kernel_call(
        halve_rows, [((half, 256), BF16), ((half, 256), F32)], [winv_mid]
    )
    top_w, top_t = kernel_call(
        join_cols,
        [((half, 256), BF16), ((256, half), BF16)],
        [top_keep, swap(top_send, CORE)],
    )
    (cou_w,) = kernel_call(
        join_rows, [((512, half), BF16)], [cou_keep, swap(cou_send, CORE)]
    )
    mid_w, mid_t = kernel_call(
        join_cols,
        [((half, 512), BF16), ((512, half), BF16)],
        [mid_keep, swap(mid_send, CORE)],
    )

    pieces = run_forward(top_w, [load, load_other], 4, 64)
    inner = depth_sum(*plane_sum(pieces), 4, 64)
    own, other = run_backward(top_t, everywhere(inner, 4, 64), 4, 64)
    top_adjoint = own + swap(other, CORE)

    mids = [mids[0]] + [swap(mids[r], r) for r in range(1, 8)]
    mid0, mid1 = kernel_call(
        mid_load_kernel,
        [((256, LANES), F32)] * 2,
        [*mids, sol_all],
        [pltpu.VMEM((256, 512), BF16), pltpu.VMEM((LANES, 512), F32)],
        flops=2 * 256 * 512 * 128,
    )
    mid_load = mid0 + swap(mid1, ZBIT)
    mid_other = swap(mid_load, CORE)

    part0, part1 = run_backward(cou_w, everywhere(top_adjoint, 4, 64), 4, 64)
    vec = [mid_load, mid_other, part0, part1, swap(part0, CORE), swap(part1, CORE)]
    pieces = run_forward(mid_w, vec, 2, 128)
    inner = depth_sum(*plane_sum(pieces), 2, 128)
    own, other = run_backward(mid_t, everywhere(inner, 2, 128), 2, 128)
    return top_adjoint, own + swap(other, CORE)


def solution(mesh):
    placed = (
        P("leaf", "panel", None),
        P("leaf", "panel", None),
        P(None, AXES),
        P(None, AXES),
        P(AXES, None),
    )
    fits = mesh.shape["leaf"] == 8 and mesh.shape["panel"] == 4
    return jax.shard_map(
        fast_body if fits else plain_body,
        mesh=mesh,
        in_specs=placed,
        out_specs=(P(AXES, None), P(AXES, None)),
        check_vma=False,
    )
```

```python
import functools

import jax
import jax.numpy as jnp
from jax import lax
from jax.experimental import pallas as pl
from jax.experimental.pallas import tpu as pltpu
from jax.sharding import PartitionSpec as P

AXES = ("leaf", "panel")
F32 = jnp.float32
BF16 = jnp.bfloat16
LANES = 128


def plain_body(border, solution, winv_top, winv_mid, coupling):
    leaves = lax.axis_size("leaf")
    panels = lax.axis_size("panel")
    half = leaves // 2
    leaf_id = lax.axis_index("leaf")
    front = winv_top.shape[0]
    top_cols = winv_top.shape[1]
    mid_cols = winv_mid.shape[1]
    contribution = lax.dot_general(
        border[0], solution[0], (((0,), (0,)), ((), ())), preferred_element_type=F32
    )
    groups = [list(range(half)), list(range(half, leaves))]
    device = leaf_id * panels + lax.axis_index("panel")
    in_half = device % (half * panels)
    top_load = lax.psum(contribution[:front], AXES)
    top_block = lax.dynamic_slice_in_dim(top_load, device * top_cols, top_cols, 0)
    mid_load = lax.psum(contribution[front:], "panel")
    mid_load = lax.psum(mid_load, "leaf", axis_index_groups=groups)
    mid_block = lax.dynamic_slice_in_dim(mid_load, in_half * mid_cols, mid_cols, 0)
    top_factor = winv_top.astype(F32)
    mid_factor = winv_mid.astype(F32)
    exact = lax.Precision.HIGHEST
    top_inner = lax.psum(jnp.dot(top_factor, top_block, precision=exact), AXES)
    top_adjoint = jnp.dot(top_factor.T, top_inner, precision=exact)
    top_whole = lax.all_gather(top_adjoint, AXES, axis=0, tiled=True)
    mid_rhs = mid_block - jnp.dot(coupling.astype(F32), top_whole, precision=exact)
    mid_inner = lax.psum(jnp.dot(mid_factor, mid_rhs, precision=exact), "panel")
    mid_inner = lax.psum(mid_inner, "leaf", axis_index_groups=groups)
    mid_adjoint = jnp.dot(mid_factor.T, mid_inner, precision=exact)
    return top_adjoint, mid_adjoint


def swap(value, mask):
    return lax.ppermute(value, AXES, [(i, i ^ mask) for i in range(32)])


CORE, ZBIT = 1, 8
PLANE8 = [[z * 8 + p for p in range(8)] for z in range(4)]
PLANE4 = [[z * 8 + p * 2 + c for p in range(4)] for z in range(4) for c in range(2)]
DEPTH4 = [[z * 8 + p for z in range(4)] for p in range(8)]


def exchange(value, groups):
    return lax.all_to_all(value, AXES, 0, 0, axis_index_groups=groups, tiled=True)


def sum_over(value, groups):
    got = exchange(value, groups)
    total = got[0]
    for i in range(1, got.shape[0]):
        total = total + got[i]
    return total


def spread(value, groups):
    return exchange(jnp.broadcast_to(value, (4, *value.shape)), groups)


def coords():
    leaf = lax.axis_index("leaf")
    panel = lax.axis_index("panel")
    return leaf // 2, leaf % 2, panel // 2, panel % 2


def kernel_call(kernel, outs, ins, scratch=(), flops=0, limit=24):
    vmem = pl.BlockSpec(memory_space=pltpu.VMEM)
    size = lambda s: s.size * s.dtype.itemsize
    return pl.pallas_call(
        kernel,
        out_shape=[jax.ShapeDtypeStruct(*o) for o in outs],
        in_specs=[vmem] * len(ins),
        out_specs=[vmem] * len(outs),
        scratch_shapes=list(scratch),
        compiler_params=pltpu.CompilerParams(vmem_limit_bytes=limit * 2**20),
        cost_estimate=pl.CostEstimate(
            flops=flops,
            transcendentals=0,
            bytes_accessed=sum(map(size, ins))
            + sum(size(jax.ShapeDtypeStruct(*o)) for o in outs),
        ),
    )(*ins)


def split2(value):
    high = value.astype(BF16)
    low = (value - high.astype(F32)).astype(BF16)
    return high, low


def prep_border(border_ref, sol_ref, top_ref, mid_ref):
    front = border_ref.shape[1] // 2
    sol = sol_ref[...].astype(F32)
    for p in range(8):
        for k in range(4):
            col = k * 1024 + p * 128
            top_ref[p, :, k * 128 : (k + 1) * 128] = border_ref[:, col : col + 128].astype(F32)
        top_ref[p, :, 512:640] = sol
        for k in range(2):
            col = front + k * 2048 + p * 256
            mid_ref[p, :, k * 256 : (k + 1) * 256] = border_ref[:, col : col + 256].astype(F32)


def top_load_kernel(in_ref, out_ref, sol_ref):
    rows = in_ref[:, :512].astype(BF16)
    sol_ref[...] = in_ref[:, 512:640].astype(BF16)
    total = lax.dot_general(
        sol_ref[...], rows, (((0,), (0,)), ((), ())), preferred_element_type=F32
    )
    for k in range(4):
        out_ref[k] = total[:, k * 128 : (k + 1) * 128].T


def mid_load_kernel(in_ref, sol_ref, keep_ref, send_ref):
    z, y, x, c = coords()
    total = lax.dot_general(
        sol_ref[...], in_ref[...].astype(BF16), (((0,), (0,)), ((), ())),
        preferred_element_type=F32,
    ).T
    low, high = total[:256], total[256:]
    here = z % 2 == 0
    keep_ref[...] = jnp.where(here, low, high)
    send_ref[...] = jnp.where(here, high, low)


def halve_rows(w_ref, keep_ref, send_ref):
    z, y, x, c = coords()
    rows = w_ref.shape[0] // 2
    keep_ref[...] = w_ref[pl.ds(pl.multiple_of(c * rows, rows), rows), :]
    send_ref[...] = w_ref[pl.ds(pl.multiple_of((1 - c) * rows, rows), rows), :].astype(F32)


def halve_cols(w_ref, keep_ref, send_ref):
    z, y, x, c = coords()
    for i in range(w_ref.shape[1] // 256):
        here = slice(i * 128, (i + 1) * 128)
        kept = pl.multiple_of(i * 256 + c * 128, 128)
        sent = pl.multiple_of(i * 256 + (1 - c) * 128, 128)
        keep_ref[:, here] = w_ref[:, pl.ds(kept, 128)]
        send_ref[:, here] = w_ref[:, pl.ds(sent, 128)].astype(F32)


def join_cols(keep_ref, recv_ref, w_ref, t_ref):
    n = keep_ref.shape[1]
    w_ref[:, :n] = keep_ref[...]
    w_ref[:, n:] = recv_ref[...].astype(BF16)
    t_ref[:n, :] = keep_ref[...].T
    t_ref[n:, :] = recv_ref[...].astype(BF16).T


def join_rows(keep_ref, recv_ref, w_ref):
    n = keep_ref.shape[0]
    w_ref[:n, :] = keep_ref[...]
    w_ref[n:, :] = recv_ref[...].astype(BF16)


def forward(nz, w_ref, *refs):
    vec, out_ref, rhs_ref = refs[:-2], refs[-2], refs[-1]
    if len(vec) == 2:
        pair = [vec[0][...], vec[1][...]]
    else:
        mine, theirs, part0, part1, recv0, recv1 = vec
        pair = [
            mine[...] - part0[...] - recv1[...],
            theirs[...] - part1[...] - recv0[...],
        ]
    n = pair[0].shape[0]
    for i in range(2):
        high, low = split2(pair[i])
        rhs_ref[i * n : (i + 1) * n, :LANES] = high
        rhs_ref[i * n : (i + 1) * n, LANES:] = low
    both = jnp.dot(w_ref[...], rhs_ref[...], preferred_element_type=F32)
    total = both[:, :LANES] + both[:, LANES:]
    rows = w_ref.shape[0] // (4 * nz)
    for k in range(nz):
        for p in range(4):
            start = (k * 4 + p) * rows
            out_ref[p, k] = total[start : start + rows]


def backward(nz, w_ref, in_ref, own_ref, other_ref, rhs_ref):
    rows = rhs_ref.shape[0] // (4 * nz)
    for k in range(nz):
        for p in range(4):
            start = (k * 4 + p) * rows
            high, low = split2(in_ref[p, k])
            rhs_ref[start : start + rows, :LANES] = high
            rhs_ref[start : start + rows, LANES:] = low
    both = jnp.dot(w_ref[...], rhs_ref[...], preferred_element_type=F32)
    total = both[:, :LANES] + both[:, LANES:]
    n = own_ref.shape[0]
    own_ref[...] = total[:n]
    other_ref[...] = total[n:]


def run_forward(w, vec, nz):
    m, k = w.shape
    return kernel_call(
        functools.partial(forward, nz),
        [((4, nz, m // (4 * nz), LANES), F32)],
        [w, *vec],
        [pltpu.VMEM((k, 2 * LANES), BF16)],
        flops=4 * m * k * LANES,
    )[0]


def run_backward(w, pieces, nz):
    m, k = w.shape
    return kernel_call(
        functools.partial(backward, nz),
        [((m // 2, LANES), F32)] * 2,
        [w, pieces],
        [pltpu.VMEM((k, 2 * LANES), BF16)],
        flops=4 * m * k * LANES,
    )


def pair_spread(own, z):
    got = swap(own, ZBIT)
    here = z % 2 == 0
    return jnp.stack([jnp.where(here, own, got), jnp.where(here, got, own)])


def pair_sum(parts, z):
    here = z % 2 == 0
    keep = jnp.where(here, parts[0], parts[1])
    return keep + swap(jnp.where(here, parts[1], parts[0]), ZBIT)


def fast_body(border, solution, winv_top, winv_mid, coupling):
    front = winv_top.shape[0]
    half = front // 2
    z = lax.axis_index("leaf") // 2
    top_out, mid_out = kernel_call(
        prep_border,
        [((8, 32, 640), F32), ((8, 32, 512), F32)],
        [border[0], solution[0]],
    )
    top_in = exchange(top_out, PLANE8).reshape(256, 640)
    loads, sol_all = kernel_call(
        top_load_kernel,
        [((4, 128, LANES), F32), ((256, LANES), BF16)],
        [top_in],
        flops=2 * 256 * 512 * 128,
    )
    load = sum_over(loads, DEPTH4)
    load_other = swap(load, CORE)

    top_keep, top_send = kernel_call(
        halve_rows, [((half, 128), BF16), ((half, 128), F32)], [winv_top]
    )
    cou_keep, cou_send = kernel_call(
        halve_cols, [((256, half), BF16), ((256, half), F32)], [coupling]
    )
    mid_keep, mid_send = kernel_call(
        halve_rows, [((half, 256), BF16), ((half, 256), F32)], [winv_mid]
    )
    top_w, top_t = kernel_call(
        join_cols,
        [((half, 256), BF16), ((256, half), BF16)],
        [top_keep, swap(top_send, CORE)],
    )
    (cou_w,) = kernel_call(
        join_rows, [((512, half), BF16)], [cou_keep, swap(cou_send, CORE)]
    )
    mid_w, mid_t = kernel_call(
        join_cols,
        [((half, 512), BF16), ((512, half), BF16)],
        [mid_keep, swap(mid_send, CORE)],
    )

    parts = run_forward(top_w, [load, load_other], 4)
    inner = sum_over(sum_over(parts, PLANE4), DEPTH4)
    pieces = spread(spread(inner, DEPTH4), PLANE4)
    own, other = run_backward(top_t, pieces, 4)
    top_adjoint = own + swap(other, CORE)

    mid_in = exchange(mid_out, PLANE8).reshape(256, 512)
    mid_keep_load, mid_send_load = kernel_call(
        mid_load_kernel,
        [((256, LANES), F32)] * 2,
        [mid_in, sol_all],
        flops=2 * 256 * 512 * 128,
    )
    mid_load = mid_keep_load + swap(mid_send_load, ZBIT)
    mid_other = swap(mid_load, CORE)

    pieces = spread(spread(top_adjoint, DEPTH4), PLANE4)
    part0, part1 = run_backward(cou_w, pieces, 4)
    vec = [mid_load, mid_other, part0, part1, swap(part0, CORE), swap(part1, CORE)]
    parts = run_forward(mid_w, vec, 2)
    inner = pair_sum(sum_over(parts, PLANE4), z)
    pieces = spread(pair_spread(inner, z), PLANE4)
    own, other = run_backward(mid_t, pieces, 2)
    return top_adjoint, own + swap(other, CORE)


def solution(mesh):
    placed = (
        P("leaf", "panel", None),
        P("leaf", "panel", None),
        P(None, AXES),
        P(None, AXES),
        P(AXES, None),
    )
    fits = mesh.shape["leaf"] == 8 and mesh.shape["panel"] == 4
    return jax.shard_map(
        fast_body if fits else plain_body,
        mesh=mesh,
        in_specs=placed,
        out_specs=(P(AXES, None), P(AXES, None)),
        check_vma=False,
    )
```

```python
import functools

import jax
import jax.numpy as jnp
from jax import lax
from jax.experimental import pallas as pl
from jax.experimental.pallas import tpu as pltpu
from jax.sharding import PartitionSpec as P

AXES = ("leaf", "panel")
F32 = jnp.float32
BF16 = jnp.bfloat16
LANES = 128


def plain_body(border, solution, winv_top, winv_mid, coupling):
    leaves = lax.axis_size("leaf")
    panels = lax.axis_size("panel")
    half = leaves // 2
    leaf_id = lax.axis_index("leaf")
    front = winv_top.shape[0]
    top_cols = winv_top.shape[1]
    mid_cols = winv_mid.shape[1]
    contribution = lax.dot_general(
        border[0], solution[0], (((0,), (0,)), ((), ())), preferred_element_type=F32
    )
    groups = [list(range(half)), list(range(half, leaves))]
    device = leaf_id * panels + lax.axis_index("panel")
    in_half = device % (half * panels)
    top_load = lax.psum(contribution[:front], AXES)
    top_block = lax.dynamic_slice_in_dim(top_load, device * top_cols, top_cols, 0)
    mid_load = lax.psum(contribution[front:], "panel")
    mid_load = lax.psum(mid_load, "leaf", axis_index_groups=groups)
    mid_block = lax.dynamic_slice_in_dim(mid_load, in_half * mid_cols, mid_cols, 0)
    top_factor = winv_top.astype(F32)
    mid_factor = winv_mid.astype(F32)
    exact = lax.Precision.HIGHEST
    top_inner = lax.psum(jnp.dot(top_factor, top_block, precision=exact), AXES)
    top_adjoint = jnp.dot(top_factor.T, top_inner, precision=exact)
    top_whole = lax.all_gather(top_adjoint, AXES, axis=0, tiled=True)
    mid_rhs = mid_block - jnp.dot(coupling.astype(F32), top_whole, precision=exact)
    mid_inner = lax.psum(jnp.dot(mid_factor, mid_rhs, precision=exact), "panel")
    mid_inner = lax.psum(mid_inner, "leaf", axis_index_groups=groups)
    mid_adjoint = jnp.dot(mid_factor.T, mid_inner, precision=exact)
    return top_adjoint, mid_adjoint


CHAINS = 2
WIDE = 64


def permute(value, partner):
    return lax.ppermute(value, AXES, [(i, partner(i)) for i in range(32)])


def swap_core(value):
    return permute(value, lambda i: i ^ 1)


def swap_first(value):
    return permute(value, lambda i: i ^ (4 if i & 1 else 2))


def swap_second(value):
    return permute(value, lambda i: i ^ (2 if i & 1 else 4))


def swap_cross(value):
    return permute(value, lambda i: i ^ (3 if i & 1 else 5))


def swap_near(value):
    return permute(value, lambda i: i ^ 8)


def swap_far(value):
    return permute(value, lambda i: i ^ 16)


def coords():
    leaf = lax.axis_index("leaf")
    panel = lax.axis_index("panel")
    return leaf // 2, leaf % 2, panel // 2, panel % 2


def flip(a, k):
    return a + k - 2 * a * k


def z_flip(z, k):
    return flip(z // 2, k // 2) * 2 + flip(z % 2, k % 2)


Z_ORDER = (0, 2, 1, 3)


def plane_at(y, x, c, first, second):
    along_x = first * (1 - c) + second * c
    along_y = first * c + second * (1 - c)
    return flip(y, along_y) * 2 + flip(x, along_x)


def block_starts(deep):
    z, y, x, c = coords()
    starts = []
    for first in range(2):
        for second in range(2):
            plane = plane_at(y, x, c, first, second)
            for j in range(4):
                if deep:
                    start = (z_flip(z, Z_ORDER[j]) * 4 + plane) * 128
                else:
                    start = (flip(z % 2, j // 2) * 4 + plane) * 256 + j % 2 * 128
                starts.append(pl.multiple_of(start, 128))
    return starts


def kernel_call(kernel, outs, ins, scratch=(), flops=0, limit=24):
    vmem = pl.BlockSpec(memory_space=pltpu.VMEM)
    size = lambda s: s.size * s.dtype.itemsize
    return pl.pallas_call(
        kernel,
        out_shape=[jax.ShapeDtypeStruct(*o) for o in outs],
        in_specs=[vmem] * len(ins),
        out_specs=[vmem] * len(outs),
        scratch_shapes=list(scratch),
        compiler_params=pltpu.CompilerParams(vmem_limit_bytes=limit * 2**20),
        cost_estimate=pl.CostEstimate(
            flops=flops,
            transcendentals=0,
            bytes_accessed=sum(map(size, ins))
            + sum(size(jax.ShapeDtypeStruct(*o)) for o in outs),
        ),
    )(*ins)


def left_lanes(shape):
    return lax.broadcasted_iota(jnp.int32, shape, 1) < WIDE


def pack(low, high):
    left = left_lanes(low.shape)
    return (
        jnp.where(left, low, pltpu.roll(high, WIDE, 1)),
        jnp.where(left, pltpu.roll(low, WIDE, 1), high),
    )


def put_split(rhs_ref, start, block):
    left = left_lanes(block.shape)
    turned = pltpu.roll(block, WIDE, 1)
    for i, rows in enumerate((jnp.where(left, block, turned), jnp.where(left, turned, block))):
        high = rows.astype(BF16).astype(F32)
        both = jnp.where(left, high, rows - high)
        rhs_ref[pl.ds(start + i * WIDE, WIDE), :] = both.astype(BF16)


def product(w_ref, rhs_ref):
    both = jnp.dot(w_ref[...], rhs_ref[...], preferred_element_type=F32)
    return both + pltpu.roll(both, WIDE, 1)


def take_block(total, start):
    low = total[start : start + WIDE]
    high = total[start + WIDE : start + 2 * WIDE]
    return jnp.where(left_lanes(low.shape), low, high)


def prep_border(border_ref, sol_ref, *out_refs):
    z, y, x, c = coords()
    tops, mids = out_refs[:4], out_refs[4:]
    front = border_ref.shape[1] // 2
    sol = sol_ref[...].astype(F32)
    for rel in range(4):
        core = flip(c, rel % 2)
        for second in range(2):
            plane = plane_at(y, x, core, rel // 2, second)
            for j in range(4):
                col = pl.multiple_of((z_flip(z, Z_ORDER[j]) * 8 + plane * 2 + core) * 128, 128)
                here = (second * 4 + j) * 128
                tops[rel][:, here : here + 128] = border_ref[:, pl.ds(col, 128)].astype(F32)
            for k in range(2):
                col = front + (flip(z % 2, k) * 8 + plane * 2 + core) * 256
                here = (second * 2 + k) * 256
                mids[rel][:, here : here + 256] = border_ref[
                    :, pl.ds(pl.multiple_of(col, 256), 256)
                ].astype(F32)
        tops[rel][:, 1024:] = sol


def stack_rows(refs, cols, out_ref):
    n = refs[0].shape[0]
    for i, ref in enumerate(refs):
        out_ref[i * n : (i + 1) * n, :] = ref[:, cols].astype(BF16)


def put_loads(sol, rows, outs):
    total = lax.dot_general(
        sol, rows, (((0,), (0,)), ((), ())), preferred_element_type=F32
    )
    for second in range(2):
        for j in range(4):
            here = (second * 4 + j) * 128
            block = total[:, here : here + 128].T
            packed = pack(block[:WIDE], block[WIDE:])
            for h in range(CHAINS):
                outs[h][second][j] = packed[h]


def top_load_kernel(*refs):
    ins, outs, sol_ref, rows_ref = refs[:4], refs[4:8], refs[8], refs[9]
    stack_rows(ins, slice(0, 1024), rows_ref)
    stack_rows(ins, slice(1024, 1152), sol_ref)
    put_loads(sol_ref[...], rows_ref[...], [outs[:2], outs[2:]])


def mid_load_kernel(*refs):
    ins, sol_ref, keep_ref, send_ref, rows_ref = refs[:4], *refs[4:]
    stack_rows(ins, slice(0, 1024), rows_ref)
    outs = [[keep_ref.at[h], send_ref.at[h]] for h in range(CHAINS)]
    put_loads(sol_ref[...], rows_ref[...], outs)


def halve_rows(w_ref, keep_ref, send_ref):
    z, y, x, c = coords()
    rows = w_ref.shape[0] // 2
    keep_ref[...] = w_ref[pl.ds(pl.multiple_of(c * rows, rows), rows), :]
    send_ref[...] = w_ref[pl.ds(pl.multiple_of((1 - c) * rows, rows), rows), :].astype(F32)


def halve_cols(w_ref, keep_ref, send_ref):
    z, y, x, c = coords()
    for i in range(w_ref.shape[1] // 256):
        here = slice(i * 128, (i + 1) * 128)
        kept = pl.multiple_of(i * 256 + c * 128, 128)
        sent = pl.multiple_of(i * 256 + (1 - c) * 128, 128)
        keep_ref[:, here] = w_ref[:, pl.ds(kept, 128)]
        send_ref[:, here] = w_ref[:, pl.ds(sent, 128)].astype(F32)


def join_cols(keep_ref, recv_ref, w_ref, t_ref):
    n = keep_ref.shape[1]
    w_ref[:, :n] = keep_ref[...]
    w_ref[:, n:] = recv_ref[...].astype(BF16)
    t_ref[:n, :] = keep_ref[...].T
    t_ref[n:, :] = recv_ref[...].astype(BF16).T


def join_rows(keep_ref, recv_ref, w_ref):
    n = keep_ref.shape[0]
    w_ref[:n, :] = keep_ref[...]
    w_ref[n:, :] = recv_ref[...].astype(BF16)


def forward(deep, w_ref, *refs):
    vec, (send_ref, next_ref, keep_ref), (rhs_ref, sum_ref) = refs[:-5], refs[-5:-2], refs[-2:]
    blocks = vec[0].shape[0]
    if len(vec) == 2:
        own, other = vec[0][...], vec[1][...]
    else:
        mine, theirs, part, recv = [v[...] for v in vec]
        own = mine - part[:blocks] - recv[blocks:]
        other = theirs - part[blocks:] - recv[:blocks]
    for i in range(blocks):
        put_split(rhs_ref, i * 128, own[i])
        put_split(rhs_ref, (blocks + i) * 128, other[i])
    sum_ref[...] = product(w_ref, rhs_ref)
    left = left_lanes((WIDE, 2 * WIDE))
    for i, start in enumerate(block_starts(deep)):
        low = sum_ref[pl.ds(start, WIDE), :]
        high = sum_ref[pl.ds(start + WIDE, WIDE), :]
        block = jnp.where(left, low, high)
        if i < 4:
            keep_ref[i] = block
        elif i < 8:
            next_ref[i - 4] = block
        else:
            send_ref[i - 8] = block


def backward(deep, w_ref, near_ref, far_ref, out_ref, rhs_ref):
    for i, start in enumerate(block_starts(deep)):
        put_split(rhs_ref, start, near_ref[i] if i < 8 else far_ref[i - 8])
    total = product(w_ref, rhs_ref)
    for i in range(out_ref.shape[0]):
        out_ref[i] = take_block(total, i * 128)


def run_forward(w, vec, deep):
    m, k = w.shape
    return kernel_call(
        functools.partial(forward, deep),
        [((8, WIDE, 128), F32), ((4, WIDE, 128), F32), ((4, WIDE, 128), F32)],
        [w, *vec],
        [pltpu.VMEM((k, 128), BF16), pltpu.VMEM((m, 128), F32)],
        flops=2 * m * k * 128,
    )


def run_backward(w, near, far, deep):
    m, k = w.shape
    return kernel_call(
        functools.partial(backward, deep),
        [((m // 128, WIDE, 128), F32)],
        [w, near, far],
        [pltpu.VMEM((k, 128), BF16)],
        flops=2 * m * k * 128,
    )[0]


def depth_sum(value, deep):
    half = value.shape[-3] // 2
    keep, send = value[..., :half, :, :], value[..., half:, :, :]
    value = keep + swap_near(send)
    if deep:
        value = value[:1] + swap_far(value[1:])
    return value


def whole_sum(send, follow, keep, deep):
    got = swap_first(send)
    got_next = swap_second(follow + got[4:])
    return depth_sum(keep + got[:4] + got_next, deep)


def whole_spread(own, deep):
    if deep:
        own = jnp.concatenate([own, swap_far(own)], 0)
    line = jnp.concatenate([own, swap_near(own)], 0)
    near = jnp.concatenate([line, swap_second(line)], 0)
    return near, swap_first(near)


def unpack(pair):
    blocks = pair[0].shape[0]
    rows = [
        jnp.concatenate([p[:, :, i * WIDE : (i + 1) * WIDE] for p in pair], 2)
        for i in range(2)
    ]
    return jnp.stack(rows, 1).reshape(blocks * 128, 128)


def fast_body(border, solution, winv_top, winv_mid, coupling):
    front = winv_top.shape[0]
    half = front // 2
    out = kernel_call(
        prep_border,
        [((32, 1152), F32)] * 4 + [((32, 1024), F32)] * 4,
        [border[0], solution[0]],
    )
    tops, mids = out[:4], out[4:]
    tops = [tops[0], swap_core(tops[1]), swap_first(tops[2]), swap_cross(tops[3])]
    *loads, sol_all = kernel_call(
        top_load_kernel,
        [((4, WIDE, 128), F32)] * 4 + [((128, 128), BF16)],
        tops,
        [pltpu.VMEM((128, 1024), BF16)],
        flops=2 * 128 * 1024 * 128,
    )
    load = [
        depth_sum(loads[2 * h] + swap_second(loads[2 * h + 1]), True) for h in range(CHAINS)
    ]

    top_keep, top_send = kernel_call(
        halve_rows, [((half, 128), BF16), ((half, 128), F32)], [winv_top]
    )
    cou_keep, cou_send = kernel_call(
        halve_cols, [((256, half), BF16), ((256, half), F32)], [coupling]
    )
    mid_keep, mid_send = kernel_call(
        halve_rows, [((half, 256), BF16), ((half, 256), F32)], [winv_mid]
    )
    top_w, top_t = kernel_call(
        join_cols,
        [((half, 256), BF16), ((256, half), BF16)],
        [top_keep, swap_core(top_send)],
    )
    (cou_w,) = kernel_call(
        join_rows, [((512, half), BF16)], [cou_keep, swap_core(cou_send)]
    )
    mid_w, mid_t = kernel_call(
        join_cols,
        [((half, 512), BF16), ((512, half), BF16)],
        [mid_keep, swap_core(mid_send)],
    )

    mids = [mids[0], swap_core(mids[1]), swap_first(mids[2]), swap_cross(mids[3])]
    keep, send = kernel_call(
        mid_load_kernel,
        [((CHAINS, 4, WIDE, 128), F32)] * 2,
        [*mids, sol_all],
        [pltpu.VMEM((128, 1024), BF16)],
        flops=2 * 128 * 1024 * 128,
    )
    mid_load = depth_sum(keep + swap_second(send), False)
    mid_other = swap_core(mid_load)

    top_out, mid_out = [], []
    for h in range(CHAINS):
        parts = run_forward(top_w, [load[h], swap_core(load[h])], True)
        inner = whole_sum(*parts, True)
        both = run_backward(top_t, *whole_spread(inner, True), True)
        adjoint = both[:1] + swap_core(both[1:])
        top_out.append(adjoint)
        both = run_backward(cou_w, *whole_spread(adjoint, True), True)
        vec = [mid_load[h], mid_other[h], both, swap_core(both)]
        inner = whole_sum(*run_forward(mid_w, vec, False), False)
        both = run_backward(mid_t, *whole_spread(inner, False), False)
        mid_out.append(both[:2] + swap_core(both[2:]))
    return unpack(top_out), unpack(mid_out)


def solution(mesh):
    placed = (
        P("leaf", "panel", None),
        P("leaf", "panel", None),
        P(None, AXES),
        P(None, AXES),
        P(AXES, None),
    )
    fits = mesh.shape["leaf"] == 8 and mesh.shape["panel"] == 4
    return jax.shard_map(
        fast_body if fits else plain_body,
        mesh=mesh,
        in_specs=placed,
        out_specs=(P(AXES, None), P(AXES, None)),
        check_vma=False,
    )
```

```python
import functools

import jax
import jax.numpy as jnp
from jax import lax
from jax.experimental import pallas as pl
from jax.experimental.pallas import tpu as pltpu
from jax.sharding import PartitionSpec as P

AXES = ("leaf", "panel")
F32 = jnp.float32
BF16 = jnp.bfloat16
LANES = 128


def plain_body(border, solution, winv_top, winv_mid, coupling):
    leaves = lax.axis_size("leaf")
    panels = lax.axis_size("panel")
    half = leaves // 2
    leaf_id = lax.axis_index("leaf")
    front = winv_top.shape[0]
    top_cols = winv_top.shape[1]
    mid_cols = winv_mid.shape[1]
    contribution = lax.dot_general(
        border[0], solution[0], (((0,), (0,)), ((), ())), preferred_element_type=F32
    )
    groups = [list(range(half)), list(range(half, leaves))]
    device = leaf_id * panels + lax.axis_index("panel")
    in_half = device % (half * panels)
    top_load = lax.psum(contribution[:front], AXES)
    top_block = lax.dynamic_slice_in_dim(top_load, device * top_cols, top_cols, 0)
    mid_load = lax.psum(contribution[front:], "panel")
    mid_load = lax.psum(mid_load, "leaf", axis_index_groups=groups)
    mid_block = lax.dynamic_slice_in_dim(mid_load, in_half * mid_cols, mid_cols, 0)
    top_factor = winv_top.astype(F32)
    mid_factor = winv_mid.astype(F32)
    exact = lax.Precision.HIGHEST
    top_inner = lax.psum(jnp.dot(top_factor, top_block, precision=exact), AXES)
    top_adjoint = jnp.dot(top_factor.T, top_inner, precision=exact)
    top_whole = lax.all_gather(top_adjoint, AXES, axis=0, tiled=True)
    mid_rhs = mid_block - jnp.dot(coupling.astype(F32), top_whole, precision=exact)
    mid_inner = lax.psum(jnp.dot(mid_factor, mid_rhs, precision=exact), "panel")
    mid_inner = lax.psum(mid_inner, "leaf", axis_index_groups=groups)
    mid_adjoint = jnp.dot(mid_factor.T, mid_inner, precision=exact)
    return top_adjoint, mid_adjoint


CHAINS = 2
WIDE = 64


def permute(value, partner):
    return lax.ppermute(value, AXES, [(i, partner(i)) for i in range(32)])


def swap_core(value):
    return permute(value, lambda i: i ^ 1)


def swap_first(value):
    return permute(value, lambda i: i ^ (4 if i & 1 else 2))


def swap_second(value):
    return permute(value, lambda i: i ^ (2 if i & 1 else 4))


def swap_cross(value):
    return permute(value, lambda i: i ^ (3 if i & 1 else 5))


def swap_near(value):
    return permute(value, lambda i: i ^ 8)


def swap_far(value):
    return permute(value, lambda i: i ^ 16)


def coords():
    leaf = lax.axis_index("leaf")
    panel = lax.axis_index("panel")
    return leaf // 2, leaf % 2, panel // 2, panel % 2


def flip(a, k):
    return a + k - 2 * a * k


def z_flip(z, k):
    return flip(z // 2, k // 2) * 2 + flip(z % 2, k % 2)


Z_ORDER = (0, 2, 1, 3)


def plane_at(y, x, c, first, second):
    along_x = first * (1 - c) + second * c
    along_y = first * c + second * (1 - c)
    return flip(y, along_y) * 2 + flip(x, along_x)


def block_starts(deep):
    z, y, x, c = coords()
    starts = []
    for first in range(2):
        for second in range(2):
            plane = plane_at(y, x, c, first, second)
            for j in range(4):
                if deep:
                    start = (z_flip(z, Z_ORDER[j]) * 4 + plane) * 128
                else:
                    start = (flip(z % 2, j // 2) * 4 + plane) * 256 + j % 2 * 128
                starts.append(pl.multiple_of(start, 128))
    return starts


def kernel_call(kernel, outs, ins, scratch=(), flops=0, limit=24, after=()):
    vmem = pl.BlockSpec(memory_space=pltpu.VMEM)
    size = lambda s: s.size * s.dtype.itemsize

    def ordered(*refs):
        kernel(*refs[: len(ins)], *refs[len(ins) + len(after) :])

    return pl.pallas_call(
        ordered,
        out_shape=[jax.ShapeDtypeStruct(*o) for o in outs],
        in_specs=[vmem] * len(ins) + [pl.BlockSpec(memory_space=pl.ANY)] * len(after),
        out_specs=[vmem] * len(outs),
        scratch_shapes=list(scratch),
        compiler_params=pltpu.CompilerParams(vmem_limit_bytes=limit * 2**20),
        cost_estimate=pl.CostEstimate(
            flops=flops,
            transcendentals=0,
            bytes_accessed=sum(map(size, ins))
            + sum(size(jax.ShapeDtypeStruct(*o)) for o in outs),
        ),
    )(*ins, *after)


def left_lanes(shape):
    return lax.broadcasted_iota(jnp.int32, shape, 1) < WIDE


def pack(low, high):
    left = left_lanes(low.shape)
    return (
        jnp.where(left, low, pltpu.roll(high, WIDE, 1)),
        jnp.where(left, pltpu.roll(low, WIDE, 1), high),
    )


def put_split(rhs_ref, start, block):
    left = left_lanes(block.shape)
    turned = pltpu.roll(block, WIDE, 1)
    for i, rows in enumerate((jnp.where(left, block, turned), jnp.where(left, turned, block))):
        high = rows.astype(BF16).astype(F32)
        both = jnp.where(left, high, rows - high)
        rhs_ref[pl.ds(start + i * WIDE, WIDE), :] = both.astype(BF16)


def product(w_ref, rhs_ref):
    both = jnp.dot(w_ref[...], rhs_ref[...], preferred_element_type=F32)
    return both + pltpu.roll(both, WIDE, 1)


def take_block(total, start):
    low = total[start : start + WIDE]
    high = total[start + WIDE : start + 2 * WIDE]
    return jnp.where(left_lanes(low.shape), low, high)


def prep_top(border_ref, sol_ref, *tops):
    z, y, x, c = coords()
    sol = sol_ref[...].astype(F32)
    for rel in range(4):
        core = flip(c, rel % 2)
        for second in range(2):
            plane = plane_at(y, x, core, rel // 2, second)
            for j in range(4):
                col = pl.multiple_of((z_flip(z, Z_ORDER[j]) * 8 + plane * 2 + core) * 128, 128)
                here = (second * 4 + j) * 128
                tops[rel][:, here : here + 128] = border_ref[:, pl.ds(col, 128)].astype(F32)
        tops[rel][:, 1024:] = sol


def prep_mid(border_ref, *mids):
    z, y, x, c = coords()
    front = border_ref.shape[1] // 2
    for rel in range(4):
        core = flip(c, rel % 2)
        for second in range(2):
            plane = plane_at(y, x, core, rel // 2, second)
            for k in range(2):
                col = front + (flip(z % 2, k) * 8 + plane * 2 + core) * 256
                here = (second * 2 + k) * 256
                mids[rel][:, here : here + 256] = border_ref[
                    :, pl.ds(pl.multiple_of(col, 256), 256)
                ].astype(F32)


def stack_rows(refs, cols, out_ref):
    n = refs[0].shape[0]
    for i, ref in enumerate(refs):
        out_ref[i * n : (i + 1) * n, :] = ref[:, cols].astype(BF16)


def put_loads(sol, rows, outs):
    total = lax.dot_general(
        sol, rows, (((0,), (0,)), ((), ())), preferred_element_type=F32
    )
    for second in range(2):
        for j in range(4):
            here = (second * 4 + j) * 128
            block = total[:, here : here + 128].T
            packed = pack(block[:WIDE], block[WIDE:])
            for h in range(CHAINS):
                outs[h][second][j] = packed[h]


def top_load_kernel(*refs):
    ins, outs, sol_ref, rows_ref = refs[:4], refs[4:8], refs[8], refs[9]
    stack_rows(ins, slice(0, 1024), rows_ref)
    stack_rows(ins, slice(1024, 1152), sol_ref)
    put_loads(sol_ref[...], rows_ref[...], [outs[:2], outs[2:]])


def mid_load_kernel(*refs):
    ins, sol_ref, keep_ref, send_ref, rows_ref = refs[:4], *refs[4:]
    stack_rows(ins, slice(0, 1024), rows_ref)
    outs = [[keep_ref.at[h], send_ref.at[h]] for h in range(CHAINS)]
    put_loads(sol_ref[...], rows_ref[...], outs)


def halve_rows(w_ref, keep_ref, send_ref):
    z, y, x, c = coords()
    rows = w_ref.shape[0] // 2
    keep_ref[...] = w_ref[pl.ds(pl.multiple_of(c * rows, rows), rows), :]
    send_ref[...] = w_ref[pl.ds(pl.multiple_of((1 - c) * rows, rows), rows), :].astype(F32)


def halve_cols(w_ref, keep_ref, send_ref):
    z, y, x, c = coords()
    for i in range(w_ref.shape[1] // 256):
        here = slice(i * 128, (i + 1) * 128)
        kept = pl.multiple_of(i * 256 + c * 128, 128)
        sent = pl.multiple_of(i * 256 + (1 - c) * 128, 128)
        keep_ref[:, here] = w_ref[:, pl.ds(kept, 128)]
        send_ref[:, here] = w_ref[:, pl.ds(sent, 128)].astype(F32)


def join_cols(keep_ref, recv_ref, w_ref, t_ref):
    n = keep_ref.shape[1]
    w_ref[:, :n] = keep_ref[...]
    w_ref[:, n:] = recv_ref[...].astype(BF16)
    t_ref[:n, :] = keep_ref[...].T
    t_ref[n:, :] = recv_ref[...].astype(BF16).T


def join_rows(keep_ref, recv_ref, w_ref):
    n = keep_ref.shape[0]
    w_ref[:n, :] = keep_ref[...]
    w_ref[n:, :] = recv_ref[...].astype(BF16)


def forward(deep, w_ref, *refs):
    vec, (send_ref, next_ref, keep_ref), (rhs_ref, sum_ref) = refs[:-5], refs[-5:-2], refs[-2:]
    blocks = vec[0].shape[0]
    if len(vec) == 2:
        own, other = vec[0][...], vec[1][...]
    else:
        mine, theirs, part, recv = [v[...] for v in vec]
        own = mine - part[:blocks] - recv[blocks:]
        other = theirs - part[blocks:] - recv[:blocks]
    for i in range(blocks):
        put_split(rhs_ref, i * 128, own[i])
        put_split(rhs_ref, (blocks + i) * 128, other[i])
    sum_ref[...] = product(w_ref, rhs_ref)
    left = left_lanes((WIDE, 2 * WIDE))
    for i, start in enumerate(block_starts(deep)):
        low = sum_ref[pl.ds(start, WIDE), :]
        high = sum_ref[pl.ds(start + WIDE, WIDE), :]
        block = jnp.where(left, low, high)
        if i < 4:
            keep_ref[i] = block
        elif i < 8:
            next_ref[i - 4] = block
        else:
            send_ref[i - 8] = block


def backward(deep, w_ref, near_ref, far_ref, out_ref, rhs_ref):
    for i, start in enumerate(block_starts(deep)):
        put_split(rhs_ref, start, near_ref[i] if i < 8 else far_ref[i - 8])
    total = product(w_ref, rhs_ref)
    for i in range(out_ref.shape[0]):
        out_ref[i] = take_block(total, i * 128)


def run_forward(w, vec, deep, after=()):
    m, k = w.shape
    return kernel_call(
        functools.partial(forward, deep),
        [((8, WIDE, 128), F32), ((4, WIDE, 128), F32), ((4, WIDE, 128), F32)],
        [w, *vec],
        [pltpu.VMEM((k, 128), BF16), pltpu.VMEM((m, 128), F32)],
        flops=2 * m * k * 128,
        after=after,
    )


def run_backward(w, near, far, deep, after=()):
    m, k = w.shape
    return kernel_call(
        functools.partial(backward, deep),
        [((m // 128, WIDE, 128), F32)],
        [w, near, far],
        [pltpu.VMEM((k, 128), BF16)],
        flops=2 * m * k * 128,
        after=after,
    )[0]


def depth_sum(value, deep):
    half = value.shape[-3] // 2
    keep, send = value[..., :half, :, :], value[..., half:, :, :]
    value = keep + swap_near(send)
    if deep:
        value = value[:1] + swap_far(value[1:])
    return value


def plane_sum(send, follow, keep, first):
    second = swap_second(follow + first[4:])
    return keep + first[:4] + second


def depth_total(value, deep):
    if not deep:
        return value + swap_near(jnp.concatenate([value[2:], value[:2]], 0))
    keep = value[:2] + swap_near(value[2:])
    got = swap_far(keep[::-1])
    keep = keep + got
    return jnp.concatenate([keep, swap_near(keep)], 0)


def plane_spread(line):
    near = jnp.concatenate([line, swap_second(line)], 0)
    return near, swap_first(near)


def whole_spread(own):
    pair = jnp.concatenate([own, swap_far(own)], 0)
    return plane_spread(jnp.concatenate([pair, swap_near(pair)], 0))


def unpack(pair):
    blocks = pair[0].shape[0]
    rows = [
        jnp.concatenate([p[:, :, i * WIDE : (i + 1) * WIDE] for p in pair], 2)
        for i in range(2)
    ]
    return jnp.stack(rows, 1).reshape(blocks * 128, 128)


def fast_body(border, solution, winv_top, winv_mid, coupling):
    front = winv_top.shape[0]
    half = front // 2
    tops = kernel_call(
        prep_top, [((32, 1152), F32)] * 4, [border[0], solution[0]]
    )
    tops = [tops[0], swap_core(tops[1]), swap_first(tops[2]), swap_cross(tops[3])]
    *loads, sol_all = kernel_call(
        top_load_kernel,
        [((4, WIDE, 128), F32)] * 4 + [((128, 128), BF16)],
        tops,
        [pltpu.VMEM((128, 1024), BF16)],
        flops=2 * 128 * 1024 * 128,
    )
    plane_loads = [swap_second(loads[2 * h + 1]) for h in range(CHAINS)]
    load = [depth_sum(loads[2 * h] + plane_loads[h], True) for h in range(CHAINS)]

    top_keep, top_send = kernel_call(
        halve_rows, [((half, 128), BF16), ((half, 128), F32)], [winv_top]
    )
    cou_keep, cou_send = kernel_call(
        halve_cols, [((256, half), BF16), ((256, half), F32)], [coupling]
    )
    mid_keep, mid_send = kernel_call(
        halve_rows, [((half, 256), BF16), ((half, 256), F32)], [winv_mid]
    )
    top_w, top_t = kernel_call(
        join_cols,
        [((half, 256), BF16), ((256, half), BF16)],
        [top_keep, swap_core(top_send)],
    )
    (cou_w,) = kernel_call(
        join_rows, [((512, half), BF16)], [cou_keep, swap_core(cou_send)]
    )
    mid_w, mid_t = kernel_call(
        join_cols,
        [((half, 512), BF16), ((512, half), BF16)],
        [mid_keep, swap_core(mid_send)],
    )

    mids = kernel_call(
        prep_mid, [((32, 1024), F32)] * 4, [border[0]], after=[plane_loads[0]]
    )
    mids = [mids[0], swap_core(mids[1]), swap_first(mids[2]), swap_cross(mids[3])]
    keep, send = kernel_call(
        mid_load_kernel,
        [((CHAINS, 4, WIDE, 128), F32)] * 2,
        [*mids, sol_all],
        [pltpu.VMEM((128, 1024), BF16)],
        flops=2 * 128 * 1024 * 128,
    )
    mid_load = depth_sum(keep + swap_second(send), False)
    mid_other = swap_core(mid_load)

    top_out, mid_out = [], []
    turn = []
    joined = [cou_w, mid_w]
    for h in range(CHAINS):
        send, follow, keep = run_forward(
            top_w, [load[h], swap_core(load[h])], True, after=turn
        )
        first = swap_first(send)
        turn = [first]
        line = depth_total(plane_sum(send, follow, keep, first), True)
        both = run_backward(top_t, *plane_spread(line), True, after=joined)
        adjoint = both[:1] + swap_core(both[1:])
        top_out.append(adjoint)
        both = run_backward(cou_w, *whole_spread(adjoint), True)
        vec = [mid_load[h], mid_other[h], both, swap_core(both)]
        send, follow, keep = run_forward(mid_w, vec, False)
        line = depth_total(plane_sum(send, follow, keep, swap_first(send)), False)
        both = run_backward(mid_t, *plane_spread(line), False)
        mid_out.append(both[:2] + swap_core(both[2:]))
    return unpack(top_out), unpack(mid_out)


def solution(mesh):
    placed = (
        P("leaf", "panel", None),
        P("leaf", "panel", None),
        P(None, AXES),
        P(None, AXES),
        P(AXES, None),
    )
    fits = mesh.shape["leaf"] == 8 and mesh.shape["panel"] == 4
    return jax.shard_map(
        fast_body if fits else plain_body,
        mesh=mesh,
        in_specs=placed,
        out_specs=(P(AXES, None), P(AXES, None)),
        check_vma=False,
    )
```

```python
import functools

import jax
import jax.numpy as jnp
from jax import lax
from jax.experimental import pallas as pl
from jax.experimental.pallas import tpu as pltpu
from jax.sharding import PartitionSpec as P

AXES = ("leaf", "panel")
F32 = jnp.float32
BF16 = jnp.bfloat16
LANES = 128


def plain_body(border, solution, winv_top, winv_mid, coupling):
    leaves = lax.axis_size("leaf")
    panels = lax.axis_size("panel")
    half = leaves // 2
    leaf_id = lax.axis_index("leaf")
    front = winv_top.shape[0]
    top_cols = winv_top.shape[1]
    mid_cols = winv_mid.shape[1]
    contribution = lax.dot_general(
        border[0], solution[0], (((0,), (0,)), ((), ())), preferred_element_type=F32
    )
    groups = [list(range(half)), list(range(half, leaves))]
    device = leaf_id * panels + lax.axis_index("panel")
    in_half = device % (half * panels)
    top_load = lax.psum(contribution[:front], AXES)
    top_block = lax.dynamic_slice_in_dim(top_load, device * top_cols, top_cols, 0)
    mid_load = lax.psum(contribution[front:], "panel")
    mid_load = lax.psum(mid_load, "leaf", axis_index_groups=groups)
    mid_block = lax.dynamic_slice_in_dim(mid_load, in_half * mid_cols, mid_cols, 0)
    top_factor = winv_top.astype(F32)
    mid_factor = winv_mid.astype(F32)
    exact = lax.Precision.HIGHEST
    top_inner = lax.psum(jnp.dot(top_factor, top_block, precision=exact), AXES)
    top_adjoint = jnp.dot(top_factor.T, top_inner, precision=exact)
    top_whole = lax.all_gather(top_adjoint, AXES, axis=0, tiled=True)
    mid_rhs = mid_block - jnp.dot(coupling.astype(F32), top_whole, precision=exact)
    mid_inner = lax.psum(jnp.dot(mid_factor, mid_rhs, precision=exact), "panel")
    mid_inner = lax.psum(mid_inner, "leaf", axis_index_groups=groups)
    mid_adjoint = jnp.dot(mid_factor.T, mid_inner, precision=exact)
    return top_adjoint, mid_adjoint


CHAINS = 2
WIDE = 64


def permute(value, partner):
    return lax.ppermute(value, AXES, [(i, partner(i)) for i in range(32)])


def swap_core(value):
    return permute(value, lambda i: i ^ 1)


def swap_first(value, chain=0):
    return permute(value, lambda i: i ^ (4 if (i ^ chain) & 1 else 2))


def swap_second(value, chain=0):
    return permute(value, lambda i: i ^ (2 if (i ^ chain) & 1 else 4))


def swap_cross(value):
    return permute(value, lambda i: i ^ (3 if i & 1 else 5))


def swap_near(value):
    return permute(value, lambda i: i ^ 8)


def swap_far(value):
    return permute(value, lambda i: i ^ 16)


def coords():
    leaf = lax.axis_index("leaf")
    panel = lax.axis_index("panel")
    return leaf // 2, leaf % 2, panel // 2, panel % 2


def flip(a, k):
    return a + k - 2 * a * k


def z_flip(z, k):
    return flip(z // 2, k // 2) * 2 + flip(z % 2, k % 2)


Z_ORDER = (0, 2, 1, 3)


def plane_at(y, x, c, first, second):
    along_x = first * (1 - c) + second * c
    along_y = first * c + second * (1 - c)
    return flip(y, along_y) * 2 + flip(x, along_x)


def block_starts(deep, chain):
    z, y, x, c = coords()
    c = flip(c, chain)
    starts = []
    for first in range(2):
        for second in range(2):
            plane = plane_at(y, x, c, first, second)
            for j in range(4):
                if deep:
                    start = (z_flip(z, Z_ORDER[j]) * 4 + plane) * 128
                else:
                    start = (flip(z % 2, j // 2) * 4 + plane) * 256 + j % 2 * 128
                starts.append(pl.multiple_of(start, 128))
    return starts


def kernel_call(kernel, outs, ins, scratch=(), flops=0, limit=24, after=()):
    vmem = pl.BlockSpec(memory_space=pltpu.VMEM)
    size = lambda s: s.size * s.dtype.itemsize

    def ordered(*refs):
        kernel(*refs[: len(ins)], *refs[len(ins) + len(after) :])

    return pl.pallas_call(
        ordered,
        out_shape=[jax.ShapeDtypeStruct(*o) for o in outs],
        in_specs=[vmem] * len(ins) + [pl.BlockSpec(memory_space=pl.ANY)] * len(after),
        out_specs=[vmem] * len(outs),
        scratch_shapes=list(scratch),
        compiler_params=pltpu.CompilerParams(vmem_limit_bytes=limit * 2**20),
        cost_estimate=pl.CostEstimate(
            flops=flops,
            transcendentals=0,
            bytes_accessed=sum(map(size, ins))
            + sum(size(jax.ShapeDtypeStruct(*o)) for o in outs),
        ),
    )(*ins, *after)


def left_lanes(shape):
    return lax.broadcasted_iota(jnp.int32, shape, 1) < WIDE


def pack(low, high):
    left = left_lanes(low.shape)
    return (
        jnp.where(left, low, pltpu.roll(high, WIDE, 1)),
        jnp.where(left, pltpu.roll(low, WIDE, 1), high),
    )


def put_split(rhs_ref, start, block):
    left = left_lanes(block.shape)
    turned = pltpu.roll(block, WIDE, 1)
    for i, rows in enumerate((jnp.where(left, block, turned), jnp.where(left, turned, block))):
        high = rows.astype(BF16).astype(F32)
        both = jnp.where(left, high, rows - high)
        rhs_ref[pl.ds(start + i * WIDE, WIDE), :] = both.astype(BF16)


def product(w_ref, rhs_ref):
    both = jnp.dot(w_ref[...], rhs_ref[...], preferred_element_type=F32)
    return both + pltpu.roll(both, WIDE, 1)


def take_block(total, start):
    low = total[start : start + WIDE]
    high = total[start + WIDE : start + 2 * WIDE]
    return jnp.where(left_lanes(low.shape), low, high)


def prep_top(border_ref, sol_ref, *tops):
    z, y, x, c = coords()
    sol = sol_ref[...].astype(F32)
    for rel in range(4):
        core = flip(c, rel % 2)
        for second in range(2):
            plane = plane_at(y, x, core, rel // 2, second)
            for j in range(4):
                col = pl.multiple_of((z_flip(z, Z_ORDER[j]) * 8 + plane * 2 + core) * 128, 128)
                here = (second * 4 + j) * 128
                tops[rel][:, here : here + 128] = border_ref[:, pl.ds(col, 128)].astype(F32)
        tops[rel][:, 1024:] = sol


def prep_mid(border_ref, *mids):
    z, y, x, c = coords()
    front = border_ref.shape[1] // 2
    for rel in range(4):
        core = flip(c, rel % 2)
        for second in range(2):
            plane = plane_at(y, x, core, rel // 2, second)
            for k in range(2):
                col = front + (flip(z % 2, k) * 8 + plane * 2 + core) * 256
                here = (second * 2 + k) * 256
                mids[rel][:, here : here + 256] = border_ref[
                    :, pl.ds(pl.multiple_of(col, 256), 256)
                ].astype(F32)


def stack_rows(refs, cols, out_ref):
    n = refs[0].shape[0]
    for i, ref in enumerate(refs):
        out_ref[i * n : (i + 1) * n, :] = ref[:, cols].astype(BF16)


def put_loads(sol, rows, outs):
    total = lax.dot_general(
        sol, rows, (((0,), (0,)), ((), ())), preferred_element_type=F32
    )
    for second in range(2):
        for j in range(4):
            here = (second * 4 + j) * 128
            block = total[:, here : here + 128].T
            packed = pack(block[:WIDE], block[WIDE:])
            for h in range(CHAINS):
                outs[h][second][j] = packed[h]


def top_load_kernel(*refs):
    ins, outs, sol_ref, rows_ref = refs[:4], refs[4:8], refs[8], refs[9]
    stack_rows(ins, slice(0, 1024), rows_ref)
    stack_rows(ins, slice(1024, 1152), sol_ref)
    put_loads(sol_ref[...], rows_ref[...], [outs[:2], outs[2:]])


def mid_load_kernel(*refs):
    ins, sol_ref, keep_ref, send_ref, rows_ref = refs[:4], *refs[4:]
    stack_rows(ins, slice(0, 1024), rows_ref)
    outs = [[keep_ref.at[h], send_ref.at[h]] for h in range(CHAINS)]
    put_loads(sol_ref[...], rows_ref[...], outs)


def halve_rows(w_ref, keep_ref, send_ref):
    z, y, x, c = coords()
    rows = w_ref.shape[0] // 2
    keep_ref[...] = w_ref[pl.ds(pl.multiple_of(c * rows, rows), rows), :]
    send_ref[...] = w_ref[pl.ds(pl.multiple_of((1 - c) * rows, rows), rows), :].astype(F32)


def halve_cols(w_ref, keep_ref, send_ref):
    z, y, x, c = coords()
    for i in range(w_ref.shape[1] // 256):
        here = slice(i * 128, (i + 1) * 128)
        kept = pl.multiple_of(i * 256 + c * 128, 128)
        sent = pl.multiple_of(i * 256 + (1 - c) * 128, 128)
        keep_ref[:, here] = w_ref[:, pl.ds(kept, 128)]
        send_ref[:, here] = w_ref[:, pl.ds(sent, 128)].astype(F32)


def join_cols(keep_ref, recv_ref, w_ref, t_ref):
    n = keep_ref.shape[1]
    w_ref[:, :n] = keep_ref[...]
    w_ref[:, n:] = recv_ref[...].astype(BF16)
    t_ref[:n, :] = keep_ref[...].T
    t_ref[n:, :] = recv_ref[...].astype(BF16).T


def join_rows(keep_ref, recv_ref, w_ref):
    n = keep_ref.shape[0]
    w_ref[:n, :] = keep_ref[...]
    w_ref[n:, :] = recv_ref[...].astype(BF16)


def forward(deep, chain, w_ref, *refs):
    vec, (send_ref, next_ref, keep_ref), (rhs_ref, sum_ref) = refs[:-5], refs[-5:-2], refs[-2:]
    blocks = vec[0].shape[0]
    if len(vec) == 2:
        own, other = vec[0][...], vec[1][...]
    else:
        mine, theirs, part, recv = [v[...] for v in vec]
        own = mine - part[:blocks] - recv[blocks:]
        other = theirs - part[blocks:] - recv[:blocks]
    for i in range(blocks):
        put_split(rhs_ref, i * 128, own[i])
        put_split(rhs_ref, (blocks + i) * 128, other[i])
    sum_ref[...] = product(w_ref, rhs_ref)
    left = left_lanes((WIDE, 2 * WIDE))
    for i, start in enumerate(block_starts(deep, chain)):
        low = sum_ref[pl.ds(start, WIDE), :]
        high = sum_ref[pl.ds(start + WIDE, WIDE), :]
        block = jnp.where(left, low, high)
        if i < 4:
            keep_ref[i] = block
        elif i < 8:
            next_ref[i - 4] = block
        else:
            send_ref[i - 8] = block


def backward(deep, chain, w_ref, near_ref, far_ref, out_ref, rhs_ref):
    for i, start in enumerate(block_starts(deep, chain)):
        put_split(rhs_ref, start, near_ref[i] if i < 8 else far_ref[i - 8])
    total = product(w_ref, rhs_ref)
    for i in range(out_ref.shape[0]):
        out_ref[i] = take_block(total, i * 128)


def run_forward(w, vec, deep, chain, after=()):
    m, k = w.shape
    return kernel_call(
        functools.partial(forward, deep, chain),
        [((8, WIDE, 128), F32), ((4, WIDE, 128), F32), ((4, WIDE, 128), F32)],
        [w, *vec],
        [pltpu.VMEM((k, 128), BF16), pltpu.VMEM((m, 128), F32)],
        flops=2 * m * k * 128,
        after=after,
    )


def run_backward(w, near, far, deep, chain, after=()):
    m, k = w.shape
    return kernel_call(
        functools.partial(backward, deep, chain),
        [((m // 128, WIDE, 128), F32)],
        [w, near, far],
        [pltpu.VMEM((k, 128), BF16)],
        flops=2 * m * k * 128,
        after=after,
    )[0]


def depth_sum(value, deep):
    half = value.shape[-3] // 2
    keep, send = value[..., :half, :, :], value[..., half:, :, :]
    value = keep + swap_near(send)
    if deep:
        value = value[:1] + swap_far(value[1:])
    return value


def plane_sum(send, follow, keep, chain):
    first = swap_first(send, chain)
    second = swap_second(follow + first[4:], chain)
    return keep + first[:4] + second


def depth_total(value, deep):
    if not deep:
        return value + swap_near(jnp.concatenate([value[2:], value[:2]], 0))
    keep = value[:2] + swap_near(value[2:])
    got = swap_far(keep[::-1])
    keep = keep + got
    return jnp.concatenate([keep, swap_near(keep)], 0)


def plane_spread(line, chain):
    near = jnp.concatenate([line, swap_second(line, chain)], 0)
    return near, swap_first(near, chain)


def whole_spread(own, chain):
    pair = jnp.concatenate([own, swap_far(own)], 0)
    return plane_spread(jnp.concatenate([pair, swap_near(pair)], 0), chain)


def unpack(pair):
    blocks = pair[0].shape[0]
    rows = [
        jnp.concatenate([p[:, :, i * WIDE : (i + 1) * WIDE] for p in pair], 2)
        for i in range(2)
    ]
    return jnp.stack(rows, 1).reshape(blocks * 128, 128)


def fast_body(border, solution, winv_top, winv_mid, coupling):
    front = winv_top.shape[0]
    half = front // 2
    tops = ready = kernel_call(
        prep_top, [((32, 1152), F32)] * 4, [border[0], solution[0]]
    )
    tops = [tops[0], swap_core(tops[1]), swap_first(tops[2]), swap_cross(tops[3])]
    *loads, sol_all = kernel_call(
        top_load_kernel,
        [((4, WIDE, 128), F32)] * 4 + [((128, 128), BF16)],
        tops,
        [pltpu.VMEM((128, 1024), BF16)],
        flops=2 * 128 * 1024 * 128,
    )
    plane_loads = [swap_second(loads[2 * h + 1]) for h in range(CHAINS)]
    load = [depth_sum(loads[2 * h] + plane_loads[h], True) for h in range(CHAINS)]

    top_keep, top_send = kernel_call(
        halve_rows, [((half, 128), BF16), ((half, 128), F32)], [winv_top], after=ready[:1]
    )
    cou_keep, cou_send = kernel_call(
        halve_cols, [((256, half), BF16), ((256, half), F32)], [coupling]
    )
    mid_keep, mid_send = kernel_call(
        halve_rows, [((half, 256), BF16), ((half, 256), F32)], [winv_mid]
    )
    top_w, top_t = kernel_call(
        join_cols,
        [((half, 256), BF16), ((256, half), BF16)],
        [top_keep, swap_core(top_send)],
    )
    (cou_w,) = kernel_call(
        join_rows, [((512, half), BF16)], [cou_keep, swap_core(cou_send)]
    )
    mid_w, mid_t = kernel_call(
        join_cols,
        [((half, 512), BF16), ((512, half), BF16)],
        [mid_keep, swap_core(mid_send)],
    )

    mids = kernel_call(
        prep_mid, [((32, 1024), F32)] * 4, [border[0]], after=[plane_loads[0]]
    )
    mids = [mids[0], swap_core(mids[1]), swap_first(mids[2]), swap_cross(mids[3])]
    keep, send = kernel_call(
        mid_load_kernel,
        [((CHAINS, 4, WIDE, 128), F32)] * 2,
        [*mids, sol_all],
        [pltpu.VMEM((128, 1024), BF16)],
        flops=2 * 128 * 1024 * 128,
    )
    mid_load = depth_sum(keep + swap_second(send), False)
    mid_other = swap_core(mid_load)

    top_out, mid_out = [], []
    for h in range(CHAINS):
        parts = run_forward(top_w, [load[h], swap_core(load[h])], True, h, after=mids)
        line = depth_total(plane_sum(*parts, h), True)
        both = run_backward(top_t, *plane_spread(line, h), True, h, after=[cou_w, mid_w])
        adjoint = both[:1] + swap_core(both[1:])
        top_out.append(adjoint)
        both = run_backward(cou_w, *whole_spread(adjoint, h), True, h)
        vec = [mid_load[h], mid_other[h], both, swap_core(both)]
        parts = run_forward(mid_w, vec, False, h)
        line = depth_total(plane_sum(*parts, h), False)
        both = run_backward(mid_t, *plane_spread(line, h), False, h)
        mid_out.append(both[:2] + swap_core(both[2:]))
    return unpack(top_out), unpack(mid_out)


def solution(mesh):
    placed = (
        P("leaf", "panel", None),
        P("leaf", "panel", None),
        P(None, AXES),
        P(None, AXES),
        P(AXES, None),
    )
    fits = mesh.shape["leaf"] == 8 and mesh.shape["panel"] == 4
    return jax.shard_map(
        fast_body if fits else plain_body,
        mesh=mesh,
        in_specs=placed,
        out_specs=(P(AXES, None), P(AXES, None)),
        check_vma=False,
    )
```

```python
import functools

import jax
import jax.numpy as jnp
from jax import lax
from jax.experimental import pallas as pl
from jax.experimental.pallas import tpu as pltpu
from jax.sharding import PartitionSpec as P

AXES = ("leaf", "panel")
F32 = jnp.float32
BF16 = jnp.bfloat16
LANES = 128


def plain_body(border, solution, winv_top, winv_mid, coupling):
    leaves = lax.axis_size("leaf")
    panels = lax.axis_size("panel")
    half = leaves // 2
    leaf_id = lax.axis_index("leaf")
    front = winv_top.shape[0]
    top_cols = winv_top.shape[1]
    mid_cols = winv_mid.shape[1]
    contribution = lax.dot_general(
        border[0], solution[0], (((0,), (0,)), ((), ())), preferred_element_type=F32
    )
    groups = [list(range(half)), list(range(half, leaves))]
    device = leaf_id * panels + lax.axis_index("panel")
    in_half = device % (half * panels)
    top_load = lax.psum(contribution[:front], AXES)
    top_block = lax.dynamic_slice_in_dim(top_load, device * top_cols, top_cols, 0)
    mid_load = lax.psum(contribution[front:], "panel")
    mid_load = lax.psum(mid_load, "leaf", axis_index_groups=groups)
    mid_block = lax.dynamic_slice_in_dim(mid_load, in_half * mid_cols, mid_cols, 0)
    top_factor = winv_top.astype(F32)
    mid_factor = winv_mid.astype(F32)
    exact = lax.Precision.HIGHEST
    top_inner = lax.psum(jnp.dot(top_factor, top_block, precision=exact), AXES)
    top_adjoint = jnp.dot(top_factor.T, top_inner, precision=exact)
    top_whole = lax.all_gather(top_adjoint, AXES, axis=0, tiled=True)
    mid_rhs = mid_block - jnp.dot(coupling.astype(F32), top_whole, precision=exact)
    mid_inner = lax.psum(jnp.dot(mid_factor, mid_rhs, precision=exact), "panel")
    mid_inner = lax.psum(mid_inner, "leaf", axis_index_groups=groups)
    mid_adjoint = jnp.dot(mid_factor.T, mid_inner, precision=exact)
    return top_adjoint, mid_adjoint


CHAINS = 2
WIDE = 64


def permute(value, partner):
    return lax.ppermute(value, AXES, [(i, partner(i)) for i in range(32)])


def swap_core(value):
    return permute(value, lambda i: i ^ 1)


def swap_first(value, chain=0):
    return permute(value, lambda i: i ^ (4 if (i ^ chain) & 1 else 2))


def swap_second(value, chain=0):
    return permute(value, lambda i: i ^ (2 if (i ^ chain) & 1 else 4))


def swap_cross(value):
    return permute(value, lambda i: i ^ (3 if i & 1 else 5))


def swap_near(value):
    return permute(value, lambda i: i ^ 8)


def swap_far(value):
    return permute(value, lambda i: i ^ 16)


def coords():
    leaf = lax.axis_index("leaf")
    panel = lax.axis_index("panel")
    return leaf // 2, leaf % 2, panel // 2, panel % 2


def flip(a, k):
    return a + k - 2 * a * k


def z_flip(z, k):
    return flip(z // 2, k // 2) * 2 + flip(z % 2, k % 2)


Z_ORDER = (0, 2, 1, 3)


def plane_at(y, x, c, first, second):
    along_x = first * (1 - c) + second * c
    along_y = first * c + second * (1 - c)
    return flip(y, along_y) * 2 + flip(x, along_x)


def block_starts(deep, chain):
    z, y, x, c = coords()
    c = flip(c, chain)
    starts = []
    for first in range(2):
        for second in range(2):
            plane = plane_at(y, x, c, first, second)
            for j in range(4):
                if deep:
                    start = (z_flip(z, Z_ORDER[j]) * 4 + plane) * 128
                else:
                    start = (flip(z % 2, j // 2) * 4 + plane) * 256 + j % 2 * 128
                starts.append(pl.multiple_of(start, 128))
    return starts


def kernel_call(kernel, outs, ins, scratch=(), flops=0, limit=10, after=()):
    vmem = pl.BlockSpec(memory_space=pltpu.VMEM)
    size = lambda s: s.size * s.dtype.itemsize

    def ordered(*refs):
        kernel(*refs[: len(ins)], *refs[len(ins) + len(after) :])

    return pl.pallas_call(
        ordered,
        out_shape=[jax.ShapeDtypeStruct(*o) for o in outs],
        in_specs=[vmem] * len(ins) + [pl.BlockSpec(memory_space=pl.ANY)] * len(after),
        out_specs=[vmem] * len(outs),
        scratch_shapes=list(scratch),
        compiler_params=pltpu.CompilerParams(vmem_limit_bytes=limit * 2**20),
        cost_estimate=pl.CostEstimate(
            flops=flops,
            transcendentals=0,
            bytes_accessed=sum(map(size, ins))
            + sum(size(jax.ShapeDtypeStruct(*o)) for o in outs),
        ),
    )(*ins, *after)


def left_lanes(shape):
    return lax.broadcasted_iota(jnp.int32, shape, 1) < WIDE


def pack(low, high):
    left = left_lanes(low.shape)
    return (
        jnp.where(left, low, pltpu.roll(high, WIDE, 1)),
        jnp.where(left, pltpu.roll(low, WIDE, 1), high),
    )


def put_split(rhs_ref, start, block):
    left = left_lanes(block.shape)
    turned = pltpu.roll(block, WIDE, 1)
    for i, rows in enumerate((jnp.where(left, block, turned), jnp.where(left, turned, block))):
        high = rows.astype(BF16).astype(F32)
        both = jnp.where(left, high, rows - high)
        rhs_ref[pl.ds(start + i * WIDE, WIDE), :] = both.astype(BF16)


def product(w_ref, rhs_ref):
    both = jnp.dot(w_ref[...], rhs_ref[...], preferred_element_type=F32)
    return both + pltpu.roll(both, WIDE, 1)


def take_block(total, start):
    low = total[start : start + WIDE]
    high = total[start + WIDE : start + 2 * WIDE]
    return jnp.where(left_lanes(low.shape), low, high)


def prep_top(border_ref, sol_ref, *tops):
    z, y, x, c = coords()
    sol = sol_ref[...].astype(F32)
    for rel in range(4):
        core = flip(c, rel % 2)
        for second in range(2):
            plane = plane_at(y, x, core, rel // 2, second)
            for j in range(4):
                col = pl.multiple_of((z_flip(z, Z_ORDER[j]) * 8 + plane * 2 + core) * 128, 128)
                here = (second * 4 + j) * 128
                tops[rel][:, here : here + 128] = border_ref[:, pl.ds(col, 128)].astype(F32)
        tops[rel][:, 1024:] = sol


def prep_mid(border_ref, *mids):
    z, y, x, c = coords()
    front = border_ref.shape[1] // 2
    for rel in range(4):
        core = flip(c, rel % 2)
        for second in range(2):
            plane = plane_at(y, x, core, rel // 2, second)
            for k in range(2):
                col = front + (flip(z % 2, k) * 8 + plane * 2 + core) * 256
                here = (second * 2 + k) * 256
                mids[rel][:, here : here + 256] = border_ref[
                    :, pl.ds(pl.multiple_of(col, 256), 256)
                ].astype(F32)


def stack_rows(refs, cols, out_ref):
    n = refs[0].shape[0]
    for i, ref in enumerate(refs):
        out_ref[i * n : (i + 1) * n, :] = ref[:, cols].astype(BF16)


def put_loads(sol, rows, outs):
    total = lax.dot_general(
        sol, rows, (((0,), (0,)), ((), ())), preferred_element_type=F32
    )
    for second in range(2):
        for j in range(4):
            here = (second * 4 + j) * 128
            block = total[:, here : here + 128].T
            packed = pack(block[:WIDE], block[WIDE:])
            for h in range(CHAINS):
                outs[h][second][j] = packed[h]


def top_load_kernel(*refs):
    ins, outs, sol_ref, rows_ref = refs[:4], refs[4:8], refs[8], refs[9]
    stack_rows(ins, slice(0, 1024), rows_ref)
    stack_rows(ins, slice(1024, 1152), sol_ref)
    put_loads(sol_ref[...], rows_ref[...], [outs[:2], outs[2:]])


def mid_load_kernel(*refs):
    ins, sol_ref, keep_ref, send_ref, rows_ref = refs[:4], *refs[4:]
    stack_rows(ins, slice(0, 1024), rows_ref)
    outs = [[keep_ref.at[h], send_ref.at[h]] for h in range(CHAINS)]
    put_loads(sol_ref[...], rows_ref[...], outs)


def halve_rows(w_ref, keep_ref, send_ref):
    z, y, x, c = coords()
    rows = w_ref.shape[0] // 2
    keep_ref[...] = w_ref[pl.ds(pl.multiple_of(c * rows, rows), rows), :]
    send_ref[...] = w_ref[pl.ds(pl.multiple_of((1 - c) * rows, rows), rows), :].astype(F32)


def halve_cols(w_ref, keep_ref, send_ref):
    z, y, x, c = coords()
    for i in range(w_ref.shape[1] // 256):
        here = slice(i * 128, (i + 1) * 128)
        kept = pl.multiple_of(i * 256 + c * 128, 128)
        sent = pl.multiple_of(i * 256 + (1 - c) * 128, 128)
        keep_ref[:, here] = w_ref[:, pl.ds(kept, 128)]
        send_ref[:, here] = w_ref[:, pl.ds(sent, 128)].astype(F32)


def join_cols(keep_ref, recv_ref, w_ref, t_ref):
    n = keep_ref.shape[1]
    w_ref[:, :n] = keep_ref[...]
    w_ref[:, n:] = recv_ref[...].astype(BF16)
    t_ref[:n, :] = keep_ref[...].T
    t_ref[n:, :] = recv_ref[...].astype(BF16).T


def join_rows(keep_ref, recv_ref, w_ref):
    n = keep_ref.shape[0]
    w_ref[:n, :] = keep_ref[...]
    w_ref[n:, :] = recv_ref[...].astype(BF16)


def forward(deep, chain, w_ref, *refs):
    vec, (send_ref, next_ref, keep_ref), (rhs_ref, sum_ref) = refs[:-5], refs[-5:-2], refs[-2:]
    blocks = vec[0].shape[0]
    if len(vec) == 2:
        own, other = vec[0][...], vec[1][...]
    else:
        mine, theirs, part, recv = [v[...] for v in vec]
        own = mine - part[:blocks] - recv[blocks:]
        other = theirs - part[blocks:] - recv[:blocks]
    for i in range(blocks):
        put_split(rhs_ref, i * 128, own[i])
        put_split(rhs_ref, (blocks + i) * 128, other[i])
    sum_ref[...] = product(w_ref, rhs_ref)
    left = left_lanes((WIDE, 2 * WIDE))
    for i, start in enumerate(block_starts(deep, chain)):
        low = sum_ref[pl.ds(start, WIDE), :]
        high = sum_ref[pl.ds(start + WIDE, WIDE), :]
        block = jnp.where(left, low, high)
        if i < 4:
            keep_ref[i] = block
        elif i < 8:
            next_ref[i - 4] = block
        else:
            send_ref[i - 8] = block


def backward(deep, chain, w_ref, near_ref, far_ref, out_ref, rhs_ref):
    for i, start in enumerate(block_starts(deep, chain)):
        put_split(rhs_ref, start, near_ref[i] if i < 8 else far_ref[i - 8])
    total = product(w_ref, rhs_ref)
    for i in range(out_ref.shape[0]):
        out_ref[i] = take_block(total, i * 128)


def run_forward(w, vec, deep, chain, after=()):
    m, k = w.shape
    return kernel_call(
        functools.partial(forward, deep, chain),
        [((8, WIDE, 128), F32), ((4, WIDE, 128), F32), ((4, WIDE, 128), F32)],
        [w, *vec],
        [pltpu.VMEM((k, 128), BF16), pltpu.VMEM((m, 128), F32)],
        flops=2 * m * k * 128,
        after=after,
    )


def run_backward(w, near, far, deep, chain, after=()):
    m, k = w.shape
    return kernel_call(
        functools.partial(backward, deep, chain),
        [((m // 128, WIDE, 128), F32)],
        [w, near, far],
        [pltpu.VMEM((k, 128), BF16)],
        flops=2 * m * k * 128,
        after=after,
    )[0]


def depth_sum(value, deep):
    half = value.shape[-3] // 2
    keep, send = value[..., :half, :, :], value[..., half:, :, :]
    value = keep + swap_near(send)
    if deep:
        value = value[:1] + swap_far(value[1:])
    return value


def plane_sum(send, follow, keep, chain):
    first = swap_first(send, chain)
    second = swap_second(follow + first[4:], chain)
    return keep + first[:4] + second


def depth_total(value, deep):
    if not deep:
        return value + swap_near(jnp.concatenate([value[2:], value[:2]], 0))
    keep = value[:2] + swap_near(value[2:])
    got = swap_far(jnp.concatenate([keep[1:], keep[:1]], 0))
    keep = keep + got
    return jnp.concatenate([keep, swap_near(keep)], 0)


def plane_spread(line, chain):
    near = jnp.concatenate([line, swap_second(line, chain)], 0)
    return near, swap_first(near, chain)


def whole_spread(own, chain):
    pair = jnp.concatenate([own, swap_far(own)], 0)
    return plane_spread(jnp.concatenate([pair, swap_near(pair)], 0), chain)


def unpack(pair):
    blocks = pair[0].shape[0]
    rows = [
        jnp.concatenate([p[:, :, i * WIDE : (i + 1) * WIDE] for p in pair], 2)
        for i in range(2)
    ]
    return jnp.stack(rows, 1).reshape(blocks * 128, 128)


def fast_body(border, solution, winv_top, winv_mid, coupling):
    front = winv_top.shape[0]
    half = front // 2
    tops = ready = kernel_call(
        prep_top, [((32, 1152), F32)] * 4, [border[0], solution[0]]
    )
    tops = [tops[0], swap_core(tops[1]), swap_first(tops[2]), swap_cross(tops[3])]
    *loads, sol_all = kernel_call(
        top_load_kernel,
        [((4, WIDE, 128), F32)] * 4 + [((128, 128), BF16)],
        tops,
        [pltpu.VMEM((128, 1024), BF16)],
        flops=2 * 128 * 1024 * 128,
    )
    plane_loads = [swap_second(loads[2 * h + 1]) for h in range(CHAINS)]
    load = [depth_sum(loads[2 * h] + plane_loads[h], True) for h in range(CHAINS)]

    top_keep, top_send = kernel_call(
        halve_rows, [((half, 128), BF16), ((half, 128), F32)], [winv_top], after=ready[:1]
    )
    cou_keep, cou_send = kernel_call(
        halve_cols, [((256, half), BF16), ((256, half), F32)], [coupling]
    )
    mid_keep, mid_send = kernel_call(
        halve_rows, [((half, 256), BF16), ((half, 256), F32)], [winv_mid]
    )
    top_w, top_t = kernel_call(
        join_cols,
        [((half, 256), BF16), ((256, half), BF16)],
        [top_keep, swap_core(top_send)],
    )
    (cou_w,) = kernel_call(
        join_rows, [((512, half), BF16)], [cou_keep, swap_core(cou_send)]
    )
    mid_w, mid_t = kernel_call(
        join_cols,
        [((half, 512), BF16), ((512, half), BF16)],
        [mid_keep, swap_core(mid_send)],
    )

    mids = kernel_call(
        prep_mid, [((32, 1024), F32)] * 4, [border[0]], after=[plane_loads[0]]
    )
    mids = [mids[0], swap_core(mids[1]), swap_first(mids[2]), swap_cross(mids[3])]
    keep, send = kernel_call(
        mid_load_kernel,
        [((CHAINS, 4, WIDE, 128), F32)] * 2,
        [*mids, sol_all],
        [pltpu.VMEM((128, 1024), BF16)],
        flops=2 * 128 * 1024 * 128,
    )
    mid_load = depth_sum(keep + swap_second(send), False)
    mid_other = swap_core(mid_load)

    top_out, mid_out = [], []
    for h in range(CHAINS):
        parts = run_forward(top_w, [load[h], swap_core(load[h])], True, h, after=mids)
        line = depth_total(plane_sum(*parts, h), True)
        both = run_backward(top_t, *plane_spread(line, h), True, h, after=[cou_w, mid_w])
        adjoint = both[:1] + swap_core(both[1:])
        top_out.append(adjoint)
        both = run_backward(cou_w, *whole_spread(adjoint, h), True, h)
        vec = [mid_load[h], mid_other[h], both, swap_core(both)]
        parts = run_forward(mid_w, vec, False, h)
        line = depth_total(plane_sum(*parts, h), False)
        both = run_backward(mid_t, *plane_spread(line, h), False, h)
        mid_out.append(both[:2] + swap_core(both[2:]))
    return unpack(top_out), unpack(mid_out)


def solution(mesh):
    placed = (
        P("leaf", "panel", None),
        P("leaf", "panel", None),
        P(None, AXES),
        P(None, AXES),
        P(AXES, None),
    )
    fits = mesh.shape["leaf"] == 8 and mesh.shape["panel"] == 4
    return jax.shard_map(
        fast_body if fits else plain_body,
        mesh=mesh,
        in_specs=placed,
        out_specs=(P(AXES, None), P(AXES, None)),
        check_vma=False,
    )
```

```python
import functools

import jax
import jax.numpy as jnp
from jax import lax
from jax.experimental import pallas as pl
from jax.experimental.pallas import tpu as pltpu
from jax.sharding import PartitionSpec as P

AXES = ("leaf", "panel")
F32 = jnp.float32
BF16 = jnp.bfloat16
LANES = 128


def plain_body(border, solution, winv_top, winv_mid, coupling):
    leaves = lax.axis_size("leaf")
    panels = lax.axis_size("panel")
    half = leaves // 2
    leaf_id = lax.axis_index("leaf")
    front = winv_top.shape[0]
    top_cols = winv_top.shape[1]
    mid_cols = winv_mid.shape[1]
    contribution = lax.dot_general(
        border[0], solution[0], (((0,), (0,)), ((), ())), preferred_element_type=F32
    )
    groups = [list(range(half)), list(range(half, leaves))]
    device = leaf_id * panels + lax.axis_index("panel")
    in_half = device % (half * panels)
    top_load = lax.psum(contribution[:front], AXES)
    top_block = lax.dynamic_slice_in_dim(top_load, device * top_cols, top_cols, 0)
    mid_load = lax.psum(contribution[front:], "panel")
    mid_load = lax.psum(mid_load, "leaf", axis_index_groups=groups)
    mid_block = lax.dynamic_slice_in_dim(mid_load, in_half * mid_cols, mid_cols, 0)
    top_factor = winv_top.astype(F32)
    mid_factor = winv_mid.astype(F32)
    exact = lax.Precision.HIGHEST
    top_inner = lax.psum(jnp.dot(top_factor, top_block, precision=exact), AXES)
    top_adjoint = jnp.dot(top_factor.T, top_inner, precision=exact)
    top_whole = lax.all_gather(top_adjoint, AXES, axis=0, tiled=True)
    mid_rhs = mid_block - jnp.dot(coupling.astype(F32), top_whole, precision=exact)
    mid_inner = lax.psum(jnp.dot(mid_factor, mid_rhs, precision=exact), "panel")
    mid_inner = lax.psum(mid_inner, "leaf", axis_index_groups=groups)
    mid_adjoint = jnp.dot(mid_factor.T, mid_inner, precision=exact)
    return top_adjoint, mid_adjoint


WIDE = 64
CORE, XBIT, YBIT, NEAR, FAR = 1, 2, 4, 8, 16


def permute(value, partner):
    return lax.ppermute(value, AXES, [(i, partner(i)) for i in range(32)])


def swap(value, mask):
    return permute(value, lambda i: i ^ mask)


def swap_first(value, colour):
    return swap(value, YBIT if colour else XBIT)


def swap_second(value, colour):
    return swap(value, XBIT if colour else YBIT)


def coords():
    leaf = lax.axis_index("leaf")
    panel = lax.axis_index("panel")
    return leaf // 2, leaf % 2, panel // 2, panel % 2


def flip(a, k):
    return a + k - 2 * a * k


def z_flip(z, k):
    return flip(z // 2, k // 2) * 2 + flip(z % 2, k % 2)


Z_ORDER = (0, 2, 1, 3)


def plane_at(y, x, colour, first, second):
    along_x = first * (1 - colour) + second * colour
    along_y = first * colour + second * (1 - colour)
    return flip(y, along_y) * 2 + flip(x, along_x)


def block_starts(deep, colour):
    z, y, x, c = coords()
    core = flip(c, colour)
    starts = []
    for first in range(2):
        for second in range(2):
            plane = plane_at(y, x, colour, first, second)
            for j in range(4):
                if deep:
                    start = ((z_flip(z, Z_ORDER[j]) * 4 + plane) * 2 + core) * 128
                else:
                    start = ((flip(z % 2, j // 2) * 4 + plane) * 2 + core) * 256 + j % 2 * 128
                starts.append(pl.multiple_of(start, 128))
    return starts


def size_of(array):
    return array.size * array.dtype.itemsize


def kernel_call(kernel, outs, ins, scratch=(), flops=0, limit=10, after=()):
    vmem = pl.BlockSpec(memory_space=pltpu.VMEM)
    shapes = [jax.ShapeDtypeStruct(*o) for o in outs]

    def ordered(*refs):
        kernel(*refs[: len(ins)], *refs[len(ins) + len(after) :])

    return pl.pallas_call(
        ordered,
        out_shape=shapes,
        in_specs=[vmem] * len(ins) + [pl.BlockSpec(memory_space=pl.ANY)] * len(after),
        out_specs=[vmem] * len(outs),
        scratch_shapes=list(scratch),
        compiler_params=pltpu.CompilerParams(vmem_limit_bytes=limit * 2**20),
        cost_estimate=pl.CostEstimate(
            flops=flops,
            transcendentals=0,
            bytes_accessed=sum(map(size_of, [*ins, *shapes])),
        ),
    )(*ins, *after)


def glue(fn, *ins, after=()):
    shapes = jax.eval_shape(fn, *ins)

    def kernel(*refs):
        values = fn(*[r[...] for r in refs[: len(ins)]])
        for ref, value in zip(refs[len(ins) :], values):
            ref[...] = value

    return kernel_call(kernel, [(o.shape, o.dtype) for o in shapes], ins, after=after)


def left_lanes(shape):
    return lax.broadcasted_iota(jnp.int32, shape, 1) < WIDE


def pack(low, high):
    left = left_lanes(low.shape)
    return (
        jnp.where(left, low, pltpu.roll(high, WIDE, 1)),
        jnp.where(left, pltpu.roll(low, WIDE, 1), high),
    )


def put_split(rhs_ref, start, block):
    left = left_lanes(block.shape)
    turned = pltpu.roll(block, WIDE, 1)
    for i, rows in enumerate((jnp.where(left, block, turned), jnp.where(left, turned, block))):
        high = rows.astype(BF16).astype(F32)
        both = jnp.where(left, high, rows - high)
        rhs_ref[pl.ds(start + i * WIDE, WIDE), :] = both.astype(BF16)


def product(w, rhs_ref):
    both = jnp.dot(w, rhs_ref[...], preferred_element_type=F32)
    return both + pltpu.roll(both, WIDE, 1)


def take_block(total, start):
    low = total[start : start + WIDE]
    high = total[start + WIDE : start + 2 * WIDE]
    return jnp.where(left_lanes(low.shape), low, high)


def prep_top(border_ref, sol_ref, *tops):
    z, y, x, c = coords()
    sol = sol_ref[...].astype(F32)
    for rel in range(4):
        core = flip(c, rel % 2)
        for second in range(2):
            plane = plane_at(y, x, core, rel // 2, second)
            for j in range(4):
                col = pl.multiple_of((z_flip(z, Z_ORDER[j]) * 8 + plane * 2 + core) * 128, 128)
                here = (second * 4 + j) * 128
                tops[rel][:, here : here + 128] = border_ref[:, pl.ds(col, 128)].astype(F32)
        tops[rel][:, 1024:] = sol


def prep_mid(border_ref, *mids):
    z, y, x, c = coords()
    front = border_ref.shape[1] // 2
    for rel in range(4):
        core = flip(c, rel % 2)
        for second in range(2):
            plane = plane_at(y, x, core, rel // 2, second)
            for k in range(2):
                col = front + (flip(z % 2, k) * 8 + plane * 2 + core) * 256
                here = (second * 2 + k) * 256
                mids[rel][:, here : here + 256] = border_ref[
                    :, pl.ds(pl.multiple_of(col, 256), 256)
                ].astype(F32)


def plane_inputs(parts):
    return [
        parts[0],
        swap(parts[1], CORE),
        permute(parts[2], lambda i: i ^ (YBIT if i & 1 else XBIT)),
        permute(parts[3], lambda i: i ^ (XBIT + CORE if i & 1 else YBIT + CORE)),
    ]


def swap_loads(value):
    return permute(value, lambda i: i ^ (XBIT if i & 1 else YBIT))


def stack_rows(refs, cols, out_ref):
    n = refs[0].shape[0]
    for i, ref in enumerate(refs):
        out_ref[i * n : (i + 1) * n, :] = ref[:, cols].astype(BF16)


def put_loads(sol, rows, outs):
    total = lax.dot_general(
        sol, rows, (((0,), (0,)), ((), ())), preferred_element_type=F32
    )
    for second in range(2):
        for j in range(4):
            here = (second * 4 + j) * 128
            block = total[:, here : here + 128].T
            for h, packed in enumerate(pack(block[:WIDE], block[WIDE:])):
                outs[second][j, h] = packed


def top_load_kernel(*refs):
    ins, (keep_ref, send_ref, sol_ref, rows_ref) = refs[:4], refs[4:]
    stack_rows(ins, slice(0, 1024), rows_ref)
    stack_rows(ins, slice(1024, 1152), sol_ref)
    put_loads(sol_ref[...], rows_ref[...], [keep_ref, send_ref])


def mid_load_kernel(*refs):
    ins, (sol_ref, keep_ref, send_ref, rows_ref) = refs[:4], refs[4:]
    stack_rows(ins, slice(0, 1024), rows_ref)
    put_loads(sol_ref[...], rows_ref[...], [keep_ref, send_ref])


def widen_kernel(w_ref, out_ref):
    out_ref[...] = w_ref[...].astype(F32)


def widen(w, after=()):
    return kernel_call(widen_kernel, [(w.shape, F32)], [w], after=after)[0]


def widen_half(w, half):
    rows = w.shape[0] // 2

    def kernel(w_ref, out_ref):
        out_ref[...] = w_ref[half * rows : (half + 1) * rows, :].astype(F32)

    return kernel_call(kernel, [((rows, w.shape[1]), F32)], [w])[0]


def join_halves(keep, recv):
    m, n = keep.shape

    def kernel(keep_ref, low_ref, high_ref, w_ref, t_ref):
        w_ref[:, :n] = keep_ref[...]
        t_ref[:n, :] = keep_ref[...].T
        for i, ref in enumerate((low_ref, high_ref)):
            here = slice(i * m // 2, (i + 1) * m // 2)
            part = ref[...].astype(BF16)
            w_ref[here, n:] = part
            t_ref[n:, here] = part.T

    return kernel_call(kernel, [((m, 2 * n), BF16), ((2 * n, m), BF16)], [keep, *recv])


def join_cols_kernel(keep_ref, recv_ref, w_ref, t_ref):
    n = keep_ref.shape[1]
    recv = recv_ref[...].astype(BF16)
    w_ref[:, :n] = keep_ref[...]
    w_ref[:, n:] = recv
    t_ref[:n, :] = keep_ref[...].T
    t_ref[n:, :] = recv.T


def join_cols(keep, recv, parts=4):
    m, n = keep.shape
    step = m // parts
    shapes = [jax.ShapeDtypeStruct((m, 2 * n), BF16), jax.ShapeDtypeStruct((2 * n, m), BF16)]
    return pl.pallas_call(
        join_cols_kernel,
        grid=(parts,),
        out_shape=shapes,
        in_specs=[pl.BlockSpec((step, n), lambda i: (i, 0))] * 2,
        out_specs=[
            pl.BlockSpec((step, 2 * n), lambda i: (i, 0)),
            pl.BlockSpec((2 * n, step), lambda i: (0, i)),
        ],
        compiler_params=pltpu.CompilerParams(vmem_limit_bytes=12 * 2**20),
        cost_estimate=pl.CostEstimate(
            flops=0,
            transcendentals=0,
            bytes_accessed=sum(map(size_of, [keep, recv, *shapes])),
        ),
    )(keep, recv)


def join_rows_kernel(keep_ref, recv_ref, w_ref):
    n = keep_ref.shape[0]
    w_ref[:n, :] = keep_ref[...]
    w_ref[n:, :] = recv_ref[...].astype(BF16)


def join_rows(keep, recv, parts=4):
    m, n = keep.shape
    step = n // parts
    shape = jax.ShapeDtypeStruct((2 * m, n), BF16)
    return pl.pallas_call(
        join_rows_kernel,
        grid=(parts,),
        out_shape=shape,
        in_specs=[pl.BlockSpec((m, step), lambda i: (0, i))] * 2,
        out_specs=pl.BlockSpec((2 * m, step), lambda i: (0, i)),
        compiler_params=pltpu.CompilerParams(vmem_limit_bytes=12 * 2**20),
        cost_estimate=pl.CostEstimate(
            flops=0,
            transcendentals=0,
            bytes_accessed=sum(map(size_of, [keep, recv, shape])),
        ),
    )(keep, recv)


def forward(deep, w_ref, *refs):
    vec, outs, (rhs_ref, sum_ref) = refs[:-8], refs[-8:-2], refs[-2:]
    own, other = vec[0][...], vec[1][...]
    blocks = own.shape[0]
    if len(vec) == 3:
        own = own - vec[2][:blocks]
        other = other - vec[2][blocks:]
    for i in range(blocks):
        put_split(rhs_ref, i * 128, own[i])
        put_split(rhs_ref, (blocks + i) * 128, other[i])
    step = w_ref.shape[0] // 4
    for i in range(4):
        here = slice(i * step, (i + 1) * step)
        sum_ref[here, :] = product(w_ref[here, :], rhs_ref)
    left = left_lanes((WIDE, 2 * WIDE))
    for colour in range(2):
        send_ref, next_ref, keep_ref = outs[3 * colour : 3 * colour + 3]
        for i, start in enumerate(block_starts(deep, colour)):
            low = sum_ref[pl.ds(start, WIDE), :]
            high = sum_ref[pl.ds(start + WIDE, WIDE), :]
            block = jnp.where(left, low, high)
            if i < 4:
                keep_ref[i] = block
            elif i < 8:
                next_ref[i - 4] = block
            else:
                send_ref[i - 8] = block


def backward(deep, w_ref, near0, far0, near1, far1, *refs):
    outs, rhs_ref = refs[:-1], refs[-1]
    for colour, (near, far) in enumerate(((near0, far0), (near1, far1))):
        for i, start in enumerate(block_starts(deep, colour)):
            put_split(rhs_ref, start, near[i] if i < 8 else far[i - 8])
    total = product(w_ref[...], rhs_ref)
    blocks = outs[0].shape[0]
    for i in range(blocks):
        outs[0][i] = take_block(total, i * 128)
        if len(outs) > 1 and i >= blocks // 2:
            outs[1][i - blocks // 2] = outs[0][i]


def run_forward(w, vec, deep, after=()):
    m, k = w.shape
    return kernel_call(
        functools.partial(forward, deep),
        [((8, WIDE, 128), F32), ((4, WIDE, 128), F32), ((4, WIDE, 128), F32)] * 2,
        [w, *vec],
        [pltpu.VMEM((k, 128), BF16), pltpu.VMEM((m, 128), F32)],
        flops=2 * m * k * 128,
        limit=16,
        after=after,
    )


def run_backward(w, pieces, deep, alone, after=()):
    m, k = w.shape
    blocks = m // 128
    outs = [((blocks, WIDE, 128), F32)]
    if alone:
        outs.append(((blocks // 2, WIDE, 128), F32))
    return kernel_call(
        functools.partial(backward, deep),
        outs,
        [w, *pieces],
        [pltpu.VMEM((k, 128), BF16)],
        flops=2 * m * k * 128,
        limit=16,
        after=after,
    )


def depth_load(value, deep):
    half = value.shape[0] // 2
    value = value[:half] + swap(value[half:], NEAR)
    if deep:
        value = value[:1] + swap(value[1:], FAR)
    return value


def by_core(own):
    c = lax.axis_index("panel") % 2
    mine = jnp.where(c == 0, own[:, 0], own[:, 1])
    theirs = jnp.where(c == 0, own[:, 1], own[:, 0])
    return [mine, swap(theirs, CORE)]


def plane_sum(parts):
    out = []
    firsts = [swap_first(parts[3 * k], k) for k in range(2)]
    for k in range(2):
        (follow,) = glue(lambda a, b: (a + b[4:],), parts[3 * k + 1], firsts[k])
        out += [parts[3 * k + 2], firsts[k], swap_second(follow, k)]
    return out


def colours(k0, f0, s0, k1, f1, s1):
    return jnp.stack([k0 + f0[:4] + s0, k1 + f1[:4] + s1], 1)


def depth_total(pieces, deep):
    if not deep:

        def both(*p):
            v = colours(*p)
            return v, jnp.concatenate([v[2:], v[:2]], 0)

        value, turned = glue(both, *pieces)
        got = swap(turned, NEAR)
        return glue(lambda v, g: ((v + g)[:, 0], (v + g)[:, 1]), value, got), [got]

    def halves(*p):
        v = colours(*p)
        return v[:2], v[2:]

    keep, send = glue(halves, *pieces)

    def turn(k, g):
        v = k + g
        return v, jnp.concatenate([v[1:], v[:1]], 0)

    near = swap(send, NEAR)
    keep, turned = glue(turn, keep, near)
    far = swap(turned, FAR)
    (pair,) = glue(lambda k, g: (k + g,), keep, far)
    return lines(pair), [near, far]


def lines(pair, after=()):
    def put(p, g):
        return tuple(jnp.concatenate([p[:, k], g[:, k]], 0) for k in range(2))

    return glue(put, pair, swap(pair, NEAR), after=after)


def plane_spread(pair_of_lines):
    pieces = []
    seconds = [swap_second(line, k) for k, line in enumerate(pair_of_lines)]
    for k, line in enumerate(pair_of_lines):
        (near,) = glue(lambda a, b: (jnp.concatenate([a, b], 0),), line, seconds[k])
        pieces += [near, swap_first(near, k)]
    return pieces


def unpack_kernel(mine_ref, recv_ref, out_ref):
    c = lax.axis_index("panel") % 2
    blocks = recv_ref.shape[0]
    left = left_lanes((WIDE, 128))
    for i in range(blocks):
        mine, recv = mine_ref[i], recv_ref[i]
        here = jnp.broadcast_to(c == 0, mine.shape)
        p0, p1 = jnp.where(here, mine, recv), jnp.where(here, recv, mine)
        out_ref[i * 128 : i * 128 + WIDE, :] = jnp.where(left, p0, pltpu.roll(p1, WIDE, 1))
        out_ref[i * 128 + WIDE : (i + 1) * 128, :] = jnp.where(left, pltpu.roll(p0, WIDE, 1), p1)


def unpack(mine, recv):
    return kernel_call(unpack_kernel, [((recv.shape[0] * 128, 128), F32)], [mine, recv])[0]


def fast_body(border, solution, winv_top, winv_mid, coupling):
    ready = kernel_call(
        prep_top, [((32, 1152), F32)] * 4, [border[0], solution[0]]
    )
    tops = plane_inputs(ready)
    top_w, top_t = join_halves(winv_top, [swap(widen_half(winv_top, i), CORE) for i in range(2)])
    keep, send, sol_all = kernel_call(
        top_load_kernel,
        [((4, 2, WIDE, 128), F32)] * 2 + [((128, 128), BF16)],
        tops,
        [pltpu.VMEM((128, 1024), BF16)],
        flops=2 * 128 * 1024 * 128,
    )
    got = swap_loads(send)
    load = by_core(depth_load(keep + got, True))

    mids = plane_inputs(
        kernel_call(prep_mid, [((32, 1024), F32)] * 4, [border[0]], after=[got])
    )

    parts = run_forward(top_w, load, True, after=mids)
    line, marks = depth_total(plane_sum(parts), True)
    cou_w = join_rows(coupling, swap(widen(coupling, after=marks[:1]), CORE))
    mid_w, mid_t = join_cols(winv_mid, swap(widen(winv_mid, after=marks[:1]), CORE))
    pieces = plane_spread(line)
    adjoint, theirs = run_backward(top_t, pieces, True, True)
    top_out = unpack(adjoint, swap(theirs, CORE))

    keep, send = kernel_call(
        mid_load_kernel,
        [((4, 2, WIDE, 128), F32)] * 2,
        [*mids, sol_all],
        [pltpu.VMEM((128, 1024), BF16)],
        flops=2 * 128 * 1024 * 128,
    )
    load = by_core(depth_load(keep + swap_loads(send), False))

    (pair,) = glue(lambda a, b: (jnp.stack([a, b]),), adjoint, swap(adjoint, FAR))
    pieces = plane_spread(lines(pair))
    (part,) = run_backward(cou_w, pieces, True, False)
    parts = run_forward(mid_w, [*load, part], False)
    pieces = plane_spread(depth_total(plane_sum(parts), False)[0])
    adjoint, theirs = run_backward(mid_t, pieces, False, True)
    return top_out, unpack(adjoint, swap(theirs, CORE))


def solution(mesh):
    placed = (
        P("leaf", "panel", None),
        P("leaf", "panel", None),
        P(None, AXES),
        P(None, AXES),
        P(AXES, None),
    )
    fits = mesh.shape["leaf"] == 8 and mesh.shape["panel"] == 4
    return jax.shard_map(
        fast_body if fits else plain_body,
        mesh=mesh,
        in_specs=placed,
        out_specs=(P(AXES, None), P(AXES, None)),
        check_vma=False,
    )
```

```python
import functools

import jax
import jax.numpy as jnp
from jax import lax
from jax.experimental import pallas as pl
from jax.experimental.pallas import tpu as pltpu
from jax.sharding import PartitionSpec as P

AXES = ("leaf", "panel")
F32 = jnp.float32
BF16 = jnp.bfloat16
LANES = 128


def plain_body(border, solution, winv_top, winv_mid, coupling):
    leaves = lax.axis_size("leaf")
    panels = lax.axis_size("panel")
    half = leaves // 2
    leaf_id = lax.axis_index("leaf")
    front = winv_top.shape[0]
    top_cols = winv_top.shape[1]
    mid_cols = winv_mid.shape[1]
    contribution = lax.dot_general(
        border[0], solution[0], (((0,), (0,)), ((), ())), preferred_element_type=F32
    )
    groups = [list(range(half)), list(range(half, leaves))]
    device = leaf_id * panels + lax.axis_index("panel")
    in_half = device % (half * panels)
    top_load = lax.psum(contribution[:front], AXES)
    top_block = lax.dynamic_slice_in_dim(top_load, device * top_cols, top_cols, 0)
    mid_load = lax.psum(contribution[front:], "panel")
    mid_load = lax.psum(mid_load, "leaf", axis_index_groups=groups)
    mid_block = lax.dynamic_slice_in_dim(mid_load, in_half * mid_cols, mid_cols, 0)
    top_factor = winv_top.astype(F32)
    mid_factor = winv_mid.astype(F32)
    exact = lax.Precision.HIGHEST
    top_inner = lax.psum(jnp.dot(top_factor, top_block, precision=exact), AXES)
    top_adjoint = jnp.dot(top_factor.T, top_inner, precision=exact)
    top_whole = lax.all_gather(top_adjoint, AXES, axis=0, tiled=True)
    mid_rhs = mid_block - jnp.dot(coupling.astype(F32), top_whole, precision=exact)
    mid_inner = lax.psum(jnp.dot(mid_factor, mid_rhs, precision=exact), "panel")
    mid_inner = lax.psum(mid_inner, "leaf", axis_index_groups=groups)
    mid_adjoint = jnp.dot(mid_factor.T, mid_inner, precision=exact)
    return top_adjoint, mid_adjoint


WIDE = 64
CORE, XBIT, YBIT, ZBIT = 1, 2, 4, 8
FAR_FIRST = (2, 3, 1)


def permute(value, partner):
    return lax.ppermute(value, AXES, [(i, partner(i)) for i in range(32)])


def swap(value, mask):
    return permute(value, lambda i: i ^ mask)


def swap_first(value, colour):
    return swap(value, YBIT if colour else XBIT)


def swap_second(value, colour):
    return swap(value, XBIT if colour else YBIT)


def coords():
    leaf = lax.axis_index("leaf")
    panel = lax.axis_index("panel")
    return leaf // 2, leaf % 2, panel // 2, panel % 2


def flip(a, k):
    return a + k - 2 * a * k


def z_flip(z, k):
    return flip(z // 2, k // 2) * 2 + flip(z % 2, k % 2)


def plane_at(y, x, colour, first, second):
    along_x = first * (1 - colour) + second * colour
    along_y = first * colour + second * (1 - colour)
    return flip(y, along_y) * 2 + flip(x, along_x)


def block_starts(deep, colour):
    z, y, x, c = coords()
    core = flip(c, colour)
    starts = []
    for first in range(2):
        for second in range(2):
            plane = plane_at(y, x, colour, first, second)
            for j in range(4):
                if deep:
                    start = ((z_flip(z, j) * 4 + plane) * 2 + core) * 128
                else:
                    start = ((flip(z % 2, j // 2) * 4 + plane) * 2 + core) * 256 + j % 2 * 128
                starts.append(pl.multiple_of(start, 128))
    return starts


def size_of(array):
    return array.size * array.dtype.itemsize


def kernel_call(kernel, outs, ins, scratch=(), flops=0, limit=10, after=()):
    vmem = pl.BlockSpec(memory_space=pltpu.VMEM)
    shapes = [jax.ShapeDtypeStruct(*o) for o in outs]

    def ordered(*refs):
        kernel(*refs[: len(ins)], *refs[len(ins) + len(after) :])

    return pl.pallas_call(
        ordered,
        out_shape=shapes,
        in_specs=[vmem] * len(ins) + [pl.BlockSpec(memory_space=pl.ANY)] * len(after),
        out_specs=[vmem] * len(outs),
        scratch_shapes=list(scratch),
        compiler_params=pltpu.CompilerParams(vmem_limit_bytes=limit * 2**20),
        cost_estimate=pl.CostEstimate(
            flops=flops,
            transcendentals=0,
            bytes_accessed=sum(map(size_of, [*ins, *shapes])),
        ),
    )(*ins, *after)


def glue(fn, *ins, after=()):
    shapes = jax.eval_shape(fn, *ins)

    def kernel(*refs):
        values = fn(*[r[...] for r in refs[: len(ins)]])
        for ref, value in zip(refs[len(ins) :], values):
            ref[...] = value

    return kernel_call(kernel, [(o.shape, o.dtype) for o in shapes], ins, after=after)


def left_lanes(shape):
    return lax.broadcasted_iota(jnp.int32, shape, 1) < WIDE


def pack(low, high):
    left = left_lanes(low.shape)
    return (
        jnp.where(left, low, pltpu.roll(high, WIDE, 1)),
        jnp.where(left, pltpu.roll(low, WIDE, 1), high),
    )


def put_split(rhs_ref, start, block):
    left = left_lanes(block.shape)
    turned = pltpu.roll(block, WIDE, 1)
    for i, rows in enumerate((jnp.where(left, block, turned), jnp.where(left, turned, block))):
        high = rows.astype(BF16).astype(F32)
        both = jnp.where(left, high, rows - high)
        rhs_ref[pl.ds(start + i * WIDE, WIDE), :] = both.astype(BF16)


def product(w, rhs_ref):
    both = jnp.dot(w, rhs_ref[...], preferred_element_type=F32)
    return both + pltpu.roll(both, WIDE, 1)


def take_block(total, start):
    low = total[start : start + WIDE]
    high = total[start + WIDE : start + 2 * WIDE]
    return jnp.where(left_lanes(low.shape), low, high)


def prep_top(border_ref, sol_ref, *tops):
    z, y, x, c = coords()
    sol = sol_ref[...].astype(F32)
    for rel in range(4):
        core = flip(c, rel % 2)
        for second in range(2):
            plane = plane_at(y, x, core, rel // 2, second)
            for j in range(4):
                col = pl.multiple_of((z_flip(z, j) * 8 + plane * 2 + core) * 128, 128)
                here = (second * 4 + j) * 128
                tops[rel][:, here : here + 128] = border_ref[:, pl.ds(col, 128)].astype(F32)
        tops[rel][:, 1024:] = sol


def prep_mid(border_ref, *mids):
    z, y, x, c = coords()
    front = border_ref.shape[1] // 2
    for rel in range(4):
        core = flip(c, rel % 2)
        for second in range(2):
            plane = plane_at(y, x, core, rel // 2, second)
            for k in range(2):
                col = front + (flip(z % 2, k) * 8 + plane * 2 + core) * 256
                here = (second * 2 + k) * 256
                mids[rel][:, here : here + 256] = border_ref[
                    :, pl.ds(pl.multiple_of(col, 256), 256)
                ].astype(F32)


def plane_inputs(parts):
    return [
        parts[0],
        swap(parts[1], CORE),
        permute(parts[2], lambda i: i ^ (YBIT if i & 1 else XBIT)),
        permute(parts[3], lambda i: i ^ (XBIT + CORE if i & 1 else YBIT + CORE)),
    ]


def swap_loads(value):
    return permute(value, lambda i: i ^ (XBIT if i & 1 else YBIT))


def stack_rows(refs, cols, out_ref):
    n = refs[0].shape[0]
    for i, ref in enumerate(refs):
        out_ref[i * n : (i + 1) * n, :] = ref[:, cols].astype(BF16)


def put_loads(sol, rows, outs):
    total = lax.dot_general(
        sol, rows, (((0,), (0,)), ((), ())), preferred_element_type=F32
    )
    for second in range(2):
        for j in range(4):
            here = (second * 4 + j) * 128
            block = total[:, here : here + 128].T
            for h, packed in enumerate(pack(block[:WIDE], block[WIDE:])):
                outs[second][j, h] = packed


def top_load_kernel(*refs):
    ins, (keep_ref, send_ref, sol_ref, rows_ref) = refs[:4], refs[4:]
    stack_rows(ins, slice(0, 1024), rows_ref)
    stack_rows(ins, slice(1024, 1152), sol_ref)
    put_loads(sol_ref[...], rows_ref[...], [keep_ref, send_ref])


def mid_load_kernel(*refs):
    ins, (sol_ref, keep_ref, send_ref, rows_ref) = refs[:4], refs[4:]
    stack_rows(ins, slice(0, 1024), rows_ref)
    put_loads(sol_ref[...], rows_ref[...], [keep_ref, send_ref])


def widen_kernel(w_ref, out_ref):
    out_ref[...] = w_ref[...].astype(F32)


def widen(w, after=()):
    return kernel_call(widen_kernel, [(w.shape, F32)], [w], after=after)[0]


def widen_halves_kernel(w_ref, low_ref, high_ref):
    rows = low_ref.shape[0]
    low_ref[...] = w_ref[:rows, :].astype(F32)
    high_ref[...] = w_ref[rows:, :].astype(F32)


def widen_halves(w):
    shape = (w.shape[0] // 2, w.shape[1])
    return kernel_call(widen_halves_kernel, [(shape, F32)] * 2, [w])


def join_halves(keep, recv):
    m, n = keep.shape

    def kernel(keep_ref, low_ref, high_ref, w_ref, t_ref):
        w_ref[:, :n] = keep_ref[...]
        t_ref[:n, :] = keep_ref[...].T
        for i, ref in enumerate((low_ref, high_ref)):
            here = slice(i * m // 2, (i + 1) * m // 2)
            part = ref[...].astype(BF16)
            w_ref[here, n:] = part
            t_ref[n:, here] = part.T

    return kernel_call(kernel, [((m, 2 * n), BF16), ((2 * n, m), BF16)], [keep, *recv])


def join_cols_kernel(keep_ref, recv_ref, w_ref, t_ref):
    n = keep_ref.shape[1]
    recv = recv_ref[...].astype(BF16)
    w_ref[:, :n] = keep_ref[...]
    w_ref[:, n:] = recv
    t_ref[:n, :] = keep_ref[...].T
    t_ref[n:, :] = recv.T


def join_cols(keep, recv, parts=4):
    m, n = keep.shape
    step = m // parts
    shapes = [jax.ShapeDtypeStruct((m, 2 * n), BF16), jax.ShapeDtypeStruct((2 * n, m), BF16)]
    return pl.pallas_call(
        join_cols_kernel,
        grid=(parts,),
        out_shape=shapes,
        in_specs=[pl.BlockSpec((step, n), lambda i: (i, 0))] * 2,
        out_specs=[
            pl.BlockSpec((step, 2 * n), lambda i: (i, 0)),
            pl.BlockSpec((2 * n, step), lambda i: (0, i)),
        ],
        compiler_params=pltpu.CompilerParams(vmem_limit_bytes=12 * 2**20),
        cost_estimate=pl.CostEstimate(
            flops=0,
            transcendentals=0,
            bytes_accessed=sum(map(size_of, [keep, recv, *shapes])),
        ),
    )(keep, recv)


def join_rows_kernel(keep_ref, recv_ref, w_ref):
    n = keep_ref.shape[0]
    w_ref[:n, :] = keep_ref[...]
    w_ref[n:, :] = recv_ref[...].astype(BF16)


def join_rows(keep, recv, parts=4):
    m, n = keep.shape
    step = n // parts
    shape = jax.ShapeDtypeStruct((2 * m, n), BF16)
    return pl.pallas_call(
        join_rows_kernel,
        grid=(parts,),
        out_shape=shape,
        in_specs=[pl.BlockSpec((m, step), lambda i: (0, i))] * 2,
        out_specs=pl.BlockSpec((2 * m, step), lambda i: (0, i)),
        compiler_params=pltpu.CompilerParams(vmem_limit_bytes=12 * 2**20),
        cost_estimate=pl.CostEstimate(
            flops=0,
            transcendentals=0,
            bytes_accessed=sum(map(size_of, [keep, recv, shape])),
        ),
    )(keep, recv)


def forward(deep, w_ref, *refs):
    vec, outs, (rhs_ref, sum_ref) = refs[:-8], refs[-8:-2], refs[-2:]
    own, other = vec[0][...], vec[1][...]
    blocks = own.shape[0]
    if len(vec) == 3:
        own = own - vec[2][:blocks]
        other = other - vec[2][blocks:]
    for i in range(blocks):
        put_split(rhs_ref, i * 128, own[i])
        put_split(rhs_ref, (blocks + i) * 128, other[i])
    step = w_ref.shape[0] // 4
    for i in range(4):
        here = slice(i * step, (i + 1) * step)
        sum_ref[here, :] = product(w_ref[here, :], rhs_ref)
    left = left_lanes((WIDE, 2 * WIDE))
    for colour in range(2):
        send_ref, next_ref, keep_ref = outs[3 * colour : 3 * colour + 3]
        for i, start in enumerate(block_starts(deep, colour)):
            low = sum_ref[pl.ds(start, WIDE), :]
            high = sum_ref[pl.ds(start + WIDE, WIDE), :]
            block = jnp.where(left, low, high)
            if i < 4:
                keep_ref[i] = block
            elif i < 8:
                next_ref[i - 4] = block
            else:
                send_ref[i - 8] = block


def backward(deep, w_ref, near0, far0, near1, far1, *refs):
    outs, rhs_ref = refs[:-1], refs[-1]
    for colour, (near, far) in enumerate(((near0, far0), (near1, far1))):
        for i, start in enumerate(block_starts(deep, colour)):
            put_split(rhs_ref, start, near[i] if i < 8 else far[i - 8])
    total = product(w_ref[...], rhs_ref)
    blocks = outs[0].shape[0]
    for i in range(blocks):
        outs[0][i] = take_block(total, i * 128)
        if len(outs) > 1 and i >= blocks // 2:
            outs[1][i - blocks // 2] = outs[0][i]


def run_forward(w, vec, deep, after=()):
    m, k = w.shape
    return kernel_call(
        functools.partial(forward, deep),
        [((8, WIDE, 128), F32), ((4, WIDE, 128), F32), ((4, WIDE, 128), F32)] * 2,
        [w, *vec],
        [pltpu.VMEM((k, 128), BF16), pltpu.VMEM((m, 128), F32)],
        flops=2 * m * k * 128,
        limit=16,
        after=after,
    )


def run_backward(w, pieces, deep, alone, after=()):
    m, k = w.shape
    blocks = m // 128
    outs = [((blocks, WIDE, 128), F32)]
    if alone:
        outs.append(((blocks // 2, WIDE, 128), F32))
    return kernel_call(
        functools.partial(backward, deep),
        outs,
        [w, *pieces],
        [pltpu.VMEM((k, 128), BF16)],
        flops=2 * m * k * 128,
        limit=16,
        after=after,
    )


def along_line(parts):
    got = {j: swap(parts[j], j * ZBIT) for j in FAR_FIRST}
    return [got[j] for j in (1, 2, 3)]


def cut(v):
    return tuple(v[j] for j in range(4))


def depth_load(keep, got):
    parts = glue(lambda a, b: cut(a + b), keep, got)
    (own,) = glue(lambda *p: (p[0] + p[1] + p[2] + p[3],), parts[0], *along_line(parts))
    return own


def pair_load(keep, got):
    v = keep + got
    return v[:2] + swap(v[2:], ZBIT)


def by_core(own):
    c = lax.axis_index("panel") % 2
    mine = jnp.where(c == 0, own[:, 0], own[:, 1])
    theirs = jnp.where(c == 0, own[:, 1], own[:, 0])
    return [mine, swap(theirs, CORE)]


def plane_sum(parts):
    out = []
    firsts = [swap_first(parts[3 * k], k) for k in range(2)]
    for k in range(2):
        (follow,) = glue(lambda a, b: (a + b[4:],), parts[3 * k + 1], firsts[k])
        out += [parts[3 * k + 2], firsts[k], swap_second(follow, k)]
    return out


def colours(k0, f0, s0, k1, f1, s1):
    return jnp.stack([k0 + f0[:4] + s0, k1 + f1[:4] + s1], 1)


def depth_sum(pieces):
    parts = glue(lambda *p: cut(colours(*p)), *pieces)
    got = along_line(parts)
    (own,) = glue(lambda *p: (p[0] + p[1] + p[2] + p[3],), parts[0], *got)
    return own, got


def depth_spread(own, after=()):
    def lines(*p):
        return tuple(jnp.stack([v[k] for v in p]) for k in range(2))

    return glue(lines, own, *along_line([own] * 4), after=after)


def pair_total(pieces):
    def both(*p):
        v = colours(*p)
        return v, jnp.concatenate([v[2:], v[:2]], 0)

    value, turned = glue(both, *pieces)
    got = swap(turned, ZBIT)
    return glue(lambda v, g: ((v + g)[:, 0], (v + g)[:, 1]), value, got)


def plane_spread(pair_of_lines):
    pieces = []
    seconds = [swap_second(line, k) for k, line in enumerate(pair_of_lines)]
    for k, line in enumerate(pair_of_lines):
        (near,) = glue(lambda a, b: (jnp.concatenate([a, b], 0),), line, seconds[k])
        pieces += [near, swap_first(near, k)]
    return pieces


def unpack_kernel(mine_ref, recv_ref, out_ref):
    c = lax.axis_index("panel") % 2
    blocks = recv_ref.shape[0]
    left = left_lanes((WIDE, 128))
    for i in range(blocks):
        mine, recv = mine_ref[i], recv_ref[i]
        here = jnp.broadcast_to(c == 0, mine.shape)
        p0, p1 = jnp.where(here, mine, recv), jnp.where(here, recv, mine)
        out_ref[i * 128 : i * 128 + WIDE, :] = jnp.where(left, p0, pltpu.roll(p1, WIDE, 1))
        out_ref[i * 128 + WIDE : (i + 1) * 128, :] = jnp.where(left, pltpu.roll(p0, WIDE, 1), p1)


def unpack(mine, recv):
    return kernel_call(unpack_kernel, [((recv.shape[0] * 128, 128), F32)], [mine, recv])[0]


def fast_body(border, solution, winv_top, winv_mid, coupling):
    ready = kernel_call(
        prep_top, [((32, 1152), F32)] * 4, [border[0], solution[0]]
    )
    tops = plane_inputs(ready)
    keep, send, sol_all = kernel_call(
        top_load_kernel,
        [((4, 2, WIDE, 128), F32)] * 2 + [((128, 128), BF16)],
        tops,
        [pltpu.VMEM((128, 1024), BF16)],
        flops=2 * 128 * 1024 * 128,
    )
    top_w, top_t = join_halves(
        winv_top, [swap(part, CORE) for part in widen_halves(winv_top)]
    )
    load = by_core(depth_load(keep, swap_loads(send))[None])

    parts = run_forward(top_w, load, True)
    inner, marks = depth_sum(plane_sum(parts))
    mids = plane_inputs(
        kernel_call(prep_mid, [((32, 1024), F32)] * 4, [border[0]], after=marks[:1])
    )
    pair = depth_spread(inner, after=mids)
    cou_w = join_rows(coupling, swap(widen(coupling, after=pair[:1]), CORE))
    mid_w, mid_t = join_cols(winv_mid, swap(widen(winv_mid, after=pair[:1]), CORE))
    pieces = plane_spread(pair)
    adjoint, theirs = run_backward(top_t, pieces, True, True)
    top_out = unpack(adjoint, swap(theirs, CORE))

    keep, send = kernel_call(
        mid_load_kernel,
        [((4, 2, WIDE, 128), F32)] * 2,
        [*mids, sol_all],
        [pltpu.VMEM((128, 1024), BF16)],
        flops=2 * 128 * 1024 * 128,
    )
    got = swap_loads(send)
    load = by_core(pair_load(keep, got))

    pieces = plane_spread(depth_spread(adjoint, after=[got]))
    (part,) = run_backward(cou_w, pieces, True, False, after=[top_out])
    parts = run_forward(mid_w, [*load, part], False)
    pieces = plane_spread(pair_total(plane_sum(parts)))
    adjoint, theirs = run_backward(mid_t, pieces, False, True)
    return top_out, unpack(adjoint, swap(theirs, CORE))


def solution(mesh):
    placed = (
        P("leaf", "panel", None),
        P("leaf", "panel", None),
        P(None, AXES),
        P(None, AXES),
        P(AXES, None),
    )
    fits = mesh.shape["leaf"] == 8 and mesh.shape["panel"] == 4
    return jax.shard_map(
        fast_body if fits else plain_body,
        mesh=mesh,
        in_specs=placed,
        out_specs=(P(AXES, None), P(AXES, None)),
        check_vma=False,
    )
```

```python
import functools

import jax
import jax.numpy as jnp
from jax import lax
from jax.experimental import pallas as pl
from jax.experimental.pallas import tpu as pltpu
from jax.sharding import PartitionSpec as P

AXES = ("leaf", "panel")
F32 = jnp.float32
BF16 = jnp.bfloat16
LANES = 128


def plain_body(border, solution, winv_top, winv_mid, coupling):
    leaves = lax.axis_size("leaf")
    panels = lax.axis_size("panel")
    half = leaves // 2
    leaf_id = lax.axis_index("leaf")
    front = winv_top.shape[0]
    top_cols = winv_top.shape[1]
    mid_cols = winv_mid.shape[1]
    contribution = lax.dot_general(
        border[0], solution[0], (((0,), (0,)), ((), ())), preferred_element_type=F32
    )
    groups = [list(range(half)), list(range(half, leaves))]
    device = leaf_id * panels + lax.axis_index("panel")
    in_half = device % (half * panels)
    top_load = lax.psum(contribution[:front], AXES)
    top_block = lax.dynamic_slice_in_dim(top_load, device * top_cols, top_cols, 0)
    mid_load = lax.psum(contribution[front:], "panel")
    mid_load = lax.psum(mid_load, "leaf", axis_index_groups=groups)
    mid_block = lax.dynamic_slice_in_dim(mid_load, in_half * mid_cols, mid_cols, 0)
    top_factor = winv_top.astype(F32)
    mid_factor = winv_mid.astype(F32)
    exact = lax.Precision.HIGHEST
    top_inner = lax.psum(jnp.dot(top_factor, top_block, precision=exact), AXES)
    top_adjoint = jnp.dot(top_factor.T, top_inner, precision=exact)
    top_whole = lax.all_gather(top_adjoint, AXES, axis=0, tiled=True)
    mid_rhs = mid_block - jnp.dot(coupling.astype(F32), top_whole, precision=exact)
    mid_inner = lax.psum(jnp.dot(mid_factor, mid_rhs, precision=exact), "panel")
    mid_inner = lax.psum(mid_inner, "leaf", axis_index_groups=groups)
    mid_adjoint = jnp.dot(mid_factor.T, mid_inner, precision=exact)
    return top_adjoint, mid_adjoint


CHAINS = 2
WIDE = 64


def permute(value, partner):
    return lax.ppermute(value, AXES, [(i, partner(i)) for i in range(32)])


def swap_core(value):
    return permute(value, lambda i: i ^ 1)


def swap_first(value, chain=0):
    return permute(value, lambda i: i ^ (4 if (i ^ chain) & 1 else 2))


def swap_second(value, chain=0):
    return permute(value, lambda i: i ^ (2 if (i ^ chain) & 1 else 4))


def swap_cross(value):
    return permute(value, lambda i: i ^ (3 if i & 1 else 5))


def swap_near(value):
    return permute(value, lambda i: i ^ 8)


def swap_far(value):
    return permute(value, lambda i: i ^ 16)


def coords():
    leaf = lax.axis_index("leaf")
    panel = lax.axis_index("panel")
    return leaf // 2, leaf % 2, panel // 2, panel % 2


def flip(a, k):
    return a + k - 2 * a * k


def z_flip(z, k):
    return flip(z // 2, k // 2) * 2 + flip(z % 2, k % 2)


Z_ORDER = (0, 2, 1, 3)


def plane_at(y, x, c, first, second):
    along_x = first * (1 - c) + second * c
    along_y = first * c + second * (1 - c)
    return flip(y, along_y) * 2 + flip(x, along_x)


def block_starts(deep, chain):
    z, y, x, c = coords()
    c = flip(c, chain)
    starts = []
    for first in range(2):
        for second in range(2):
            plane = plane_at(y, x, c, first, second)
            for j in range(4):
                if deep:
                    start = (z_flip(z, Z_ORDER[j]) * 4 + plane) * 128
                else:
                    start = (flip(z % 2, j // 2) * 4 + plane) * 256 + j % 2 * 128
                starts.append(pl.multiple_of(start, 128))
    return starts


def kernel_call(kernel, outs, ins, scratch=(), flops=0, limit=10, after=()):
    vmem = pl.BlockSpec(memory_space=pltpu.VMEM)
    size = lambda s: s.size * s.dtype.itemsize

    def ordered(*refs):
        kernel(*refs[: len(ins)], *refs[len(ins) + len(after) :])

    return pl.pallas_call(
        ordered,
        out_shape=[jax.ShapeDtypeStruct(*o) for o in outs],
        in_specs=[vmem] * len(ins) + [pl.BlockSpec(memory_space=pl.ANY)] * len(after),
        out_specs=[vmem] * len(outs),
        scratch_shapes=list(scratch),
        compiler_params=pltpu.CompilerParams(vmem_limit_bytes=limit * 2**20),
        cost_estimate=pl.CostEstimate(
            flops=flops,
            transcendentals=0,
            bytes_accessed=sum(map(size, ins))
            + sum(size(jax.ShapeDtypeStruct(*o)) for o in outs),
        ),
    )(*ins, *after)


def glue(fn, *ins, after=()):
    shapes = jax.eval_shape(fn, *ins)

    def kernel(*refs):
        values = fn(*[r[...] for r in refs[: len(ins)]])
        for ref, value in zip(refs[len(ins) :], values):
            ref[...] = value

    return kernel_call(kernel, [(o.shape, o.dtype) for o in shapes], ins, after=after)


def left_lanes(shape):
    return lax.broadcasted_iota(jnp.int32, shape, 1) < WIDE


def pack(low, high):
    left = left_lanes(low.shape)
    return (
        jnp.where(left, low, pltpu.roll(high, WIDE, 1)),
        jnp.where(left, pltpu.roll(low, WIDE, 1), high),
    )


def put_split(rhs_ref, start, block):
    left = left_lanes(block.shape)
    turned = pltpu.roll(block, WIDE, 1)
    for i, rows in enumerate((jnp.where(left, block, turned), jnp.where(left, turned, block))):
        high = rows.astype(BF16).astype(F32)
        both = jnp.where(left, high, rows - high)
        rhs_ref[pl.ds(start + i * WIDE, WIDE), :] = both.astype(BF16)


def product(w_ref, rhs_ref):
    both = jnp.dot(w_ref[...], rhs_ref[...], preferred_element_type=F32)
    return both + pltpu.roll(both, WIDE, 1)


def take_block(total, start):
    low = total[start : start + WIDE]
    high = total[start + WIDE : start + 2 * WIDE]
    return jnp.where(left_lanes(low.shape), low, high)


def prep_top(border_ref, sol_ref, *tops):
    z, y, x, c = coords()
    sol = sol_ref[...].astype(F32)
    for rel in range(4):
        core = flip(c, rel % 2)
        for second in range(2):
            plane = plane_at(y, x, core, rel // 2, second)
            for j in range(4):
                col = pl.multiple_of((z_flip(z, Z_ORDER[j]) * 8 + plane * 2 + core) * 128, 128)
                here = (second * 4 + j) * 128
                tops[rel][:, here : here + 128] = border_ref[:, pl.ds(col, 128)].astype(F32)
        tops[rel][:, 1024:] = sol


def prep_mid(border_ref, *mids):
    z, y, x, c = coords()
    front = border_ref.shape[1] // 2
    for rel in range(4):
        core = flip(c, rel % 2)
        for second in range(2):
            plane = plane_at(y, x, core, rel // 2, second)
            for k in range(2):
                col = front + (flip(z % 2, k) * 8 + plane * 2 + core) * 256
                here = (second * 2 + k) * 256
                mids[rel][:, here : here + 256] = border_ref[
                    :, pl.ds(pl.multiple_of(col, 256), 256)
                ].astype(F32)


def stack_rows(refs, cols, out_ref):
    n = refs[0].shape[0]
    for i, ref in enumerate(refs):
        out_ref[i * n : (i + 1) * n, :] = ref[:, cols].astype(BF16)


def put_loads(sol, rows, outs):
    total = lax.dot_general(
        sol, rows, (((0,), (0,)), ((), ())), preferred_element_type=F32
    )
    for second in range(2):
        for j in range(4):
            here = (second * 4 + j) * 128
            block = total[:, here : here + 128].T
            packed = pack(block[:WIDE], block[WIDE:])
            for h in range(CHAINS):
                outs[h][second][j] = packed[h]


def top_load_kernel(*refs):
    ins, outs, sol_ref, rows_ref = refs[:4], refs[4:8], refs[8], refs[9]
    stack_rows(ins, slice(0, 1024), rows_ref)
    stack_rows(ins, slice(1024, 1152), sol_ref)
    put_loads(sol_ref[...], rows_ref[...], [outs[:2], outs[2:]])


def mid_load_kernel(*refs):
    ins, sol_ref, keep_ref, send_ref, rows_ref = refs[:4], *refs[4:]
    stack_rows(ins, slice(0, 1024), rows_ref)
    outs = [[keep_ref.at[h], send_ref.at[h]] for h in range(CHAINS)]
    put_loads(sol_ref[...], rows_ref[...], outs)


def halve_rows(w_ref, keep_ref, send_ref):
    z, y, x, c = coords()
    rows = w_ref.shape[0] // 2
    keep_ref[...] = w_ref[pl.ds(pl.multiple_of(c * rows, rows), rows), :]
    send_ref[...] = w_ref[pl.ds(pl.multiple_of((1 - c) * rows, rows), rows), :].astype(F32)


def halve_cols(w_ref, keep_ref, send_ref):
    z, y, x, c = coords()
    for i in range(w_ref.shape[1] // 256):
        here = slice(i * 128, (i + 1) * 128)
        kept = pl.multiple_of(i * 256 + c * 128, 128)
        sent = pl.multiple_of(i * 256 + (1 - c) * 128, 128)
        keep_ref[:, here] = w_ref[:, pl.ds(kept, 128)]
        send_ref[:, here] = w_ref[:, pl.ds(sent, 128)].astype(F32)


def join_cols(keep_ref, recv_ref, w_ref, t_ref):
    n = keep_ref.shape[1]
    w_ref[:, :n] = keep_ref[...]
    w_ref[:, n:] = recv_ref[...].astype(BF16)
    t_ref[:n, :] = keep_ref[...].T
    t_ref[n:, :] = recv_ref[...].astype(BF16).T


def join_rows(keep_ref, recv_ref, w_ref):
    n = keep_ref.shape[0]
    w_ref[:n, :] = keep_ref[...]
    w_ref[n:, :] = recv_ref[...].astype(BF16)


def forward(deep, chain, w_ref, *refs):
    vec, (send_ref, next_ref, keep_ref), (rhs_ref, sum_ref) = refs[:-5], refs[-5:-2], refs[-2:]
    blocks = vec[0].shape[0]
    if len(vec) == 2:
        own, other = vec[0][...], vec[1][...]
    else:
        mine, theirs, part, recv = [v[...] for v in vec]
        own = mine - part[:blocks] - recv[blocks:]
        other = theirs - part[blocks:] - recv[:blocks]
    for i in range(blocks):
        put_split(rhs_ref, i * 128, own[i])
        put_split(rhs_ref, (blocks + i) * 128, other[i])
    sum_ref[...] = product(w_ref, rhs_ref)
    left = left_lanes((WIDE, 2 * WIDE))
    for i, start in enumerate(block_starts(deep, chain)):
        low = sum_ref[pl.ds(start, WIDE), :]
        high = sum_ref[pl.ds(start + WIDE, WIDE), :]
        block = jnp.where(left, low, high)
        if i < 4:
            keep_ref[i] = block
        elif i < 8:
            next_ref[i - 4] = block
        else:
            send_ref[i - 8] = block


def backward(deep, chain, w_ref, near_ref, far_ref, *refs):
    outs, rhs_ref = refs[:-1], refs[-1]
    for i, start in enumerate(block_starts(deep, chain)):
        put_split(rhs_ref, start, near_ref[i] if i < 8 else far_ref[i - 8])
    total = product(w_ref, rhs_ref)
    blocks = w_ref.shape[0] // 128
    for i in range(blocks):
        if len(outs) == 1:
            outs[0][i] = take_block(total, i * 128)
        else:
            outs[2 * i // blocks][i % (blocks // 2)] = take_block(total, i * 128)


def run_forward(w, vec, deep, chain, after=()):
    m, k = w.shape
    return kernel_call(
        functools.partial(forward, deep, chain),
        [((8, WIDE, 128), F32), ((4, WIDE, 128), F32), ((4, WIDE, 128), F32)],
        [w, *vec],
        [pltpu.VMEM((k, 128), BF16), pltpu.VMEM((m, 128), F32)],
        flops=2 * m * k * 128,
        after=after,
    )


def run_backward(w, near, far, deep, chain, apart, after=()):
    m, k = w.shape
    return kernel_call(
        functools.partial(backward, deep, chain),
        [((m // 256, WIDE, 128), F32)] * 2 if apart else [((m // 128, WIDE, 128), F32)],
        [w, near, far],
        [pltpu.VMEM((k, 128), BF16)],
        flops=2 * m * k * 128,
        after=after,
    )


def depth_sum(value, deep):
    half = value.shape[-3] // 2
    keep, send = value[..., :half, :, :], value[..., half:, :, :]
    value = keep + swap_near(send)
    if deep:
        value = value[:1] + swap_far(value[1:])
    return value


def plane_sum(send, follow, keep, chain):
    first = swap_first(send, chain)
    second = swap_second(follow + first[4:], chain)
    return keep + first[:4] + second, second


def join(a, b, after=()):
    return glue(lambda p, q: (jnp.concatenate([p, q], 0),), a, b, after=after)[0]


def depth_total(value, deep, after=()):
    if not deep:
        return value + swap_near(jnp.concatenate([value[2:], value[:2]], 0))
    keep = value[:2] + swap_near(value[2:])
    keep = keep + swap_far(jnp.concatenate([keep[1:], keep[:1]], 0))
    return join(keep, swap_near(keep), after)


def depth_spread(own, after=()):
    pair = jnp.concatenate([own, swap_far(own)], 0)
    return join(pair, swap_near(pair), after)


def plane_spread(line, chain):
    near = jnp.concatenate([line, swap_second(line, chain)], 0)
    return near, swap_first(near, chain)


def unpack_kernel(mine0, recv0, mine1, recv1, out_ref):
    left = left_lanes((WIDE, 128))
    for i in range(mine0.shape[0]):
        p0 = mine0[i] + recv0[i]
        p1 = mine1[i] + recv1[i]
        out_ref[i * 128 : i * 128 + WIDE, :] = jnp.where(left, p0, pltpu.roll(p1, WIDE, 1))
        out_ref[i * 128 + WIDE : (i + 1) * 128, :] = jnp.where(left, pltpu.roll(p0, WIDE, 1), p1)


def unpack(*pairs):
    ins = [array for pair in pairs for array in pair]
    return kernel_call(unpack_kernel, [((ins[0].shape[0] * 128, 128), F32)], ins)[0]


def fast_body(border, solution, winv_top, winv_mid, coupling):
    front = winv_top.shape[0]
    half = front // 2
    tops = ready = kernel_call(
        prep_top, [((32, 1152), F32)] * 4, [border[0], solution[0]]
    )
    tops = [tops[0], swap_core(tops[1]), swap_first(tops[2]), swap_cross(tops[3])]
    *loads, sol_all = kernel_call(
        top_load_kernel,
        [((4, WIDE, 128), F32)] * 4 + [((128, 128), BF16)],
        tops,
        [pltpu.VMEM((128, 1024), BF16)],
        flops=2 * 128 * 1024 * 128,
    )
    plane_loads = [swap_second(loads[2 * h + 1]) for h in range(CHAINS)]
    load = [depth_sum(loads[2 * h] + plane_loads[h], True) for h in range(CHAINS)]

    top_keep, top_send = kernel_call(
        halve_rows, [((half, 128), BF16), ((half, 128), F32)], [winv_top], after=ready[:1]
    )
    cou_keep, cou_send = kernel_call(
        halve_cols, [((256, half), BF16), ((256, half), F32)], [coupling]
    )
    top_w, top_t = kernel_call(
        join_cols,
        [((half, 256), BF16), ((256, half), BF16)],
        [top_keep, swap_core(top_send)],
    )
    (cou_w,) = kernel_call(
        join_rows, [((512, half), BF16)], [cou_keep, swap_core(cou_send)]
    )

    chains = range(CHAINS)
    values = []
    for h in chains:
        parts = run_forward(top_w, [load[h], swap_core(load[h])], True, h)
        values.append(plane_sum(*parts, h))
    mids = kernel_call(
        prep_mid, [((32, 1024), F32)] * 4, [border[0]], after=[values[0][1]]
    )
    mids = [mids[0], swap_core(mids[1]), swap_first(mids[2]), swap_cross(mids[3])]
    top_parts, adjoint = [], []
    for h in chains:
        line = depth_total(values[h][0], True, after=mids if h else ())
        mine, theirs = run_backward(
            top_t, *plane_spread(line, h), True, h, True, after=[cou_w]
        )
        top_parts.append((mine, swap_core(theirs)))
        adjoint.append(mine + top_parts[h][1])
    top_out = unpack(*top_parts)

    mid_keep, mid_send = kernel_call(
        halve_rows, [((half, 256), BF16), ((half, 256), F32)], [winv_mid],
        after=[top_parts[0][0]],
    )
    mid_w, mid_t = kernel_call(
        join_cols,
        [((half, 512), BF16), ((512, half), BF16)],
        [mid_keep, swap_core(mid_send)],
    )

    keep, send = kernel_call(
        mid_load_kernel,
        [((CHAINS, 4, WIDE, 128), F32)] * 2,
        [*mids, sol_all],
        [pltpu.VMEM((128, 1024), BF16)],
        flops=2 * 128 * 1024 * 128,
        after=[top_parts[0][0]],
    )
    got = swap_second(send)
    lines = [depth_spread(adjoint[h], after=[got] if h else ()) for h in chains]
    keep, send = glue(
        lambda k, g: ((k + g)[:, :2], (k + g)[:, 2:]), keep, got, after=lines[1:]
    )
    mid_load = keep + swap_near(send)
    mid_other = swap_core(mid_load)

    mid_parts = []
    for h in chains:
        (both,) = run_backward(
            cou_w, *plane_spread(lines[h], h), True, h, False, after=[mid_w]
        )
        vec = [mid_load[h], mid_other[h], both, swap_core(both)]
        parts = run_forward(mid_w, vec, False, h, after=[top_out] if h else ())
        line = depth_total(plane_sum(*parts, h)[0], False)
        mine, theirs = run_backward(mid_t, *plane_spread(line, h), False, h, True)
        mid_parts.append((mine, swap_core(theirs)))
    return top_out, unpack(*mid_parts)


def solution(mesh):
    placed = (
        P("leaf", "panel", None),
        P("leaf", "panel", None),
        P(None, AXES),
        P(None, AXES),
        P(AXES, None),
    )
    fits = mesh.shape["leaf"] == 8 and mesh.shape["panel"] == 4
    return jax.shard_map(
        fast_body if fits else plain_body,
        mesh=mesh,
        in_specs=placed,
        out_specs=(P(AXES, None), P(AXES, None)),
        check_vma=False,
    )
```

```python
import functools

import jax
import jax.numpy as jnp
from jax import lax
from jax.experimental import pallas as pl
from jax.experimental.pallas import tpu as pltpu
from jax.sharding import PartitionSpec as P

AXES = ("leaf", "panel")
F32 = jnp.float32
BF16 = jnp.bfloat16
LANES = 128


def plain_body(border, solution, winv_top, winv_mid, coupling):
    leaves = lax.axis_size("leaf")
    panels = lax.axis_size("panel")
    half = leaves // 2
    leaf_id = lax.axis_index("leaf")
    front = winv_top.shape[0]
    top_cols = winv_top.shape[1]
    mid_cols = winv_mid.shape[1]
    contribution = lax.dot_general(
        border[0], solution[0], (((0,), (0,)), ((), ())), preferred_element_type=F32
    )
    groups = [list(range(half)), list(range(half, leaves))]
    device = leaf_id * panels + lax.axis_index("panel")
    in_half = device % (half * panels)
    top_load = lax.psum(contribution[:front], AXES)
    top_block = lax.dynamic_slice_in_dim(top_load, device * top_cols, top_cols, 0)
    mid_load = lax.psum(contribution[front:], "panel")
    mid_load = lax.psum(mid_load, "leaf", axis_index_groups=groups)
    mid_block = lax.dynamic_slice_in_dim(mid_load, in_half * mid_cols, mid_cols, 0)
    top_factor = winv_top.astype(F32)
    mid_factor = winv_mid.astype(F32)
    exact = lax.Precision.HIGHEST
    top_inner = lax.psum(jnp.dot(top_factor, top_block, precision=exact), AXES)
    top_adjoint = jnp.dot(top_factor.T, top_inner, precision=exact)
    top_whole = lax.all_gather(top_adjoint, AXES, axis=0, tiled=True)
    mid_rhs = mid_block - jnp.dot(coupling.astype(F32), top_whole, precision=exact)
    mid_inner = lax.psum(jnp.dot(mid_factor, mid_rhs, precision=exact), "panel")
    mid_inner = lax.psum(mid_inner, "leaf", axis_index_groups=groups)
    mid_adjoint = jnp.dot(mid_factor.T, mid_inner, precision=exact)
    return top_adjoint, mid_adjoint


CHAINS = 2
WIDE = 64


def permute(value, partner):
    return lax.ppermute(value, AXES, [(i, partner(i)) for i in range(32)])


def swap_core(value):
    return permute(value, lambda i: i ^ 1)


def swap_first(value, chain=0):
    return permute(value, lambda i: i ^ (4 if (i ^ chain) & 1 else 2))


def swap_second(value, chain=0):
    return permute(value, lambda i: i ^ (2 if (i ^ chain) & 1 else 4))


def swap_cross(value):
    return permute(value, lambda i: i ^ (3 if i & 1 else 5))


def swap_near(value):
    return permute(value, lambda i: i ^ 8)


def swap_far(value):
    return permute(value, lambda i: i ^ 16)


def coords():
    leaf = lax.axis_index("leaf")
    panel = lax.axis_index("panel")
    return leaf // 2, leaf % 2, panel // 2, panel % 2


def flip(a, k):
    return a + k - 2 * a * k


def z_flip(z, k):
    return flip(z // 2, k // 2) * 2 + flip(z % 2, k % 2)


Z_ORDER = (0, 2, 1, 3)


def plane_at(y, x, c, first, second):
    along_x = first * (1 - c) + second * c
    along_y = first * c + second * (1 - c)
    return flip(y, along_y) * 2 + flip(x, along_x)


def block_starts(deep, chain):
    z, y, x, c = coords()
    c = flip(c, chain)
    starts = []
    for first in range(2):
        for second in range(2):
            plane = plane_at(y, x, c, first, second)
            for j in range(4):
                if deep:
                    start = (z_flip(z, Z_ORDER[j]) * 4 + plane) * 128
                else:
                    start = (flip(z % 2, j // 2) * 4 + plane) * 256 + j % 2 * 128
                starts.append(pl.multiple_of(start, 128))
    return starts


def kernel_call(kernel, outs, ins, scratch=(), flops=0, limit=10, after=()):
    vmem = pl.BlockSpec(memory_space=pltpu.VMEM)
    size = lambda s: s.size * s.dtype.itemsize

    def ordered(*refs):
        kernel(*refs[: len(ins)], *refs[len(ins) + len(after) :])

    return pl.pallas_call(
        ordered,
        out_shape=[jax.ShapeDtypeStruct(*o) for o in outs],
        in_specs=[vmem] * len(ins) + [pl.BlockSpec(memory_space=pl.ANY)] * len(after),
        out_specs=[vmem] * len(outs),
        scratch_shapes=list(scratch),
        compiler_params=pltpu.CompilerParams(vmem_limit_bytes=limit * 2**20),
        cost_estimate=pl.CostEstimate(
            flops=flops,
            transcendentals=0,
            bytes_accessed=sum(map(size, ins))
            + sum(size(jax.ShapeDtypeStruct(*o)) for o in outs),
        ),
    )(*ins, *after)


def glue(fn, *ins, after=()):
    shapes = jax.eval_shape(fn, *ins)

    def kernel(*refs):
        values = fn(*[r[...] for r in refs[: len(ins)]])
        for ref, value in zip(refs[len(ins) :], values):
            ref[...] = value

    return kernel_call(kernel, [(o.shape, o.dtype) for o in shapes], ins, after=after)


def left_lanes(shape):
    return lax.broadcasted_iota(jnp.int32, shape, 1) < WIDE


def pack(low, high):
    left = left_lanes(low.shape)
    return (
        jnp.where(left, low, pltpu.roll(high, WIDE, 1)),
        jnp.where(left, pltpu.roll(low, WIDE, 1), high),
    )


def put_split(rhs_ref, start, block):
    left = left_lanes(block.shape)
    turned = pltpu.roll(block, WIDE, 1)
    for i, rows in enumerate((jnp.where(left, block, turned), jnp.where(left, turned, block))):
        high = rows.astype(BF16).astype(F32)
        both = jnp.where(left, high, rows - high)
        rhs_ref[pl.ds(start + i * WIDE, WIDE), :] = both.astype(BF16)


def product(w_ref, rhs_ref):
    both = jnp.dot(w_ref[...], rhs_ref[...], preferred_element_type=F32)
    return both + pltpu.roll(both, WIDE, 1)


def take_block(total, start):
    low = total[start : start + WIDE]
    high = total[start + WIDE : start + 2 * WIDE]
    return jnp.where(left_lanes(low.shape), low, high)


def prep_top(border_ref, sol_ref, *tops):
    z, y, x, c = coords()
    sol = sol_ref[...].astype(F32)
    for rel in range(4):
        core = flip(c, rel % 2)
        for second in range(2):
            plane = plane_at(y, x, core, rel // 2, second)
            for j in range(4):
                col = pl.multiple_of((z_flip(z, Z_ORDER[j]) * 8 + plane * 2 + core) * 128, 128)
                here = (second * 4 + j) * 128
                tops[rel][:, here : here + 128] = border_ref[:, pl.ds(col, 128)].astype(F32)
        tops[rel][:, 1024:] = sol


def prep_mid(border_ref, *mids):
    z, y, x, c = coords()
    front = border_ref.shape[1] // 2
    for rel in range(4):
        core = flip(c, rel % 2)
        for second in range(2):
            plane = plane_at(y, x, core, rel // 2, second)
            for k in range(2):
                col = front + (flip(z % 2, k) * 8 + plane * 2 + core) * 256
                here = (second * 2 + k) * 256
                mids[rel][:, here : here + 256] = border_ref[
                    :, pl.ds(pl.multiple_of(col, 256), 256)
                ].astype(F32)


def stack_rows(refs, cols, out_ref):
    n = refs[0].shape[0]
    for i, ref in enumerate(refs):
        out_ref[i * n : (i + 1) * n, :] = ref[:, cols].astype(BF16)


def put_loads(sol, rows, outs):
    total = lax.dot_general(
        sol, rows, (((0,), (0,)), ((), ())), preferred_element_type=F32
    )
    for second in range(2):
        for j in range(4):
            here = (second * 4 + j) * 128
            block = total[:, here : here + 128].T
            packed = pack(block[:WIDE], block[WIDE:])
            for h in range(CHAINS):
                outs[h][second][j] = packed[h]


def top_load_kernel(*refs):
    ins, (keep_ref, send_ref, sol_ref, rows_ref) = refs[:4], refs[4:]
    stack_rows(ins, slice(0, 1024), rows_ref)
    stack_rows(ins, slice(1024, 1152), sol_ref)
    outs = [[keep_ref.at[h], send_ref.at[h]] for h in range(CHAINS)]
    put_loads(sol_ref[...], rows_ref[...], outs)


def mid_load_kernel(*refs):
    ins, sol_ref, keep_ref, send_ref, rows_ref = refs[:4], *refs[4:]
    stack_rows(ins, slice(0, 1024), rows_ref)
    outs = [[keep_ref.at[h], send_ref.at[h]] for h in range(CHAINS)]
    put_loads(sol_ref[...], rows_ref[...], outs)


def halve_rows(w_ref, keep_ref, send_ref):
    z, y, x, c = coords()
    rows = w_ref.shape[0] // 2
    keep_ref[...] = w_ref[pl.ds(pl.multiple_of(c * rows, rows), rows), :]
    send_ref[...] = w_ref[pl.ds(pl.multiple_of((1 - c) * rows, rows), rows), :].astype(F32)


def halve_cols(w_ref, keep_ref, send_ref):
    z, y, x, c = coords()
    for i in range(w_ref.shape[1] // 256):
        here = slice(i * 128, (i + 1) * 128)
        kept = pl.multiple_of(i * 256 + c * 128, 128)
        sent = pl.multiple_of(i * 256 + (1 - c) * 128, 128)
        keep_ref[:, here] = w_ref[:, pl.ds(kept, 128)]
        send_ref[:, here] = w_ref[:, pl.ds(sent, 128)].astype(F32)


def join_cols(keep_ref, recv_ref, w_ref, t_ref):
    n = keep_ref.shape[1]
    w_ref[:, :n] = keep_ref[...]
    w_ref[:, n:] = recv_ref[...].astype(BF16)
    t_ref[:n, :] = keep_ref[...].T
    t_ref[n:, :] = recv_ref[...].astype(BF16).T


def join_rows(keep_ref, recv_ref, w_ref):
    n = keep_ref.shape[0]
    w_ref[:n, :] = keep_ref[...]
    w_ref[n:, :] = recv_ref[...].astype(BF16)


def forward(deep, chain, w_ref, *refs):
    vec, (send_ref, next_ref, keep_ref), (rhs_ref, sum_ref) = refs[:-5], refs[-5:-2], refs[-2:]
    blocks = vec[0].shape[0]
    if len(vec) == 2:
        own, other = vec[0][...], vec[1][...]
    else:
        mine, theirs, part, recv = [v[...] for v in vec]
        own = mine - part[:blocks] - recv[blocks:]
        other = theirs - part[blocks:] - recv[:blocks]
    for i in range(blocks):
        put_split(rhs_ref, i * 128, own[i])
        put_split(rhs_ref, (blocks + i) * 128, other[i])
    sum_ref[...] = product(w_ref, rhs_ref)
    left = left_lanes((WIDE, 2 * WIDE))
    for i, start in enumerate(block_starts(deep, chain)):
        low = sum_ref[pl.ds(start, WIDE), :]
        high = sum_ref[pl.ds(start + WIDE, WIDE), :]
        block = jnp.where(left, low, high)
        if i < 4:
            keep_ref[i] = block
        elif i < 8:
            next_ref[i - 4] = block
        else:
            send_ref[i - 8] = block


def backward(deep, chain, w_ref, near_ref, far_ref, *refs):
    outs, rhs_ref = refs[:-1], refs[-1]
    for i, start in enumerate(block_starts(deep, chain)):
        put_split(rhs_ref, start, near_ref[i] if i < 8 else far_ref[i - 8])
    total = product(w_ref, rhs_ref)
    blocks = w_ref.shape[0] // 128
    for i in range(blocks):
        if len(outs) == 1:
            outs[0][i] = take_block(total, i * 128)
        else:
            outs[2 * i // blocks][i % (blocks // 2)] = take_block(total, i * 128)


def run_forward(w, vec, deep, chain, after=()):
    m, k = w.shape
    return kernel_call(
        functools.partial(forward, deep, chain),
        [((8, WIDE, 128), F32), ((4, WIDE, 128), F32), ((4, WIDE, 128), F32)],
        [w, *vec],
        [pltpu.VMEM((k, 128), BF16), pltpu.VMEM((m, 128), F32)],
        flops=2 * m * k * 128,
        after=after,
    )


def run_backward(w, near, far, deep, chain, apart, after=()):
    m, k = w.shape
    return kernel_call(
        functools.partial(backward, deep, chain),
        [((m // 256, WIDE, 128), F32)] * 2 if apart else [((m // 128, WIDE, 128), F32)],
        [w, near, far],
        [pltpu.VMEM((k, 128), BF16)],
        flops=2 * m * k * 128,
        after=after,
    )


def depth_sum(value):
    value = value[:, :2] + swap_near(value[:, 2:])
    return value[:, :1] + swap_far(value[:, 1:])


def plane_sum(send, follow, keep, chain):
    first = swap_first(send, chain)
    second = swap_second(follow + first[4:], chain)
    return keep + first[:4] + second, second


def depth_total(value, deep):
    if not deep:
        return value + swap_near(jnp.concatenate([value[2:], value[:2]], 0))
    keep = value[:2] + swap_near(value[2:])
    keep = keep + swap_far(jnp.concatenate([keep[1:], keep[:1]], 0))
    return jnp.concatenate([keep, swap_near(keep)], 0)


def depth_spread(own):
    pair = jnp.concatenate([own, swap_far(own)], 0)
    return jnp.concatenate([pair, swap_near(pair)], 0)


def plane_spread(line, chain):
    near = jnp.concatenate([line, swap_second(line, chain)], 0)
    return near, swap_first(near, chain)


def unpack_kernel(mine0, recv0, mine1, recv1, out_ref):
    left = left_lanes((WIDE, 128))
    for i in range(mine0.shape[0]):
        p0 = mine0[i] + recv0[i]
        p1 = mine1[i] + recv1[i]
        out_ref[i * 128 : i * 128 + WIDE, :] = jnp.where(left, p0, pltpu.roll(p1, WIDE, 1))
        out_ref[i * 128 + WIDE : (i + 1) * 128, :] = jnp.where(left, pltpu.roll(p0, WIDE, 1), p1)


def unpack(*pairs):
    ins = [array for pair in pairs for array in pair]
    return kernel_call(unpack_kernel, [((ins[0].shape[0] * 128, 128), F32)], ins)[0]


def fast_body(border, solution, winv_top, winv_mid, coupling):
    front = winv_top.shape[0]
    half = front // 2
    tops = ready = kernel_call(
        prep_top, [((32, 1152), F32)] * 4, [border[0], solution[0]]
    )
    tops = [tops[0], swap_core(tops[1]), swap_first(tops[2]), swap_cross(tops[3])]
    keep, send, sol_all = kernel_call(
        top_load_kernel,
        [((CHAINS, 4, WIDE, 128), F32)] * 2 + [((128, 128), BF16)],
        tops,
        [pltpu.VMEM((128, 1024), BF16)],
        flops=2 * 128 * 1024 * 128,
    )
    got = swap_second(send)
    load = depth_sum(keep + got)
    load_other = swap_core(load)

    mids = kernel_call(prep_mid, [((32, 1024), F32)] * 4, [border[0]], after=[got])
    mids = [mids[0], swap_core(mids[1]), swap_first(mids[2]), swap_cross(mids[3])]

    top_keep, top_send = kernel_call(
        halve_rows, [((half, 128), BF16), ((half, 128), F32)], [winv_top], after=ready[:1]
    )
    cou_keep, cou_send = kernel_call(
        halve_cols, [((256, half), BF16), ((256, half), F32)], [coupling]
    )
    mid_keep, mid_send = kernel_call(
        halve_rows, [((half, 256), BF16), ((half, 256), F32)], [winv_mid]
    )
    top_w, top_t = kernel_call(
        join_cols,
        [((half, 256), BF16), ((256, half), BF16)],
        [top_keep, swap_core(top_send)],
    )
    (cou_w,) = kernel_call(
        join_rows, [((512, half), BF16)], [cou_keep, swap_core(cou_send)]
    )

    mid_w, mid_t = kernel_call(
        join_cols,
        [((half, 512), BF16), ((512, half), BF16)],
        [mid_keep, swap_core(mid_send)],
    )

    chains = range(CHAINS)
    values = []
    for h in chains:
        parts = run_forward(top_w, [load[h], load_other[h]], True, h, after=mids)
        values.append(plane_sum(*parts, h)[0])
    keep, send = kernel_call(
        mid_load_kernel,
        [((CHAINS, 4, WIDE, 128), F32)] * 2,
        [*mids, sol_all],
        [pltpu.VMEM((128, 1024), BF16)],
        flops=2 * 128 * 1024 * 128,
    )
    keep, send = glue(
        lambda k, g: ((k + g)[:, :2], (k + g)[:, 2:]), keep, swap_second(send)
    )
    mid_load = keep + swap_near(send)
    mid_other = swap_core(mid_load)
    top_parts, adjoint = [], []
    for h in chains:
        mine, theirs = run_backward(
            top_t,
            *plane_spread(depth_total(values[h], True), h),
            True,
            h,
            True,
            after=[cou_w, mid_w],
        )
        top_parts.append((mine, swap_core(theirs)))
        adjoint.append(mine + top_parts[h][1])
    top_out = unpack(*top_parts)

    mid_parts = []
    for h in chains:
        (both,) = run_backward(
            cou_w, *plane_spread(depth_spread(adjoint[h]), h), True, h, False
        )
        vec = [mid_load[h], mid_other[h], both, swap_core(both)]
        parts = run_forward(mid_w, vec, False, h, after=[top_out] if h else ())
        line = depth_total(plane_sum(*parts, h)[0], False)
        mine, theirs = run_backward(mid_t, *plane_spread(line, h), False, h, True)
        mid_parts.append((mine, swap_core(theirs)))
    return top_out, unpack(*mid_parts)


def solution(mesh):
    placed = (
        P("leaf", "panel", None),
        P("leaf", "panel", None),
        P(None, AXES),
        P(None, AXES),
        P(AXES, None),
    )
    fits = mesh.shape["leaf"] == 8 and mesh.shape["panel"] == 4
    return jax.shard_map(
        fast_body if fits else plain_body,
        mesh=mesh,
        in_specs=placed,
        out_specs=(P(AXES, None), P(AXES, None)),
        check_vma=False,
    )
```

```python
import functools

import jax
import jax.numpy as jnp
from jax import lax
from jax.experimental import pallas as pl
from jax.experimental.pallas import tpu as pltpu
from jax.sharding import PartitionSpec as P

AXES = ("leaf", "panel")
F32 = jnp.float32
BF16 = jnp.bfloat16
LANES = 128


def plain_body(border, solution, winv_top, winv_mid, coupling):
    leaves = lax.axis_size("leaf")
    panels = lax.axis_size("panel")
    half = leaves // 2
    leaf_id = lax.axis_index("leaf")
    front = winv_top.shape[0]
    top_cols = winv_top.shape[1]
    mid_cols = winv_mid.shape[1]
    contribution = lax.dot_general(
        border[0], solution[0], (((0,), (0,)), ((), ())), preferred_element_type=F32
    )
    groups = [list(range(half)), list(range(half, leaves))]
    device = leaf_id * panels + lax.axis_index("panel")
    in_half = device % (half * panels)
    top_load = lax.psum(contribution[:front], AXES)
    top_block = lax.dynamic_slice_in_dim(top_load, device * top_cols, top_cols, 0)
    mid_load = lax.psum(contribution[front:], "panel")
    mid_load = lax.psum(mid_load, "leaf", axis_index_groups=groups)
    mid_block = lax.dynamic_slice_in_dim(mid_load, in_half * mid_cols, mid_cols, 0)
    top_factor = winv_top.astype(F32)
    mid_factor = winv_mid.astype(F32)
    exact = lax.Precision.HIGHEST
    top_inner = lax.psum(jnp.dot(top_factor, top_block, precision=exact), AXES)
    top_adjoint = jnp.dot(top_factor.T, top_inner, precision=exact)
    top_whole = lax.all_gather(top_adjoint, AXES, axis=0, tiled=True)
    mid_rhs = mid_block - jnp.dot(coupling.astype(F32), top_whole, precision=exact)
    mid_inner = lax.psum(jnp.dot(mid_factor, mid_rhs, precision=exact), "panel")
    mid_inner = lax.psum(mid_inner, "leaf", axis_index_groups=groups)
    mid_adjoint = jnp.dot(mid_factor.T, mid_inner, precision=exact)
    return top_adjoint, mid_adjoint


CHAINS = 2
WIDE = 64


def permute(value, partner):
    return lax.ppermute(value, AXES, [(i, partner(i)) for i in range(32)])


def swap_core(value):
    return permute(value, lambda i: i ^ 1)


def swap_first(value, chain=0):
    return permute(value, lambda i: i ^ (4 if (i ^ chain) & 1 else 2))


def swap_second(value, chain=0):
    return permute(value, lambda i: i ^ (2 if (i ^ chain) & 1 else 4))


def swap_cross(value):
    return permute(value, lambda i: i ^ (3 if i & 1 else 5))


def swap_near(value):
    return permute(value, lambda i: i ^ 8)


def swap_far(value):
    return permute(value, lambda i: i ^ 16)


def coords():
    leaf = lax.axis_index("leaf")
    panel = lax.axis_index("panel")
    return leaf // 2, leaf % 2, panel // 2, panel % 2


def flip(a, k):
    return a + k - 2 * a * k


def z_flip(z, k):
    return flip(z // 2, k // 2) * 2 + flip(z % 2, k % 2)


Z_ORDER = (0, 2, 1, 3)


def plane_at(y, x, c, first, second):
    along_x = first * (1 - c) + second * c
    along_y = first * c + second * (1 - c)
    return flip(y, along_y) * 2 + flip(x, along_x)


def block_starts(deep, chain):
    z, y, x, c = coords()
    c = flip(c, chain)
    starts = []
    for first in range(2):
        for second in range(2):
            plane = plane_at(y, x, c, first, second)
            for j in range(4):
                if deep:
                    start = (z_flip(z, Z_ORDER[j]) * 4 + plane) * 128
                else:
                    start = (flip(z % 2, j // 2) * 4 + plane) * 256 + j % 2 * 128
                starts.append(pl.multiple_of(start, 128))
    return starts


def kernel_call(kernel, outs, ins, scratch=(), flops=0, limit=10, after=()):
    vmem = pl.BlockSpec(memory_space=pltpu.VMEM)
    size = lambda s: s.size * s.dtype.itemsize

    def ordered(*refs):
        kernel(*refs[: len(ins)], *refs[len(ins) + len(after) :])

    return pl.pallas_call(
        ordered,
        out_shape=[jax.ShapeDtypeStruct(*o) for o in outs],
        in_specs=[vmem] * len(ins) + [pl.BlockSpec(memory_space=pl.ANY)] * len(after),
        out_specs=[vmem] * len(outs),
        scratch_shapes=list(scratch),
        compiler_params=pltpu.CompilerParams(vmem_limit_bytes=limit * 2**20),
        cost_estimate=pl.CostEstimate(
            flops=flops,
            transcendentals=0,
            bytes_accessed=sum(map(size, ins))
            + sum(size(jax.ShapeDtypeStruct(*o)) for o in outs),
        ),
    )(*ins, *after)


def glue(fn, *ins, after=()):
    shapes = jax.eval_shape(fn, *ins)

    def kernel(*refs):
        values = fn(*[r[...] for r in refs[: len(ins)]])
        for ref, value in zip(refs[len(ins) :], values):
            ref[...] = value

    return kernel_call(kernel, [(o.shape, o.dtype) for o in shapes], ins, after=after)


def left_lanes(shape):
    return lax.broadcasted_iota(jnp.int32, shape, 1) < WIDE


def pack(low, high):
    left = left_lanes(low.shape)
    return (
        jnp.where(left, low, pltpu.roll(high, WIDE, 1)),
        jnp.where(left, pltpu.roll(low, WIDE, 1), high),
    )


def put_split(rhs_ref, start, block):
    left = left_lanes(block.shape)
    turned = pltpu.roll(block, WIDE, 1)
    for i, rows in enumerate((jnp.where(left, block, turned), jnp.where(left, turned, block))):
        high = rows.astype(BF16).astype(F32)
        both = jnp.where(left, high, rows - high)
        rhs_ref[pl.ds(start + i * WIDE, WIDE), :] = both.astype(BF16)


def product(w_ref, rhs_ref):
    both = jnp.dot(w_ref[...], rhs_ref[...], preferred_element_type=F32)
    return both + pltpu.roll(both, WIDE, 1)


def take_block(total, start):
    low = total[start : start + WIDE]
    high = total[start + WIDE : start + 2 * WIDE]
    return jnp.where(left_lanes(low.shape), low, high)


def prep_top(border_ref, sol_ref, *tops):
    z, y, x, c = coords()
    sol = sol_ref[...].astype(F32)
    for rel in range(4):
        core = flip(c, rel % 2)
        for second in range(2):
            plane = plane_at(y, x, core, rel // 2, second)
            for j in range(4):
                col = pl.multiple_of((z_flip(z, Z_ORDER[j]) * 8 + plane * 2 + core) * 128, 128)
                here = (second * 4 + j) * 128
                tops[rel][:, here : here + 128] = border_ref[:, pl.ds(col, 128)].astype(F32)
        tops[rel][:, 1024:] = sol


def prep_mid(border_ref, *mids):
    z, y, x, c = coords()
    front = border_ref.shape[1] // 2
    for rel in range(4):
        core = flip(c, rel % 2)
        for second in range(2):
            plane = plane_at(y, x, core, rel // 2, second)
            for k in range(2):
                col = front + (flip(z % 2, k) * 8 + plane * 2 + core) * 256
                here = (second * 2 + k) * 256
                mids[rel][:, here : here + 256] = border_ref[
                    :, pl.ds(pl.multiple_of(col, 256), 256)
                ].astype(F32)


def stack_rows(refs, cols, out_ref):
    n = refs[0].shape[0]
    for i, ref in enumerate(refs):
        out_ref[i * n : (i + 1) * n, :] = ref[:, cols].astype(BF16)


def put_loads(sol, rows, outs):
    total = lax.dot_general(
        sol, rows, (((0,), (0,)), ((), ())), preferred_element_type=F32
    )
    for second in range(2):
        for j in range(4):
            here = (second * 4 + j) * 128
            block = total[:, here : here + 128].T
            packed = pack(block[:WIDE], block[WIDE:])
            for h in range(CHAINS):
                outs[h][second][j] = packed[h]


def top_load_kernel(*refs):
    ins, (keep_ref, send_ref, sol_ref, rows_ref) = refs[:4], refs[4:]
    stack_rows(ins, slice(0, 1024), rows_ref)
    stack_rows(ins, slice(1024, 1152), sol_ref)
    outs = [[keep_ref.at[h], send_ref.at[h]] for h in range(CHAINS)]
    put_loads(sol_ref[...], rows_ref[...], outs)


def mid_load_kernel(*refs):
    ins, sol_ref, keep_ref, send_ref, rows_ref = refs[:4], *refs[4:]
    stack_rows(ins, slice(0, 1024), rows_ref)
    outs = [[keep_ref.at[h], send_ref.at[h]] for h in range(CHAINS)]
    put_loads(sol_ref[...], rows_ref[...], outs)


def halve_rows(w_ref, keep_ref, send_ref):
    z, y, x, c = coords()
    rows = w_ref.shape[0] // 2
    keep_ref[...] = w_ref[pl.ds(pl.multiple_of(c * rows, rows), rows), :]
    send_ref[...] = w_ref[pl.ds(pl.multiple_of((1 - c) * rows, rows), rows), :].astype(F32)


def halve_cols(w_ref, keep_ref, send_ref):
    z, y, x, c = coords()
    for i in range(w_ref.shape[1] // 256):
        here = slice(i * 128, (i + 1) * 128)
        kept = pl.multiple_of(i * 256 + c * 128, 128)
        sent = pl.multiple_of(i * 256 + (1 - c) * 128, 128)
        keep_ref[:, here] = w_ref[:, pl.ds(kept, 128)]
        send_ref[:, here] = w_ref[:, pl.ds(sent, 128)].astype(F32)


def join_cols(keep_ref, recv_ref, w_ref, t_ref):
    n = keep_ref.shape[1]
    w_ref[:, :n] = keep_ref[...]
    w_ref[:, n:] = recv_ref[...].astype(BF16)
    t_ref[:n, :] = keep_ref[...].T
    t_ref[n:, :] = recv_ref[...].astype(BF16).T


def join_rows(keep_ref, recv_ref, w_ref):
    n = keep_ref.shape[0]
    w_ref[:n, :] = keep_ref[...]
    w_ref[n:, :] = recv_ref[...].astype(BF16)


def forward(deep, chain, w_ref, *refs):
    vec, (send_ref, next_ref, keep_ref), (rhs_ref, sum_ref) = refs[:-5], refs[-5:-2], refs[-2:]
    blocks = vec[0].shape[0]
    if len(vec) == 2:
        own, other = vec[0][...], vec[1][...]
    else:
        mine, theirs, part, recv = [v[...] for v in vec]
        own = mine - part[:blocks] - recv[blocks:]
        other = theirs - part[blocks:] - recv[:blocks]
    for i in range(blocks):
        put_split(rhs_ref, i * 128, own[i])
        put_split(rhs_ref, (blocks + i) * 128, other[i])
    sum_ref[...] = product(w_ref, rhs_ref)
    left = left_lanes((WIDE, 2 * WIDE))
    for i, start in enumerate(block_starts(deep, chain)):
        low = sum_ref[pl.ds(start, WIDE), :]
        high = sum_ref[pl.ds(start + WIDE, WIDE), :]
        block = jnp.where(left, low, high)
        if i < 4:
            keep_ref[i] = block
        elif i < 8:
            next_ref[i - 4] = block
        else:
            send_ref[i - 8] = block


def backward(deep, chain, w_ref, near_ref, far_ref, *refs):
    outs, rhs_ref = refs[:-1], refs[-1]
    for i, start in enumerate(block_starts(deep, chain)):
        put_split(rhs_ref, start, near_ref[i] if i < 8 else far_ref[i - 8])
    total = product(w_ref, rhs_ref)
    blocks = w_ref.shape[0] // 128
    for i in range(blocks):
        if len(outs) == 1:
            outs[0][i] = take_block(total, i * 128)
        else:
            outs[2 * i // blocks][i % (blocks // 2)] = take_block(total, i * 128)


def run_forward(w, vec, deep, chain, after=()):
    m, k = w.shape
    return kernel_call(
        functools.partial(forward, deep, chain),
        [((8, WIDE, 128), F32), ((4, WIDE, 128), F32), ((4, WIDE, 128), F32)],
        [w, *vec],
        [pltpu.VMEM((k, 128), BF16), pltpu.VMEM((m, 128), F32)],
        flops=2 * m * k * 128,
        after=after,
    )


def run_backward(w, near, far, deep, chain, apart, after=()):
    m, k = w.shape
    return kernel_call(
        functools.partial(backward, deep, chain),
        [((m // 256, WIDE, 128), F32)] * 2 if apart else [((m // 128, WIDE, 128), F32)],
        [w, near, far],
        [pltpu.VMEM((k, 128), BF16)],
        flops=2 * m * k * 128,
        after=after,
    )


def depth_sum(value, after):
    value = value[:, :2] + swap_near(value[:, 2:])
    got = swap_far(value[:, 1:])
    return glue(lambda v, g: (v[:, :1] + g,), value, got, after=after)[0]


def plane_sum(send, follow, keep, chain):
    first = swap_first(send, chain)
    second = swap_second(follow + first[4:], chain)
    return keep + first[:4] + second, second


def depth_total(value, deep):
    if not deep:
        return value + swap_near(jnp.concatenate([value[2:], value[:2]], 0))
    keep = value[:2] + swap_near(value[2:])
    keep = keep + swap_far(jnp.concatenate([keep[1:], keep[:1]], 0))
    return jnp.concatenate([keep, swap_near(keep)], 0)


def depth_spread(own):
    pair = jnp.concatenate([own, swap_far(own)], 0)
    return jnp.concatenate([pair, swap_near(pair)], 0)


def plane_spread(line, chain):
    near = jnp.concatenate([line, swap_second(line, chain)], 0)
    return near, swap_first(near, chain)


def unpack_kernel(mine0, recv0, mine1, recv1, out_ref):
    left = left_lanes((WIDE, 128))
    for i in range(mine0.shape[0]):
        p0 = mine0[i] + recv0[i]
        p1 = mine1[i] + recv1[i]
        out_ref[i * 128 : i * 128 + WIDE, :] = jnp.where(left, p0, pltpu.roll(p1, WIDE, 1))
        out_ref[i * 128 + WIDE : (i + 1) * 128, :] = jnp.where(left, pltpu.roll(p0, WIDE, 1), p1)


def unpack(*pairs):
    ins = [array for pair in pairs for array in pair]
    return kernel_call(unpack_kernel, [((ins[0].shape[0] * 128, 128), F32)], ins)[0]


def fast_body(border, solution, winv_top, winv_mid, coupling):
    front = winv_top.shape[0]
    half = front // 2
    tops = ready = kernel_call(
        prep_top, [((32, 1152), F32)] * 4, [border[0], solution[0]]
    )
    tops = [tops[0], swap_core(tops[1]), swap_first(tops[2]), swap_cross(tops[3])]
    keep, send, sol_all = kernel_call(
        top_load_kernel,
        [((CHAINS, 4, WIDE, 128), F32)] * 2 + [((128, 128), BF16)],
        tops,
        [pltpu.VMEM((128, 1024), BF16)],
        flops=2 * 128 * 1024 * 128,
    )
    got = swap_second(send)
    mids = kernel_call(prep_mid, [((32, 1024), F32)] * 4, [border[0]], after=[got])
    mids = [mids[0], swap_core(mids[1]), swap_first(mids[2]), swap_cross(mids[3])]
    load = depth_sum(keep + got, mids)
    load_other = swap_core(load)

    top_keep, top_send = kernel_call(
        halve_rows, [((half, 128), BF16), ((half, 128), F32)], [winv_top], after=ready[:1]
    )
    cou_keep, cou_send = kernel_call(
        halve_cols, [((256, half), BF16), ((256, half), F32)], [coupling]
    )
    mid_keep, mid_send = kernel_call(
        halve_rows, [((half, 256), BF16), ((half, 256), F32)], [winv_mid]
    )
    top_w, top_t = kernel_call(
        join_cols,
        [((half, 256), BF16), ((256, half), BF16)],
        [top_keep, swap_core(top_send)],
    )
    (cou_w,) = kernel_call(
        join_rows, [((512, half), BF16)], [cou_keep, swap_core(cou_send)]
    )

    mid_w, mid_t = kernel_call(
        join_cols,
        [((half, 512), BF16), ((512, half), BF16)],
        [mid_keep, swap_core(mid_send)],
    )

    chains = range(CHAINS)
    values = []
    for h in chains:
        parts = run_forward(top_w, [load[h], load_other[h]], True, h)
        values.append(plane_sum(*parts, h)[0])
    keep, send = kernel_call(
        mid_load_kernel,
        [((CHAINS, 4, WIDE, 128), F32)] * 2,
        [*mids, sol_all],
        [pltpu.VMEM((128, 1024), BF16)],
        flops=2 * 128 * 1024 * 128,
    )
    keep, send = glue(
        lambda k, g: ((k + g)[:, :2], (k + g)[:, 2:]), keep, swap_second(send)
    )
    mid_load = keep + swap_near(send)
    mid_other = swap_core(mid_load)
    top_parts, adjoint = [], []
    for h in chains:
        mine, theirs = run_backward(
            top_t,
            *plane_spread(depth_total(values[h], True), h),
            True,
            h,
            True,
            after=[cou_w, mid_w],
        )
        top_parts.append((mine, swap_core(theirs)))
        adjoint.append(mine + top_parts[h][1])
    top_out = unpack(*top_parts)

    mid_parts = []
    for h in chains:
        (both,) = run_backward(
            cou_w, *plane_spread(depth_spread(adjoint[h]), h), True, h, False
        )
        vec = [mid_load[h], mid_other[h], both, swap_core(both)]
        parts = run_forward(mid_w, vec, False, h, after=[top_out] if h else ())
        line = depth_total(plane_sum(*parts, h)[0], False)
        mine, theirs = run_backward(mid_t, *plane_spread(line, h), False, h, True)
        mid_parts.append((mine, swap_core(theirs)))
    return top_out, unpack(*mid_parts)


def solution(mesh):
    placed = (
        P("leaf", "panel", None),
        P("leaf", "panel", None),
        P(None, AXES),
        P(None, AXES),
        P(AXES, None),
    )
    fits = mesh.shape["leaf"] == 8 and mesh.shape["panel"] == 4
    return jax.shard_map(
        fast_body if fits else plain_body,
        mesh=mesh,
        in_specs=placed,
        out_specs=(P(AXES, None), P(AXES, None)),
        check_vma=False,
    )
```

```python
import functools

import jax
import jax.numpy as jnp
from jax import lax
from jax.experimental import pallas as pl
from jax.experimental.pallas import tpu as pltpu
from jax.sharding import PartitionSpec as P

AXES = ("leaf", "panel")
F32 = jnp.float32
BF16 = jnp.bfloat16
LANES = 128


def plain_body(border, solution, winv_top, winv_mid, coupling):
    leaves = lax.axis_size("leaf")
    panels = lax.axis_size("panel")
    half = leaves // 2
    leaf_id = lax.axis_index("leaf")
    front = winv_top.shape[0]
    top_cols = winv_top.shape[1]
    mid_cols = winv_mid.shape[1]
    contribution = lax.dot_general(
        border[0], solution[0], (((0,), (0,)), ((), ())), preferred_element_type=F32
    )
    groups = [list(range(half)), list(range(half, leaves))]
    device = leaf_id * panels + lax.axis_index("panel")
    in_half = device % (half * panels)
    top_load = lax.psum(contribution[:front], AXES)
    top_block = lax.dynamic_slice_in_dim(top_load, device * top_cols, top_cols, 0)
    mid_load = lax.psum(contribution[front:], "panel")
    mid_load = lax.psum(mid_load, "leaf", axis_index_groups=groups)
    mid_block = lax.dynamic_slice_in_dim(mid_load, in_half * mid_cols, mid_cols, 0)
    top_factor = winv_top.astype(F32)
    mid_factor = winv_mid.astype(F32)
    exact = lax.Precision.HIGHEST
    top_inner = lax.psum(jnp.dot(top_factor, top_block, precision=exact), AXES)
    top_adjoint = jnp.dot(top_factor.T, top_inner, precision=exact)
    top_whole = lax.all_gather(top_adjoint, AXES, axis=0, tiled=True)
    mid_rhs = mid_block - jnp.dot(coupling.astype(F32), top_whole, precision=exact)
    mid_inner = lax.psum(jnp.dot(mid_factor, mid_rhs, precision=exact), "panel")
    mid_inner = lax.psum(mid_inner, "leaf", axis_index_groups=groups)
    mid_adjoint = jnp.dot(mid_factor.T, mid_inner, precision=exact)
    return top_adjoint, mid_adjoint


CHAINS = 2
WIDE = 64


def permute(value, partner):
    return lax.ppermute(value, AXES, [(i, partner(i)) for i in range(32)])


def swap_core(value):
    return permute(value, lambda i: i ^ 1)


def swap_first(value, chain=0):
    return permute(value, lambda i: i ^ (4 if (i ^ chain) & 1 else 2))


def swap_second(value, chain=0):
    return permute(value, lambda i: i ^ (2 if (i ^ chain) & 1 else 4))


def swap_cross(value):
    return permute(value, lambda i: i ^ (3 if i & 1 else 5))


def swap_near(value):
    return permute(value, lambda i: i ^ 8)


def swap_far(value):
    return permute(value, lambda i: i ^ 16)


def coords():
    leaf = lax.axis_index("leaf")
    panel = lax.axis_index("panel")
    return leaf // 2, leaf % 2, panel // 2, panel % 2


def flip(a, k):
    return a + k - 2 * a * k


def z_flip(z, k):
    return flip(z // 2, k // 2) * 2 + flip(z % 2, k % 2)


Z_ORDER = (0, 2, 1, 3)


def plane_at(y, x, c, first, second):
    along_x = first * (1 - c) + second * c
    along_y = first * c + second * (1 - c)
    return flip(y, along_y) * 2 + flip(x, along_x)


def block_starts(deep, chain):
    z, y, x, c = coords()
    c = flip(c, chain)
    starts = []
    for first in range(2):
        for second in range(2):
            plane = plane_at(y, x, c, first, second)
            for j in range(4):
                if deep:
                    start = (z_flip(z, Z_ORDER[j]) * 4 + plane) * 128
                else:
                    start = (flip(z % 2, j // 2) * 4 + plane) * 256 + j % 2 * 128
                starts.append(pl.multiple_of(start, 128))
    return starts


def kernel_call(kernel, outs, ins, scratch=(), flops=0, limit=10, after=()):
    vmem = pl.BlockSpec(memory_space=pltpu.VMEM)
    size = lambda s: s.size * s.dtype.itemsize

    def ordered(*refs):
        kernel(*refs[: len(ins)], *refs[len(ins) + len(after) :])

    return pl.pallas_call(
        ordered,
        out_shape=[jax.ShapeDtypeStruct(*o) for o in outs],
        in_specs=[vmem] * len(ins) + [pl.BlockSpec(memory_space=pl.ANY)] * len(after),
        out_specs=[vmem] * len(outs),
        scratch_shapes=list(scratch),
        compiler_params=pltpu.CompilerParams(vmem_limit_bytes=limit * 2**20),
        cost_estimate=pl.CostEstimate(
            flops=flops,
            transcendentals=0,
            bytes_accessed=sum(map(size, ins))
            + sum(size(jax.ShapeDtypeStruct(*o)) for o in outs),
        ),
    )(*ins, *after)


def glue(fn, *ins, after=()):
    shapes = jax.eval_shape(fn, *ins)

    def kernel(*refs):
        values = fn(*[r[...] for r in refs[: len(ins)]])
        for ref, value in zip(refs[len(ins) :], values):
            ref[...] = value

    return kernel_call(kernel, [(o.shape, o.dtype) for o in shapes], ins, after=after)


def left_lanes(shape):
    return lax.broadcasted_iota(jnp.int32, shape, 1) < WIDE


def pack(low, high):
    left = left_lanes(low.shape)
    return (
        jnp.where(left, low, pltpu.roll(high, WIDE, 1)),
        jnp.where(left, pltpu.roll(low, WIDE, 1), high),
    )


def put_split(rhs_ref, start, block):
    left = left_lanes(block.shape)
    turned = pltpu.roll(block, WIDE, 1)
    for i, rows in enumerate((jnp.where(left, block, turned), jnp.where(left, turned, block))):
        high = rows.astype(BF16).astype(F32)
        both = jnp.where(left, high, rows - high)
        rhs_ref[pl.ds(start + i * WIDE, WIDE), :] = both.astype(BF16)


def product(w_ref, rhs_ref):
    both = jnp.dot(w_ref[...], rhs_ref[...], preferred_element_type=F32)
    return both + pltpu.roll(both, WIDE, 1)


def take_block(total, start):
    low = total[start : start + WIDE]
    high = total[start + WIDE : start + 2 * WIDE]
    return jnp.where(left_lanes(low.shape), low, high)


def prep_top(border_ref, sol_ref, *tops):
    z, y, x, c = coords()
    sol = sol_ref[...].astype(F32)
    for rel in range(4):
        core = flip(c, rel % 2)
        for second in range(2):
            plane = plane_at(y, x, core, rel // 2, second)
            for j in range(4):
                col = pl.multiple_of((z_flip(z, Z_ORDER[j]) * 8 + plane * 2 + core) * 128, 128)
                here = (second * 4 + j) * 128
                tops[rel][:, here : here + 128] = border_ref[:, pl.ds(col, 128)].astype(F32)
        tops[rel][:, 1024:] = sol


def prep_mid(border_ref, *mids):
    z, y, x, c = coords()
    front = border_ref.shape[1] // 2
    for rel in range(4):
        core = flip(c, rel % 2)
        for second in range(2):
            plane = plane_at(y, x, core, rel // 2, second)
            for k in range(2):
                col = front + (flip(z % 2, k) * 8 + plane * 2 + core) * 256
                here = (second * 2 + k) * 256
                mids[rel][:, here : here + 256] = border_ref[
                    :, pl.ds(pl.multiple_of(col, 256), 256)
                ].astype(F32)


def stack_rows(refs, cols, out_ref):
    n = refs[0].shape[0]
    for i, ref in enumerate(refs):
        out_ref[i * n : (i + 1) * n, :] = ref[:, cols].astype(BF16)


def put_loads(sol, rows, outs):
    total = lax.dot_general(
        sol, rows, (((0,), (0,)), ((), ())), preferred_element_type=F32
    )
    for second in range(2):
        for j in range(4):
            here = (second * 4 + j) * 128
            block = total[:, here : here + 128].T
            packed = pack(block[:WIDE], block[WIDE:])
            for h in range(CHAINS):
                outs[h][second][j] = packed[h]


def top_load_kernel(*refs):
    ins, (keep_ref, send_ref, sol_ref, rows_ref) = refs[:4], refs[4:]
    stack_rows(ins, slice(0, 1024), rows_ref)
    stack_rows(ins, slice(1024, 1152), sol_ref)
    outs = [[keep_ref.at[h], send_ref.at[h]] for h in range(CHAINS)]
    put_loads(sol_ref[...], rows_ref[...], outs)


def mid_load_kernel(*refs):
    ins, sol_ref, keep_ref, send_ref, rows_ref = refs[:4], *refs[4:]
    stack_rows(ins, slice(0, 1024), rows_ref)
    outs = [[keep_ref.at[h], send_ref.at[h]] for h in range(CHAINS)]
    put_loads(sol_ref[...], rows_ref[...], outs)


def halve_rows(w_ref, keep_ref, send_ref):
    z, y, x, c = coords()
    rows = w_ref.shape[0] // 2
    keep_ref[...] = w_ref[pl.ds(pl.multiple_of(c * rows, rows), rows), :]
    send_ref[...] = w_ref[pl.ds(pl.multiple_of((1 - c) * rows, rows), rows), :].astype(F32)


def halve_cols(w_ref, keep_ref, send_ref):
    z, y, x, c = coords()
    for i in range(w_ref.shape[1] // 256):
        here = slice(i * 128, (i + 1) * 128)
        kept = pl.multiple_of(i * 256 + c * 128, 128)
        sent = pl.multiple_of(i * 256 + (1 - c) * 128, 128)
        keep_ref[:, here] = w_ref[:, pl.ds(kept, 128)]
        send_ref[:, here] = w_ref[:, pl.ds(sent, 128)].astype(F32)


def join_cols(keep_ref, recv_ref, w_ref, t_ref):
    n = keep_ref.shape[1]
    w_ref[:, :n] = keep_ref[...]
    w_ref[:, n:] = recv_ref[...].astype(BF16)
    t_ref[:n, :] = keep_ref[...].T
    t_ref[n:, :] = recv_ref[...].astype(BF16).T


def join_rows(keep_ref, recv_ref, w_ref):
    n = keep_ref.shape[0]
    w_ref[:n, :] = keep_ref[...]
    w_ref[n:, :] = recv_ref[...].astype(BF16)


def forward(deep, chain, w_ref, *refs):
    vec, (send_ref, next_ref, keep_ref), (rhs_ref, sum_ref) = refs[:-5], refs[-5:-2], refs[-2:]
    blocks = vec[0].shape[0]
    if len(vec) == 2:
        own, other = vec[0][...], vec[1][...]
    else:
        mine, theirs, part, recv = [v[...] for v in vec]
        own = mine - part[:blocks] - recv[blocks:]
        other = theirs - part[blocks:] - recv[:blocks]
    for i in range(blocks):
        put_split(rhs_ref, i * 128, own[i])
        put_split(rhs_ref, (blocks + i) * 128, other[i])
    sum_ref[...] = product(w_ref, rhs_ref)
    left = left_lanes((WIDE, 2 * WIDE))
    for i, start in enumerate(block_starts(deep, chain)):
        low = sum_ref[pl.ds(start, WIDE), :]
        high = sum_ref[pl.ds(start + WIDE, WIDE), :]
        block = jnp.where(left, low, high)
        if i < 4:
            keep_ref[i] = block
        elif i < 8:
            next_ref[i - 4] = block
        else:
            send_ref[i - 8] = block


def backward(deep, chain, w_ref, *refs):
    pieces, outs, rhs_ref = refs[:4], refs[4:-1], refs[-1]
    for i, start in enumerate(block_starts(deep, chain)):
        put_split(rhs_ref, start, pieces[i // 4][i % 4])
    total = product(w_ref, rhs_ref)
    blocks = w_ref.shape[0] // 128
    for i in range(blocks):
        if len(outs) == 1:
            outs[0][i] = take_block(total, i * 128)
        else:
            outs[2 * i // blocks][i % (blocks // 2)] = take_block(total, i * 128)


def run_forward(w, vec, deep, chain, after=()):
    m, k = w.shape
    return kernel_call(
        functools.partial(forward, deep, chain),
        [((8, WIDE, 128), F32), ((4, WIDE, 128), F32), ((4, WIDE, 128), F32)],
        [w, *vec],
        [pltpu.VMEM((k, 128), BF16), pltpu.VMEM((m, 128), F32)],
        flops=2 * m * k * 128,
        after=after,
    )


def run_backward(w, pieces, deep, chain, apart, after=()):
    m, k = w.shape
    return kernel_call(
        functools.partial(backward, deep, chain),
        [((m // 256, WIDE, 128), F32)] * 2 if apart else [((m // 128, WIDE, 128), F32)],
        [w, *pieces],
        [pltpu.VMEM((k, 128), BF16)],
        flops=2 * m * k * 128,
        after=after,
    )


def depth_sum(value, after):
    value = value[:, :2] + swap_near(value[:, 2:])
    got = swap_far(value[:, 1:])
    return glue(lambda v, g: (v[:, :1] + g,), value, got, after=after)[0]


def plane_sum(send, follow, keep, chain):
    first = swap_first(send, chain)
    second = swap_second(follow + first[4:], chain)
    return keep + first[:4] + second, second


def depth_total(value, deep):
    if not deep:
        return value + swap_near(jnp.concatenate([value[2:], value[:2]], 0))
    keep = value[:2] + swap_near(value[2:])
    keep = keep + swap_far(jnp.concatenate([keep[1:], keep[:1]], 0))
    return jnp.concatenate([keep, swap_near(keep)], 0)


def depth_spread(own):
    pair = jnp.concatenate([own, swap_far(own)], 0)
    return jnp.concatenate([pair, swap_near(pair)], 0)


def plane_spread(line, chain):
    second = swap_second(line, chain)
    return line, second, swap_first(line, chain), swap_first(second, chain)


def unpack_kernel(mine0, recv0, mine1, recv1, out_ref):
    left = left_lanes((WIDE, 128))
    for i in range(mine0.shape[0]):
        p0 = mine0[i] + recv0[i]
        p1 = mine1[i] + recv1[i]
        out_ref[i * 128 : i * 128 + WIDE, :] = jnp.where(left, p0, pltpu.roll(p1, WIDE, 1))
        out_ref[i * 128 + WIDE : (i + 1) * 128, :] = jnp.where(left, pltpu.roll(p0, WIDE, 1), p1)


def unpack(*pairs):
    ins = [array for pair in pairs for array in pair]
    return kernel_call(unpack_kernel, [((ins[0].shape[0] * 128, 128), F32)], ins)[0]


def fast_body(border, solution, winv_top, winv_mid, coupling):
    front = winv_top.shape[0]
    half = front // 2
    tops = ready = kernel_call(
        prep_top, [((32, 1152), F32)] * 4, [border[0], solution[0]]
    )
    tops = [tops[0], swap_core(tops[1]), swap_first(tops[2]), swap_cross(tops[3])]
    keep, send, sol_all = kernel_call(
        top_load_kernel,
        [((CHAINS, 4, WIDE, 128), F32)] * 2 + [((128, 128), BF16)],
        tops,
        [pltpu.VMEM((128, 1024), BF16)],
        flops=2 * 128 * 1024 * 128,
    )
    got = swap_second(send)
    mids = kernel_call(prep_mid, [((32, 1024), F32)] * 4, [border[0]], after=[got])
    mids = [mids[0], swap_core(mids[1]), swap_first(mids[2]), swap_cross(mids[3])]
    load = depth_sum(keep + got, mids)
    load_other = swap_core(load)

    top_keep, top_send = kernel_call(
        halve_rows, [((half, 128), BF16), ((half, 128), F32)], [winv_top], after=ready[:1]
    )
    cou_keep, cou_send = kernel_call(
        halve_cols, [((256, half), BF16), ((256, half), F32)], [coupling]
    )
    mid_keep, mid_send = kernel_call(
        halve_rows, [((half, 256), BF16), ((half, 256), F32)], [winv_mid]
    )
    top_w, top_t = kernel_call(
        join_cols,
        [((half, 256), BF16), ((256, half), BF16)],
        [top_keep, swap_core(top_send)],
    )
    (cou_w,) = kernel_call(
        join_rows, [((512, half), BF16)], [cou_keep, swap_core(cou_send)]
    )

    mid_w, mid_t = kernel_call(
        join_cols,
        [((half, 512), BF16), ((512, half), BF16)],
        [mid_keep, swap_core(mid_send)],
    )

    chains = range(CHAINS)
    values = []
    for h in chains:
        parts = run_forward(top_w, [load[h], load_other[h]], True, h)
        values.append(plane_sum(*parts, h)[0])
    keep, send = kernel_call(
        mid_load_kernel,
        [((CHAINS, 4, WIDE, 128), F32)] * 2,
        [*mids, sol_all],
        [pltpu.VMEM((128, 1024), BF16)],
        flops=2 * 128 * 1024 * 128,
    )
    keep, send = glue(
        lambda k, g: ((k + g)[:, :2], (k + g)[:, 2:]), keep, swap_second(send)
    )
    mid_load = keep + swap_near(send)
    mid_other = swap_core(mid_load)
    top_parts, adjoint = [], []
    for h in chains:
        mine, theirs = run_backward(
            top_t,
            plane_spread(depth_total(values[h], True), h),
            True,
            h,
            True,
            after=[cou_w, mid_w],
        )
        top_parts.append((mine, swap_core(theirs)))
        adjoint.append(mine + top_parts[h][1])
    top_out = unpack(*top_parts)

    mid_parts = []
    for h in chains:
        (both,) = run_backward(
            cou_w, plane_spread(depth_spread(adjoint[h]), h), True, h, False
        )
        vec = [mid_load[h], mid_other[h], both, swap_core(both)]
        parts = run_forward(mid_w, vec, False, h, after=[top_out] if h else ())
        line = depth_total(plane_sum(*parts, h)[0], False)
        mine, theirs = run_backward(mid_t, plane_spread(line, h), False, h, True)
        mid_parts.append((mine, swap_core(theirs)))
    return top_out, unpack(*mid_parts)


def solution(mesh):
    placed = (
        P("leaf", "panel", None),
        P("leaf", "panel", None),
        P(None, AXES),
        P(None, AXES),
        P(AXES, None),
    )
    fits = mesh.shape["leaf"] == 8 and mesh.shape["panel"] == 4
    return jax.shard_map(
        fast_body if fits else plain_body,
        mesh=mesh,
        in_specs=placed,
        out_specs=(P(AXES, None), P(AXES, None)),
        check_vma=False,
    )
```

```python
import functools

import jax
import jax.numpy as jnp
from jax import lax
from jax.experimental import pallas as pl
from jax.experimental.pallas import tpu as pltpu
from jax.sharding import PartitionSpec as P

AXES = ("leaf", "panel")
F32 = jnp.float32
BF16 = jnp.bfloat16
LANES = 128


def plain_body(border, solution, winv_top, winv_mid, coupling):
    leaves = lax.axis_size("leaf")
    panels = lax.axis_size("panel")
    half = leaves // 2
    leaf_id = lax.axis_index("leaf")
    front = winv_top.shape[0]
    top_cols = winv_top.shape[1]
    mid_cols = winv_mid.shape[1]
    contribution = lax.dot_general(
        border[0], solution[0], (((0,), (0,)), ((), ())), preferred_element_type=F32
    )
    groups = [list(range(half)), list(range(half, leaves))]
    device = leaf_id * panels + lax.axis_index("panel")
    in_half = device % (half * panels)
    top_load = lax.psum(contribution[:front], AXES)
    top_block = lax.dynamic_slice_in_dim(top_load, device * top_cols, top_cols, 0)
    mid_load = lax.psum(contribution[front:], "panel")
    mid_load = lax.psum(mid_load, "leaf", axis_index_groups=groups)
    mid_block = lax.dynamic_slice_in_dim(mid_load, in_half * mid_cols, mid_cols, 0)
    top_factor = winv_top.astype(F32)
    mid_factor = winv_mid.astype(F32)
    exact = lax.Precision.HIGHEST
    top_inner = lax.psum(jnp.dot(top_factor, top_block, precision=exact), AXES)
    top_adjoint = jnp.dot(top_factor.T, top_inner, precision=exact)
    top_whole = lax.all_gather(top_adjoint, AXES, axis=0, tiled=True)
    mid_rhs = mid_block - jnp.dot(coupling.astype(F32), top_whole, precision=exact)
    mid_inner = lax.psum(jnp.dot(mid_factor, mid_rhs, precision=exact), "panel")
    mid_inner = lax.psum(mid_inner, "leaf", axis_index_groups=groups)
    mid_adjoint = jnp.dot(mid_factor.T, mid_inner, precision=exact)
    return top_adjoint, mid_adjoint


CHAINS = 2
WIDE = 64


def permute(value, partner):
    return lax.ppermute(value, AXES, [(i, partner(i)) for i in range(32)])


def swap_core(value):
    return permute(value, lambda i: i ^ 1)


def swap_first(value, chain=0):
    return permute(value, lambda i: i ^ (4 if (i ^ chain) & 1 else 2))


def swap_second(value, chain=0):
    return permute(value, lambda i: i ^ (2 if (i ^ chain) & 1 else 4))


def swap_cross(value):
    return permute(value, lambda i: i ^ (3 if i & 1 else 5))


def swap_near(value):
    return permute(value, lambda i: i ^ 8)


def swap_far(value):
    return permute(value, lambda i: i ^ 16)


def coords():
    leaf = lax.axis_index("leaf")
    panel = lax.axis_index("panel")
    return leaf // 2, leaf % 2, panel // 2, panel % 2


def flip(a, k):
    return a + k - 2 * a * k


def z_flip(z, k):
    return flip(z // 2, k // 2) * 2 + flip(z % 2, k % 2)


Z_ORDER = (0, 2, 1, 3)


def plane_at(y, x, c, first, second):
    along_x = first * (1 - c) + second * c
    along_y = first * c + second * (1 - c)
    return flip(y, along_y) * 2 + flip(x, along_x)


def block_starts(deep, chain):
    z, y, x, c = coords()
    c = flip(c, chain)
    starts = []
    for first in range(2):
        for second in range(2):
            plane = plane_at(y, x, c, first, second)
            for j in range(4):
                if deep:
                    start = (z_flip(z, Z_ORDER[j]) * 4 + plane) * 128
                else:
                    start = (flip(z % 2, j // 2) * 4 + plane) * 256 + j % 2 * 128
                starts.append(pl.multiple_of(start, 128))
    return starts


def kernel_call(kernel, outs, ins, scratch=(), flops=0, limit=10, after=()):
    vmem = pl.BlockSpec(memory_space=pltpu.VMEM)
    size = lambda s: s.size * s.dtype.itemsize

    def ordered(*refs):
        kernel(*refs[: len(ins)], *refs[len(ins) + len(after) :])

    return pl.pallas_call(
        ordered,
        out_shape=[jax.ShapeDtypeStruct(*o) for o in outs],
        in_specs=[vmem] * len(ins) + [pl.BlockSpec(memory_space=pl.ANY)] * len(after),
        out_specs=[vmem] * len(outs),
        scratch_shapes=list(scratch),
        compiler_params=pltpu.CompilerParams(vmem_limit_bytes=limit * 2**20),
        cost_estimate=pl.CostEstimate(
            flops=flops,
            transcendentals=0,
            bytes_accessed=sum(map(size, ins))
            + sum(size(jax.ShapeDtypeStruct(*o)) for o in outs),
        ),
    )(*ins, *after)


def glue(fn, *ins, after=()):
    shapes = jax.eval_shape(fn, *ins)

    def kernel(*refs):
        values = fn(*[r[...] for r in refs[: len(ins)]])
        for ref, value in zip(refs[len(ins) :], values):
            ref[...] = value

    return kernel_call(kernel, [(o.shape, o.dtype) for o in shapes], ins, after=after)


def left_lanes(shape):
    return lax.broadcasted_iota(jnp.int32, shape, 1) < WIDE


def pack(low, high):
    left = left_lanes(low.shape)
    return (
        jnp.where(left, low, pltpu.roll(high, WIDE, 1)),
        jnp.where(left, pltpu.roll(low, WIDE, 1), high),
    )


def put_split(rhs_ref, start, block):
    left = left_lanes(block.shape)
    turned = pltpu.roll(block, WIDE, 1)
    for i, rows in enumerate((jnp.where(left, block, turned), jnp.where(left, turned, block))):
        high = rows.astype(BF16).astype(F32)
        both = jnp.where(left, high, rows - high)
        rhs_ref[pl.ds(start + i * WIDE, WIDE), :] = both.astype(BF16)


def product(w_ref, rhs_ref):
    both = jnp.dot(w_ref[...], rhs_ref[...], preferred_element_type=F32)
    return both + pltpu.roll(both, WIDE, 1)


def take_block(total, start):
    low = total[start : start + WIDE]
    high = total[start + WIDE : start + 2 * WIDE]
    return jnp.where(left_lanes(low.shape), low, high)


def prep_top(border_ref, sol_ref, *tops):
    z, y, x, c = coords()
    sol = sol_ref[...].astype(F32)
    for rel in range(4):
        core = flip(c, rel % 2)
        for second in range(2):
            plane = plane_at(y, x, core, rel // 2, second)
            for j in range(4):
                col = pl.multiple_of((z_flip(z, Z_ORDER[j]) * 8 + plane * 2 + core) * 128, 128)
                here = (second * 4 + j) * 128
                tops[rel][:, here : here + 128] = border_ref[:, pl.ds(col, 128)].astype(F32)
        tops[rel][:, 1024:] = sol


def prep_mid(border_ref, *mids):
    z, y, x, c = coords()
    front = border_ref.shape[1] // 2
    for rel in range(4):
        core = flip(c, rel % 2)
        for second in range(2):
            plane = plane_at(y, x, core, rel // 2, second)
            for k in range(2):
                col = front + (flip(z % 2, k) * 8 + plane * 2 + core) * 256
                here = (second * 2 + k) * 256
                mids[rel][:, here : here + 256] = border_ref[
                    :, pl.ds(pl.multiple_of(col, 256), 256)
                ].astype(F32)


def stack_rows(refs, cols, out_ref):
    n = refs[0].shape[0]
    for i, ref in enumerate(refs):
        out_ref[i * n : (i + 1) * n, :] = ref[:, cols].astype(BF16)


def put_loads(sol, rows, outs):
    total = lax.dot_general(
        sol, rows, (((0,), (0,)), ((), ())), preferred_element_type=F32
    )
    for second in range(2):
        for j in range(4):
            here = (second * 4 + j) * 128
            block = total[:, here : here + 128].T
            packed = pack(block[:WIDE], block[WIDE:])
            for h in range(CHAINS):
                outs[h][second][j] = packed[h]


def top_load_kernel(*refs):
    ins, (keep_ref, send_ref, sol_ref, rows_ref) = refs[:4], refs[4:]
    stack_rows(ins, slice(0, 1024), rows_ref)
    stack_rows(ins, slice(1024, 1152), sol_ref)
    outs = [[keep_ref.at[h], send_ref.at[h]] for h in range(CHAINS)]
    put_loads(sol_ref[...], rows_ref[...], outs)


def mid_load_kernel(*refs):
    ins, sol_ref, keep_ref, send_ref, rows_ref = refs[:4], *refs[4:]
    stack_rows(ins, slice(0, 1024), rows_ref)
    outs = [[keep_ref.at[h], send_ref.at[h]] for h in range(CHAINS)]
    put_loads(sol_ref[...], rows_ref[...], outs)


def halve_rows(w_ref, keep_ref, send_ref):
    z, y, x, c = coords()
    rows = w_ref.shape[0] // 2
    keep_ref[...] = w_ref[pl.ds(pl.multiple_of(c * rows, rows), rows), :]
    send_ref[...] = w_ref[pl.ds(pl.multiple_of((1 - c) * rows, rows), rows), :].astype(F32)


def halve_cols(w_ref, keep_ref, send_ref):
    z, y, x, c = coords()
    for i in range(w_ref.shape[1] // 256):
        here = slice(i * 128, (i + 1) * 128)
        kept = pl.multiple_of(i * 256 + c * 128, 128)
        sent = pl.multiple_of(i * 256 + (1 - c) * 128, 128)
        keep_ref[:, here] = w_ref[:, pl.ds(kept, 128)]
        send_ref[:, here] = w_ref[:, pl.ds(sent, 128)].astype(F32)


def join_cols(keep_ref, recv_ref, w_ref, t_ref):
    n = keep_ref.shape[1]
    w_ref[:, :n] = keep_ref[...]
    w_ref[:, n:] = recv_ref[...].astype(BF16)
    t_ref[:n, :] = keep_ref[...].T
    t_ref[n:, :] = recv_ref[...].astype(BF16).T


def join_rows(keep_ref, recv_ref, w_ref):
    n = keep_ref.shape[0]
    w_ref[:n, :] = keep_ref[...]
    w_ref[n:, :] = recv_ref[...].astype(BF16)


def forward(deep, chain, w_ref, *refs):
    vec, outs, (rhs_ref, sum_ref) = refs[:-6], refs[-6:-2], refs[-2:]
    blocks = vec[0].shape[0]
    if len(vec) == 2:
        own, other = vec[0][...], vec[1][...]
    else:
        mine, theirs, part, recv = [v[...] for v in vec]
        own = mine - part[:blocks] - recv[blocks:]
        other = theirs - part[blocks:] - recv[:blocks]
    for i in range(blocks):
        put_split(rhs_ref, i * 128, own[i])
        put_split(rhs_ref, (blocks + i) * 128, other[i])
    sum_ref[...] = product(w_ref, rhs_ref)
    left = left_lanes((WIDE, 2 * WIDE))
    for i, start in enumerate(block_starts(deep, chain)):
        low = sum_ref[pl.ds(start, WIDE), :]
        high = sum_ref[pl.ds(start + WIDE, WIDE), :]
        block = jnp.where(left, low, high)
        outs[i // 4][i % 4] = block


def backward(deep, chain, w_ref, *refs):
    pieces, outs, rhs_ref = refs[:4], refs[4:-1], refs[-1]
    for i, start in enumerate(block_starts(deep, chain)):
        put_split(rhs_ref, start, pieces[i // 4][i % 4])
    total = product(w_ref, rhs_ref)
    blocks = w_ref.shape[0] // 128
    for i in range(blocks):
        if len(outs) == 1:
            outs[0][i] = take_block(total, i * 128)
        else:
            outs[2 * i // blocks][i % (blocks // 2)] = take_block(total, i * 128)


def run_forward(w, vec, deep, chain, after=()):
    m, k = w.shape
    return kernel_call(
        functools.partial(forward, deep, chain),
        [((4, WIDE, 128), F32)] * 4,
        [w, *vec],
        [pltpu.VMEM((k, 128), BF16), pltpu.VMEM((m, 128), F32)],
        flops=2 * m * k * 128,
        after=after,
    )


def run_backward(w, pieces, deep, chain, apart, after=()):
    m, k = w.shape
    return kernel_call(
        functools.partial(backward, deep, chain),
        [((m // 256, WIDE, 128), F32)] * 2 if apart else [((m // 128, WIDE, 128), F32)],
        [w, *pieces],
        [pltpu.VMEM((k, 128), BF16)],
        flops=2 * m * k * 128,
        after=after,
    )


def depth_sum(value, after):
    value = value[:, :2] + swap_near(value[:, 2:])
    got = swap_far(value[:, 1:])
    return glue(lambda v, g: (v[:, :1] + g,), value, got, after=after)[0]


def plane_sum(keep, follow, send, send_ahead, chain):
    ahead = swap_first(send_ahead, chain)
    first = swap_first(send, chain)
    second = swap_second(follow + ahead, chain)
    return keep + first + second, second


def depth_total(value, deep):
    if not deep:
        return value + swap_near(jnp.concatenate([value[2:], value[:2]], 0))
    keep = value[:2] + swap_near(value[2:])
    keep = keep + swap_far(jnp.concatenate([keep[1:], keep[:1]], 0))
    return jnp.concatenate([keep, swap_near(keep)], 0)


def depth_spread(own):
    pair = jnp.concatenate([own, swap_far(own)], 0)
    return jnp.concatenate([pair, swap_near(pair)], 0)


def plane_spread(line, chain):
    second = swap_second(line, chain)
    return line, second, swap_first(line, chain), swap_first(second, chain)


def unpack_kernel(mine0, recv0, mine1, recv1, out_ref):
    left = left_lanes((WIDE, 128))
    for i in range(mine0.shape[0]):
        p0 = mine0[i] + recv0[i]
        p1 = mine1[i] + recv1[i]
        out_ref[i * 128 : i * 128 + WIDE, :] = jnp.where(left, p0, pltpu.roll(p1, WIDE, 1))
        out_ref[i * 128 + WIDE : (i + 1) * 128, :] = jnp.where(left, pltpu.roll(p0, WIDE, 1), p1)


def unpack(*pairs):
    ins = [array for pair in pairs for array in pair]
    return kernel_call(unpack_kernel, [((ins[0].shape[0] * 128, 128), F32)], ins)[0]


def fast_body(border, solution, winv_top, winv_mid, coupling):
    front = winv_top.shape[0]
    half = front // 2
    tops = ready = kernel_call(
        prep_top, [((32, 1152), F32)] * 4, [border[0], solution[0]]
    )
    tops = [tops[0], swap_core(tops[1]), swap_first(tops[2]), swap_cross(tops[3])]
    keep, send, sol_all = kernel_call(
        top_load_kernel,
        [((CHAINS, 4, WIDE, 128), F32)] * 2 + [((128, 128), BF16)],
        tops,
        [pltpu.VMEM((128, 1024), BF16)],
        flops=2 * 128 * 1024 * 128,
    )
    got = swap_second(send)
    mids = kernel_call(prep_mid, [((32, 1024), F32)] * 4, [border[0]], after=[got])
    mids = [mids[0], swap_core(mids[1]), swap_first(mids[2]), swap_cross(mids[3])]
    load = depth_sum(keep + got, mids)
    load_other = swap_core(load)

    top_keep, top_send = kernel_call(
        halve_rows, [((half, 128), BF16), ((half, 128), F32)], [winv_top], after=ready[:1]
    )
    cou_keep, cou_send = kernel_call(
        halve_cols, [((256, half), BF16), ((256, half), F32)], [coupling]
    )
    mid_keep, mid_send = kernel_call(
        halve_rows, [((half, 256), BF16), ((half, 256), F32)], [winv_mid]
    )
    top_w, top_t = kernel_call(
        join_cols,
        [((half, 256), BF16), ((256, half), BF16)],
        [top_keep, swap_core(top_send)],
    )
    (cou_w,) = kernel_call(
        join_rows, [((512, half), BF16)], [cou_keep, swap_core(cou_send)]
    )

    mid_w, mid_t = kernel_call(
        join_cols,
        [((half, 512), BF16), ((512, half), BF16)],
        [mid_keep, swap_core(mid_send)],
    )

    chains = range(CHAINS)
    values = []
    for h in chains:
        parts = run_forward(top_w, [load[h], load_other[h]], True, h)
        values.append(plane_sum(*parts, h)[0])
    keep, send = kernel_call(
        mid_load_kernel,
        [((CHAINS, 4, WIDE, 128), F32)] * 2,
        [*mids, sol_all],
        [pltpu.VMEM((128, 1024), BF16)],
        flops=2 * 128 * 1024 * 128,
    )
    keep, send = glue(
        lambda k, g: ((k + g)[:, :2], (k + g)[:, 2:]), keep, swap_second(send)
    )
    mid_load = keep + swap_near(send)
    mid_other = swap_core(mid_load)
    top_parts, adjoint = [], []
    for h in chains:
        mine, theirs = run_backward(
            top_t,
            plane_spread(depth_total(values[h], True), h),
            True,
            h,
            True,
            after=[cou_w, mid_w],
        )
        top_parts.append((mine, swap_core(theirs)))
        adjoint.append(mine + top_parts[h][1])
    top_out = unpack(*top_parts)

    mid_parts = []
    for h in chains:
        (both,) = run_backward(
            cou_w, plane_spread(depth_spread(adjoint[h]), h), True, h, False
        )
        vec = [mid_load[h], mid_other[h], both, swap_core(both)]
        parts = run_forward(mid_w, vec, False, h, after=[top_out] if h else ())
        line = depth_total(plane_sum(*parts, h)[0], False)
        mine, theirs = run_backward(mid_t, plane_spread(line, h), False, h, True)
        mid_parts.append((mine, swap_core(theirs)))
    return top_out, unpack(*mid_parts)


def solution(mesh):
    placed = (
        P("leaf", "panel", None),
        P("leaf", "panel", None),
        P(None, AXES),
        P(None, AXES),
        P(AXES, None),
    )
    fits = mesh.shape["leaf"] == 8 and mesh.shape["panel"] == 4
    return jax.shard_map(
        fast_body if fits else plain_body,
        mesh=mesh,
        in_specs=placed,
        out_specs=(P(AXES, None), P(AXES, None)),
        check_vma=False,
    )
```
